32 devices in a mesh: level: 4 (over y, x), sub: 2 (over core), rhs: 4 (over z).
Axes of the slice: x: 2, y: 2, z: 4, core: 2. Of those that a mesh axis runs over, the one named last changes fastest.
Arguments:
- rhs: float32 [4, 32, 256, 256], P('level', 'sub', 'rhs'), may hold values from -6 to 6
- lower_inv: bfloat16 [4, 32, 256, 256], P('level', 'sub'), may hold values from -0.25 to 2.1
- lower_off: bfloat16 [4, 32, 256, 256], P('level', 'sub'), may hold values from -0.25 to 0.25
- upper_inv: bfloat16 [4, 32, 256, 256], P('level', 'sub'), may hold values from -0.25 to 2.1
- upper_off: bfloat16 [4, 32, 256, 256], P('level', 'sub'), may hold values from -0.25 to 0.25
- ancestor: bfloat16 [32, 256, 256], P('sub', 'rhs'), may hold values from -6 to 6
- parent: int32 [3, 32], replicated, may hold values from 0 to 31, as said below
Outputs:
- solution: float32 [4, 32, 256, 256], P('level', 'sub', 'rhs')
- update: float32 [4, 32, 256, 256], P('level', 'sub', 'rhs')
The draws below stay inside these ranges and needn't reach their ends.
Inputs may be any that keep to these rules, and one draw needn't show every extreme that they name: parent[t, c] names a supernode of sub index c // 16 or of sub index (c // 16) XOR 2 ** (t mod 1), where supernode s has sub index s // 16; a parent may have no children or several.
All inputs are finite; a program needn't handle non-finite values.
Results may differ from the reference program's by a relative error of at most 0.009.
Values may be sent and summed in bfloat16 or wider, within the bound.
No kernel may reach another device: no remote copies, remote signals or barrier semaphores. Data moves between devices by JAX's collectives and lax.ppermute only.
A program may use at most 64 MiB of HBM per device.

```python
import jax
import jax.numpy as jnp
from jax import lax

W = 256
R = 256
SN_DEV = 16
TIERS = 4
NODES = 32
SUB_BITS = 1
N_SUB = 2


def triangle_draw(key, lower):
    key_off, key_diag = jax.random.split(key)
    shape = (TIERS, NODES, W, W)
    off_part = jnp.clip(jax.random.normal(key_off, shape, jnp.float32) * (0.6 / W ** 0.5), -0.25, 0.25)
    diag_part = jnp.exp(jax.random.uniform(key_diag, (TIERS, NODES, W, 1), jnp.float32, -0.7, 0.7))
    row_index = lax.broadcasted_iota(jnp.int32, (W, W), 0)
    col_index = lax.broadcasted_iota(jnp.int32, (W, W), 1)
    if lower:
        keep_off = row_index > col_index
    else:
        keep_off = row_index < col_index
    on_diag = row_index == col_index
    return jnp.where(keep_off, off_part, 0.0) + jnp.where(on_diag, diag_part, 0.0)


def draw_lower_inv(key, part):
    return triangle_draw(jax.random.fold_in(key, 11), False).astype(jnp.bfloat16)


def draw_upper_inv(key, part):
    return triangle_draw(jax.random.fold_in(key, 23), True).astype(jnp.bfloat16)


def draw_parent(key, part):
    key_slot, key_side, key_flip = jax.random.split(jax.random.fold_in(key, 37), 3)
    shape = (TIERS - 1, N_SUB, SN_DEV)
    parent_slot = jax.random.randint(key_slot, shape, 0, SN_DEV)
    side_pick = jax.random.randint(key_side, shape, 0, 2)
    flip_bit = jax.random.randint(key_flip, (TIERS - 1, N_SUB, 1), 0, 2)
    child_index = lax.broadcasted_iota(jnp.int32, shape, 2)
    tier_index = lax.broadcasted_iota(jnp.int32, shape, 0)
    sub_index = lax.broadcasted_iota(jnp.int32, shape, 1)
    role = jnp.bitwise_xor(child_index, flip_bit)
    forced = child_index <= 1
    parent_slot = jnp.where(forced & (role == 0), SN_DEV - 1, parent_slot)
    parent_slot = jnp.where(forced & (role == 1), 0, parent_slot)
    side_pick = jnp.where(forced, role, side_pick)
    bit_number = tier_index % SUB_BITS
    partner = jnp.bitwise_xor(sub_index, jnp.left_shift(jnp.ones(shape, jnp.int32), bit_number))
    target = jnp.where(side_pick == 1, partner, sub_index)
    return (target * SN_DEV + parent_slot).reshape(TIERS - 1, NODES).astype(jnp.int32)


def steps_of(key, extent, cuts, smallest, top_value):
    def one(axis_at, shards_of):
        steps = jax.random.uniform(jax.random.fold_in(jax.random.fold_in(key, 6), axis_at), (shards_of,), jnp.float32, smallest / len(cuts), top_value / len(cuts))
        return jnp.repeat(jnp.exp(steps), extent[axis_at] // shards_of).reshape((-1,) + (1,) * (len(extent) - axis_at - 1))

    level = one(*cuts[0])
    for cut in cuts[1:]:
        level = level * one(*cut)
    return level


def scatter_about(rng, extent, spread, limit, cuts=(), dtype=jnp.bfloat16):
    loudness = steps_of(rng, extent, cuts, -0.22, 0.18) if cuts else 1.0
    result = jax.random.normal(rng, extent, jnp.float32) * spread * loudness
    return jnp.minimum(jnp.maximum(result, -limit), limit).astype(dtype)


def setup_inputs(seed: int = 0) -> dict:
    streams_of = jax.random.split(jax.random.key(seed), 8)
    rhs = scatter_about(streams_of[0], (TIERS, NODES, R, W), 1.0, 6.0, ((0, 4), (1, 2), (2, 4)), jnp.float32)
    lower_inv = draw_lower_inv(jax.random.fold_in(streams_of[7], 71), 0)
    lower_off = scatter_about(streams_of[2], (TIERS, NODES, W, W), (2 * W) ** -0.5, 0.25, ((0, 4), (1, 2)))
    upper_inv = draw_upper_inv(jax.random.fold_in(streams_of[7], 71), 0)
    upper_off = scatter_about(streams_of[4], (TIERS, NODES, W, W), (2 * W) ** -0.5, 0.25, ((0, 4), (1, 2)))
    ancestor = scatter_about(streams_of[5], (NODES, R, W), 1.0, 6.0, ((0, 2), (1, 4)))
    parent = draw_parent(jax.random.fold_in(streams_of[7], 71), 0)
    return dict(rhs=rhs, lower_inv=lower_inv, lower_off=lower_off, upper_inv=upper_inv, upper_off=upper_off, ancestor=ancestor, parent=parent)


def tier_product(left, right):
    return jnp.einsum("srw,swv->srv", left.astype(jnp.float32), right.astype(jnp.float32))


def reference(rhs, lower_inv, lower_off, upper_inv, upper_off, ancestor, parent):
    tiers = rhs.shape[0]
    count = rhs.shape[1]
    forwards = []
    updates = []
    incoming = jnp.zeros(rhs.shape[1:], jnp.float32)
    for tier in range(tiers):
        residue = (rhs[tier] - incoming).astype(jnp.bfloat16)
        forward = tier_product(residue, lower_inv[tier]).astype(jnp.bfloat16)
        update = tier_product(forward, lower_off[tier])
        forwards.append(forward)
        updates.append(update)
        if tier + 1 < tiers:
            incoming = jax.ops.segment_sum(update, parent[tier], num_segments=count)
    solutions = [None] * tiers
    rounded = ancestor
    for tier in reversed(range(tiers)):
        if tier == tiers - 1:
            above_rows = ancestor
        else:
            above_rows = jnp.take(rounded, parent[tier], axis=0)
        reduced = (forwards[tier].astype(jnp.float32) - tier_product(above_rows, upper_off[tier])).astype(jnp.bfloat16)
        solution_part = tier_product(reduced, upper_inv[tier])
        solutions[tier] = solution_part
        rounded = solution_part.astype(jnp.bfloat16)
    return jnp.stack(solutions), jnp.stack(updates)
```

```python
import functools

import jax
import jax.numpy as jnp
from jax import lax
from jax.experimental import pallas as pl
from jax.experimental.pallas import tpu as pltpu
from jax.sharding import PartitionSpec as P

CHUNKS = 2
LOCAL_SWAP = False
VMEM_BYTES = 24 * 2**20

BF16 = jnp.bfloat16
F32 = jnp.float32
IN_VMEM = pl.BlockSpec(memory_space=pltpu.VMEM)
IN_SMEM = pl.BlockSpec(memory_space=pltpu.SMEM)


def dot(left, right):
    return jnp.dot(left, right, preferred_element_type=F32)


def forward_kernel(section, start, rows, info, rhs, incoming, inv, off, kept_f, kept_u, fwd, upd, home, far, total):
    del kept_f, kept_u
    count = inv.shape[0]

    @pl.when(info[count] == section)
    def _():
        total[...] = jnp.zeros_like(total)
        for node in range(count):
            right_side = rhs[node, pl.ds(start, rows), :]
            if incoming is not None:
                right_side = right_side - incoming[node].astype(F32)
            forward = dot(right_side.astype(BF16), inv[node]).astype(BF16)
            fwd[node] = forward
            update = dot(forward, off[node])
            upd[node] = update
            total[info[node]] += update
        home[...] = total[:count]
        far[...] = total[count:].astype(BF16)


def first_kernel(section, start, rows, info, rhs, inv, off, kept_f, kept_u, fwd, upd, home, far, total):
    forward_kernel(section, start, rows, info, rhs, None, inv, off, kept_f, kept_u, fwd, upd, home, far, total)


def top_kernel(section, start, rows, info, rhs, incoming, inv, up_off, up_inv, ancestor, kept_f, kept_s, fwd, sol, sol_bf):
    del kept_f, kept_s
    count = inv.shape[0]

    @pl.when(info[count] == section)
    def _():
        for node in range(count):
            right_side = rhs[node, pl.ds(start, rows), :] - incoming[node].astype(F32)
            forward = dot(right_side.astype(BF16), inv[node]).astype(BF16)
            fwd[node] = forward
            above = dot(ancestor[node, pl.ds(start, rows), :], up_off[node])
            reduced = (forward.astype(F32) - above).astype(BF16)
            solved = dot(reduced, up_inv[node])
            sol[node] = solved
            sol_bf[node] = solved.astype(BF16)


def top_update_kernel(section, start, rows, info, fwd, off, kept_u, upd):
    del kept_u, start, rows
    count = off.shape[0]

    @pl.when(info[count] == section)
    def _():
        for node in range(count):
            upd[node] = dot(fwd[node], off[node])


def backward_kernel(section, start, rows, info, fwd, own, partner, up_off, up_inv, kept_s, sol, sol_bf):
    del kept_s, start, rows
    count = up_inv.shape[0]

    @pl.when(info[count] == section)
    def _():
        for node in range(count):
            place = info[node]
            at_home = place < count
            slot = jnp.where(at_home, place, place - count)
            above = jnp.where(at_home, own[slot], partner[slot])
            reduced = (fwd[node].astype(F32) - dot(above, up_off[node])).astype(BF16)
            solved = dot(reduced, up_inv[node])
            sol[node] = solved
            sol_bf[node] = solved.astype(BF16)


def call(kernel, section, start, rows, operands, outs, aliases, scratch=(), products=2):
    count = operands[1].shape[0]
    return pl.pallas_call(
        functools.partial(kernel, section, start, rows),
        in_specs=[IN_SMEM] + [IN_VMEM] * (len(operands) - 1),
        out_specs=[IN_VMEM] * len(outs),
        out_shape=outs,
        scratch_shapes=scratch,
        input_output_aliases=aliases,
        compiler_params=pltpu.CompilerParams(vmem_limit_bytes=VMEM_BYTES),
        cost_estimate=pl.CostEstimate(
            flops=products * 2 * count * rows * 256 * 256, bytes_accessed=count * 256 * 256 * 2 * products, transcendentals=0
        ),
    )(*operands)


def swapped(value, section, apart):
    mask = 2**apart
    subs = lax.axis_size("sub")
    if not LOCAL_SWAP:
        return lax.ppermute(value, "sub", [(i, i ^ mask) for i in range(subs)])
    pairs = [(section * subs + i, section * subs + (i ^ mask)) for i in range(subs)]
    return lax.ppermute(value, ("level", "sub"), pairs)


def body(rhs, lower_inv, lower_off, upper_inv, upper_off, ancestor, parent):
    levels = lax.axis_size("level")
    sub_count = lax.axis_size("sub")
    sub_bits = sub_count.bit_length() - 1
    tier = lax.axis_index("level")
    sub = lax.axis_index("sub")
    rhs, lower_inv, lower_off, upper_inv, upper_off = (
        value[0] for value in (rhs, lower_inv, lower_off, upper_inv, upper_off)
    )
    count, all_rows, width = rhs.shape
    rows = all_rows // CHUNKS
    parent_row = lax.dynamic_index_in_dim(parent, jnp.minimum(tier, levels - 2), 0, keepdims=False)
    parent_here = lax.dynamic_slice_in_dim(parent_row, sub * count, count)
    place = parent_here % count + jnp.where(parent_here // count == sub, 0, count)
    info = jnp.concatenate([place, tier[None]]).astype(jnp.int32)

    def shape(dtype):
        return jax.ShapeDtypeStruct((count, rows, width), dtype)

    fwd = [jnp.zeros((count, rows, width), BF16) for _ in range(CHUNKS)]
    upd = [jnp.zeros((count, rows, width), F32) for _ in range(CHUNKS)]
    sol = [jnp.zeros((count, rows, width), F32) for _ in range(CHUNKS)]
    incoming = [None] * CHUNKS
    above = [None] * CHUNKS
    top = levels - 1
    for section in range(top):
        for c in range(CHUNKS):
            if section == 0:
                kernel, operands = first_kernel, (info, rhs, lower_inv, lower_off, fwd[c], upd[c])
            else:
                kernel, operands = forward_kernel, (info, rhs, incoming[c], lower_inv, lower_off, fwd[c], upd[c])
            at = len(operands) - 2
            fwd[c], upd[c], home, far = call(
                kernel, section, c * rows, rows, operands,
                [shape(BF16), shape(F32), shape(F32), shape(BF16)], {at: 0, at + 1: 1},
                [pltpu.VMEM((2 * count, rows, width), F32)],
            )
            received = swapped(far, section, section % sub_bits)
            summed = (home + received.astype(F32)).astype(BF16)
            incoming[c] = lax.ppermute(summed, "level", [(section, section + 1)])
    for c in range(CHUNKS):
        fwd[c], sol[c], solved = call(
            top_kernel, top, c * rows, rows,
            (info, rhs, incoming[c], lower_inv, upper_off, upper_inv, ancestor, fwd[c], sol[c]),
            [shape(BF16), shape(F32), shape(BF16)], {7: 0, 8: 1}, products=3,
        )
        above[c] = lax.ppermute(solved, "level", [(top, top - 1)])
    for c in range(CHUNKS):
        (upd[c],) = call(top_update_kernel, top, c * rows, rows, (info, fwd[c], lower_off, upd[c]), [shape(F32)], {3: 0}, products=1)
    for section in reversed(range(top)):
        for c in range(CHUNKS):
            partner = swapped(above[c], section, section % sub_bits)
            sol[c], solved = call(
                backward_kernel, section, c * rows, rows,
                (info, fwd[c], above[c], partner, upper_off, upper_inv, sol[c]),
                [shape(F32), shape(BF16)], {6: 0},
            )
            if section:
                above[c] = lax.ppermute(solved, "level", [(section, section - 1)])
    return jnp.concatenate(sol, axis=1)[None], jnp.concatenate(upd, axis=1)[None]


def solution(mesh):
    placed = (
        P("level", "sub", "rhs", None),
        P("level", "sub", None, None),
        P("level", "sub", None, None),
        P("level", "sub", None, None),
        P("level", "sub", None, None),
        P("sub", "rhs", None),
        P(),
    )
    return jax.shard_map(
        body,
        mesh=mesh,
        in_specs=placed,
        out_specs=(P("level", "sub", "rhs", None), P("level", "sub", "rhs", None)),
        check_vma=False,
    )
```

```python
import functools

import jax
import jax.numpy as jnp
from jax import lax
from jax.experimental import pallas as pl
from jax.experimental.pallas import tpu as pltpu
from jax.sharding import PartitionSpec as P

CHUNKS = 2
LOCAL_SWAP = False
VMEM_BYTES = 24 * 2**20

BF16 = jnp.bfloat16
F32 = jnp.float32
IN_VMEM = pl.BlockSpec(memory_space=pltpu.VMEM)
IN_SMEM = pl.BlockSpec(memory_space=pltpu.SMEM)


def dot(left, right):
    return jnp.dot(left, right, preferred_element_type=F32)


def forward_kernel(section, start, rows, info, rhs, incoming, inv, off, kept_f, kept_u, fwd, upd, home, far, total):
    count = inv.shape[0]

    @pl.when(info[count] != section)
    def _():
        fwd[...] = kept_f[...]
        upd[...] = kept_u[...]

    @pl.when(info[count] == section)
    def _():
        total[...] = jnp.zeros_like(total)
        for node in range(count):
            right_side = rhs[node, pl.ds(start, rows), :]
            if incoming is not None:
                right_side = right_side - incoming[node].astype(F32)
            forward = dot(right_side.astype(BF16), inv[node]).astype(BF16)
            fwd[node] = forward
            update = dot(forward, off[node])
            upd[node] = update
            total[info[node]] += update
        home[...] = total[:count]
        far[...] = total[count:].astype(BF16)


def first_kernel(section, start, rows, info, rhs, inv, off, kept_f, kept_u, fwd, upd, home, far, total):
    forward_kernel(section, start, rows, info, rhs, None, inv, off, kept_f, kept_u, fwd, upd, home, far, total)


def top_kernel(section, start, rows, info, rhs, incoming, inv, up_off, up_inv, ancestor, kept_f, kept_s, fwd, sol, sol_bf):
    count = inv.shape[0]

    @pl.when(info[count] != section)
    def _():
        fwd[...] = kept_f[...]
        sol[...] = kept_s[...]

    @pl.when(info[count] == section)
    def _():
        for node in range(count):
            right_side = rhs[node, pl.ds(start, rows), :] - incoming[node].astype(F32)
            forward = dot(right_side.astype(BF16), inv[node]).astype(BF16)
            fwd[node] = forward
            above = dot(ancestor[node, pl.ds(start, rows), :], up_off[node])
            reduced = (forward.astype(F32) - above).astype(BF16)
            solved = dot(reduced, up_inv[node])
            sol[node] = solved
            sol_bf[node] = solved.astype(BF16)


def top_update_kernel(section, start, rows, info, fwd, off, kept_u, upd):
    count = off.shape[0]

    @pl.when(info[count] != section)
    def _():
        upd[...] = kept_u[...]

    @pl.when(info[count] == section)
    def _():
        for node in range(count):
            upd[node] = dot(fwd[node], off[node])


def backward_kernel(section, start, rows, info, fwd, own, partner, up_off, up_inv, kept_s, sol, sol_bf):
    count = up_inv.shape[0]

    @pl.when(info[count] != section)
    def _():
        sol[...] = kept_s[...]

    @pl.when(info[count] == section)
    def _():
        for node in range(count):
            place = info[node]
            at_home = place < count
            slot = jnp.where(at_home, place, place - count)
            above = jnp.where(at_home, own[slot], partner[slot])
            reduced = (fwd[node].astype(F32) - dot(above, up_off[node])).astype(BF16)
            solved = dot(reduced, up_inv[node])
            sol[node] = solved
            sol_bf[node] = solved.astype(BF16)


def call(kernel, section, start, rows, operands, outs, aliases, scratch=(), products=2):
    count = operands[1].shape[0]
    return pl.pallas_call(
        functools.partial(kernel, section, start, rows),
        in_specs=[IN_SMEM] + [IN_VMEM] * (len(operands) - 1),
        out_specs=[IN_VMEM] * len(outs),
        out_shape=outs,
        scratch_shapes=scratch,
        input_output_aliases=aliases,
        compiler_params=pltpu.CompilerParams(vmem_limit_bytes=VMEM_BYTES),
        cost_estimate=pl.CostEstimate(
            flops=products * 2 * count * rows * 256 * 256, bytes_accessed=count * 256 * 256 * 2 * products, transcendentals=0
        ),
    )(*operands)


def swapped(value, section, apart):
    mask = 2**apart
    subs = lax.axis_size("sub")
    if not LOCAL_SWAP:
        return lax.ppermute(value, "sub", [(i, i ^ mask) for i in range(subs)])
    pairs = [(section * subs + i, section * subs + (i ^ mask)) for i in range(subs)]
    return lax.ppermute(value, ("level", "sub"), pairs)


def general_body(rhs, lower_inv, lower_off, upper_inv, upper_off, ancestor, parent):
    levels = lax.axis_size("level")
    sub_count = lax.axis_size("sub")
    sub_bits = sub_count.bit_length() - 1
    tier = lax.axis_index("level")
    sub = lax.axis_index("sub")
    rhs, lower_inv, lower_off, upper_inv, upper_off = (
        value[0] for value in (rhs, lower_inv, lower_off, upper_inv, upper_off)
    )
    count, all_rows, width = rhs.shape
    rows = all_rows // CHUNKS
    parent_row = lax.dynamic_index_in_dim(parent, jnp.minimum(tier, levels - 2), 0, keepdims=False)
    parent_here = lax.dynamic_slice_in_dim(parent_row, sub * count, count)
    place = parent_here % count + jnp.where(parent_here // count == sub, 0, count)
    info = jnp.concatenate([place, tier[None]]).astype(jnp.int32)

    def shape(dtype):
        return jax.ShapeDtypeStruct((count, rows, width), dtype)

    fwd = [jnp.zeros((count, rows, width), BF16) for _ in range(CHUNKS)]
    upd = [jnp.zeros((count, rows, width), F32) for _ in range(CHUNKS)]
    sol = [jnp.zeros((count, rows, width), F32) for _ in range(CHUNKS)]
    incoming = [None] * CHUNKS
    above = [None] * CHUNKS
    top = levels - 1
    for section in range(top):
        for c in range(CHUNKS):
            if section == 0:
                kernel, operands = first_kernel, (info, rhs, lower_inv, lower_off, fwd[c], upd[c])
            else:
                kernel, operands = forward_kernel, (info, rhs, incoming[c], lower_inv, lower_off, fwd[c], upd[c])
            at = len(operands) - 2
            fwd[c], upd[c], home, far = call(
                kernel, section, c * rows, rows, operands,
                [shape(BF16), shape(F32), shape(F32), shape(BF16)], {at: 0, at + 1: 1},
                [pltpu.VMEM((2 * count, rows, width), F32)],
            )
            received = swapped(far, section, section % sub_bits)
            summed = (home + received.astype(F32)).astype(BF16)
            incoming[c] = lax.ppermute(summed, "level", [(section, section + 1)])
    for c in range(CHUNKS):
        fwd[c], sol[c], solved = call(
            top_kernel, top, c * rows, rows,
            (info, rhs, incoming[c], lower_inv, upper_off, upper_inv, ancestor, fwd[c], sol[c]),
            [shape(BF16), shape(F32), shape(BF16)], {7: 0, 8: 1}, products=3,
        )
        above[c] = lax.ppermute(solved, "level", [(top, top - 1)])
    for c in range(CHUNKS):
        (upd[c],) = call(top_update_kernel, top, c * rows, rows, (info, fwd[c], lower_off, upd[c]), [shape(F32)], {3: 0}, products=1)
    for section in reversed(range(top)):
        for c in range(CHUNKS):
            partner = swapped(above[c], section, section % sub_bits)
            sol[c], solved = call(
                backward_kernel, section, c * rows, rows,
                (info, fwd[c], above[c], partner, upper_off, upper_inv, sol[c]),
                [shape(F32), shape(BF16)], {6: 0},
            )
            if section:
                above[c] = lax.ppermute(solved, "level", [(section, section - 1)])
    return jnp.concatenate(sol, axis=1)[None], jnp.concatenate(upd, axis=1)[None]


NODE_ROWS = 16


def rows_of(start):
    return pl.ds(pl.multiple_of(start, NODE_ROWS), NODE_ROWS)


def flat(value):
    return value.reshape(value.shape[0] * value.shape[1], value.shape[2])


def pick(select, values):
    high = values.astype(BF16)
    low = (values - high.astype(F32)).astype(BF16)
    return dot(select, high) + dot(select, low)


def keep(section, kept, outs):
    @pl.when(lax.axis_index("level") != section)
    def _():
        for before, after in zip(kept, outs):
            after[...] = before[...]


def start_kernel(c, rhs, inv, off, select, home, far, upd_own, upd_far, *merged):
    count = inv.shape[0]
    level, sub = lax.axis_index("level"), lax.axis_index("sub")
    half = rhs.shape[1] // 2

    @pl.when(level == 0)
    def _():
        mine, other = rows_of(half * sub + NODE_ROWS * c), rows_of(half * (1 - sub) + NODE_ROWS * c)
        for node in range(count):
            right_side = jnp.concatenate([rhs[node, mine, :], rhs[node, other, :]], axis=0)
            forward = dot(right_side.astype(BF16), inv[node]).astype(BF16)
            update = dot(forward, off[node])
            upd_own[node] = update[:NODE_ROWS]
            upd_far[node] = update[NODE_ROWS:]
        chosen = select[:, : count * NODE_ROWS]
        home[...] = pick(chosen, flat(upd_own[...])).reshape(home.shape)
        sums = pick(chosen, flat(upd_far[...])).astype(BF16).reshape(far.shape)
        far[:count] = sums[count:]
        far[count:] = sums[:count]

    if merged:

        @pl.when(level != 0)
        def _():
            for node in range(count):
                merged[0][node] = dot(inv[node], off[node]).astype(BF16)


def merge_kernel(left, right, merged):
    for node in range(left.shape[0]):
        merged[node] = dot(left[node], right[node]).astype(BF16)


def residue_of(c, rhs, rhs_far, incoming, node):
    count = rhs.shape[0]
    sub = lax.axis_index("sub")
    if node < count:
        right_side = rhs[node, rows_of(rhs.shape[1] // 2 * sub + NODE_ROWS * c), :]
    else:
        right_side = rhs_far[node - count, NODE_ROWS * c : NODE_ROWS * (c + 1), :]
    return (right_side - incoming[node].astype(F32)).astype(BF16)


def tier_kernel(section, c, rhs, rhs_far, incoming, step_own, step_far, select, kept_r, kept_o, kept_f, residue, upd_own, upd_far, sums):
    count = rhs.shape[0]
    keep(section, (kept_r, kept_o, kept_f), (residue, upd_own, upd_far))

    @pl.when(lax.axis_index("level") == section)
    def _():
        for node in range(2 * count):
            value = residue_of(c, rhs, rhs_far, incoming, node)
            residue[node] = value
            if node < count:
                upd_own[node] = dot(value, step_own[node])
            else:
                upd_far[node - count] = dot(value, step_far[node - count])
        updates = jnp.concatenate([flat(upd_own[...]), flat(upd_far[...])], axis=0)
        sums[...] = pick(select[...], updates).astype(BF16).reshape(sums.shape)


def base_kernel(c, rhs, residue, step_own, step_far, base):
    count = rhs.shape[0]
    level, sub = lax.axis_index("level"), lax.axis_index("sub")
    half = rhs.shape[1] // 2

    @pl.when(level == 0)
    def _():
        mine, other = rows_of(half * sub + NODE_ROWS * c), rows_of(half * (1 - sub) + NODE_ROWS * c)
        for node in range(count):
            right_side = jnp.concatenate([rhs[node, mine, :], rhs[node, other, :]], axis=0)
            solved = dot(right_side.astype(BF16), step_own[node])
            base[node] = solved[:NODE_ROWS]
            base[count + node] = solved[NODE_ROWS:]

    @pl.when((level != 0) & (level != lax.axis_size("level") - 1))
    def _():
        for node in range(count):
            base[node] = dot(residue[node], step_own[node])
            base[count + node] = dot(residue[count + node], step_far[node])


def ancestor_kernel(c, ancestor, ancestor_far, step_own, step_far, base):
    count = ancestor.shape[0]
    sub = lax.axis_index("sub")

    @pl.when(lax.axis_index("level") == lax.axis_size("level") - 1)
    def _():
        for node in range(count):
            base[node] = dot(ancestor[node, rows_of(ancestor.shape[1] // 2 * sub + NODE_ROWS * c), :], step_own[node])
            base[count + node] = dot(ancestor_far[node, NODE_ROWS * c : NODE_ROWS * (c + 1), :], step_far[node])


def top_kernel2(section, c, rhs, rhs_far, incoming, step_own, step_far, base, choose, kept_r, kept_o, kept_f, residue, sol_own, sol_far, sent):
    count = rhs.shape[0]
    keep(section, (kept_r, kept_o, kept_f), (residue, sol_own, sol_far))

    @pl.when(lax.axis_index("level") == section)
    def _():
        for node in range(2 * count):
            value = residue_of(c, rhs, rhs_far, incoming, node)
            residue[node] = value
            if node < count:
                sol_own[node] = dot(value, step_own[node]) - base[node]
            else:
                sol_far[node - count] = dot(value, step_far[node - count]) - base[node]
        solved = jnp.concatenate([flat(sol_own[...]), flat(sol_far[...])], axis=0).astype(BF16)
        sent[...] = dot(choose[...], solved).astype(BF16).reshape(sent.shape)


def top_update_kernel2(section, residue, step_own, step_far, kept_o, kept_f, upd_own, upd_far):
    count = step_own.shape[0]
    keep(section, (kept_o, kept_f), (upd_own, upd_far))

    @pl.when(lax.axis_index("level") == section)
    def _():
        for node in range(count):
            upd_own[node] = dot(residue[node], step_own[node])
            upd_far[node] = dot(residue[count + node], step_far[node])


def back_kernel(section, above, base, step_own, step_far, choose, kept_o, kept_f, sol_own, sol_far, sent):
    count = step_own.shape[0]
    keep(section, (kept_o, kept_f), (sol_own, sol_far))

    @pl.when(lax.axis_index("level") == section)
    def _():
        for node in range(count):
            sol_own[node] = base[node] - dot(above[node], step_own[node])
            sol_far[node] = base[count + node] - dot(above[count + node], step_far[node])
        solved = jnp.concatenate([flat(sol_own[...]), flat(sol_far[...])], axis=0).astype(BF16)
        sent[...] = dot(choose[...], solved).astype(BF16).reshape(sent.shape)


def last_kernel(above, above_far, base, step_own, kept_o, kept_f, sol_own, sol_far):
    count = step_own.shape[0]
    keep(0, (kept_o, kept_f), (sol_own, sol_far))

    @pl.when(lax.axis_index("level") == 0)
    def _():
        for node in range(count):
            rows = jnp.concatenate([above[node], above_far[node]], axis=0)
            solved = dot(rows, step_own[node])
            sol_own[node] = base[node] - solved[:NODE_ROWS]
            sol_far[node] = base[count + node] - solved[NODE_ROWS:]


def run(kernel, operands, outs, aliases=None, products=32):
    return pl.pallas_call(
        kernel,
        in_specs=[IN_VMEM] * len(operands),
        out_specs=[IN_VMEM] * len(outs),
        out_shape=outs,
        input_output_aliases=aliases or {},
        compiler_params=pltpu.CompilerParams(vmem_limit_bytes=VMEM_BYTES),
        cost_estimate=pl.CostEstimate(
            flops=products * 2 * NODE_ROWS * 256 * 256, bytes_accessed=256 * 256 * 2 * products, transcendentals=0
        ),
    )(*operands)


def exchanged(value):
    return lax.ppermute(value, "sub", [(0, 1), (1, 0)])


def relative_parents(parent_row, sub, count):
    own_first = jnp.where(sub == 0, parent_row, jnp.roll(parent_row, count))
    return own_first % count + jnp.where(own_first // count == sub, 0, count)


def pair_body(rhs, lower_inv, lower_off, upper_inv, upper_off, ancestor, parent):
    levels = lax.axis_size("level")
    tier = lax.axis_index("level")
    sub = lax.axis_index("sub")
    top = levels - 1
    rhs, lower_inv, lower_off, upper_inv, upper_off = (
        value[0] for value in (rhs, lower_inv, lower_off, upper_inv, upper_off)
    )
    count, all_rows, width = rhs.shape
    half = all_rows // 2
    chunks = half // NODE_ROWS
    nodes = 2 * count

    def shape(of, dtype):
        return jax.ShapeDtypeStruct((of, NODE_ROWS, width), dtype)

    def blank(of, dtype):
        return [jnp.zeros((of, NODE_ROWS, width), dtype) for _ in range(chunks)]

    def table(row):
        return relative_parents(lax.dynamic_index_in_dim(parent, row, 0, keepdims=False), sub, count)

    index = jnp.arange(nodes * NODE_ROWS, dtype=jnp.int32)
    lane_up = jnp.repeat(table(jnp.minimum(tier, top - 1)), NODE_ROWS) * NODE_ROWS + index % NODE_ROWS
    lane_down = jnp.repeat(table(jnp.maximum(tier - 1, 0)), NODE_ROWS) * NODE_ROWS + index % NODE_ROWS
    select = (index[:, None] == lane_up[None, :]).astype(BF16)
    choose = (lane_down[:, None] == index[None, :]).astype(BF16)

    upd_own, upd_far = blank(count, F32), blank(count, F32)
    sol_own, sol_far = blank(count, F32), blank(count, F32)
    residue = blank(nodes, BF16)
    incoming = [None] * chunks
    parts = [None] * chunks
    for c in range(chunks):
        outs = [shape(nodes, F32), shape(nodes, BF16), shape(count, F32), shape(count, F32)]
        if c == 0:
            outs.append(jax.ShapeDtypeStruct(lower_inv.shape, BF16))
        home, far, upd_own[c], upd_far[c], *more = run(
            functools.partial(start_kernel, c), (rhs, lower_inv, lower_off, select), outs
        )
        if c == 0:
            up_own = more[0]
        parts[c] = (home, exchanged(far))
    for c in range(chunks):
        home, received = parts[c]
        incoming[c] = (home + received.astype(F32)).astype(BF16)
    sent = incoming
    incoming = [lax.ppermute(value, "level", [(0, 1)]) for value in incoming]

    up_own, rhs, ancestor, lower_inv, upper_inv, upper_off, sent = lax.optimization_barrier(
        (up_own, rhs, ancestor, lower_inv, upper_inv, upper_off, sent)
    )
    up_far = exchanged(up_own)
    rhs_far = exchanged(lax.dynamic_slice_in_dim(rhs, half * (1 - sub), half, 1))
    matrix = [jax.ShapeDtypeStruct(lower_inv.shape, BF16)]
    (base_own,) = run(merge_kernel, (lower_inv, upper_inv), matrix, products=64)
    base_far = exchanged(base_own)
    (down_own,) = run(merge_kernel, (upper_off, upper_inv), matrix, products=64)
    down_far = exchanged(down_own)
    ancestor_far = exchanged(lax.dynamic_slice_in_dim(ancestor, half * (1 - sub), half, 1))

    for section in range(1, top):
        for c in range(chunks):
            residue[c], upd_own[c], upd_far[c], sums = run(
                functools.partial(tier_kernel, section, c),
                (rhs, rhs_far, incoming[c], up_own, up_far, select, residue[c], upd_own[c], upd_far[c]),
                [shape(nodes, BF16), shape(count, F32), shape(count, F32), shape(nodes, BF16)],
                {6: 0, 7: 1, 8: 2},
            )
            incoming[c] = lax.ppermute(sums, "level", [(section, section + 1)])
    base = [
        run(functools.partial(base_kernel, c), (rhs, residue[c], base_own, base_far), [shape(nodes, F32)])[0]
        for c in range(chunks)
    ]
    from_ancestor = [
        run(functools.partial(ancestor_kernel, c), (ancestor, ancestor_far, down_own, down_far), [shape(nodes, F32)])[0]
        for c in range(chunks)
    ]
    above = [None] * chunks
    for c in range(chunks):
        residue[c], sol_own[c], sol_far[c], solved = run(
            functools.partial(top_kernel2, top, c),
            (rhs, rhs_far, incoming[c], base_own, base_far, from_ancestor[c], choose, residue[c], sol_own[c], sol_far[c]),
            [shape(nodes, BF16), shape(count, F32), shape(count, F32), shape(nodes, BF16)],
            {7: 0, 8: 1, 9: 2},
        )
        above[c] = lax.ppermute(solved, "level", [(top, top - 1)])
    for c in range(chunks):
        upd_own[c], upd_far[c] = run(
            functools.partial(top_update_kernel2, top),
            (residue[c], up_own, up_far, upd_own[c], upd_far[c]),
            [shape(count, F32), shape(count, F32)],
            {3: 0, 4: 1},
        )
    for section in reversed(range(1, top)):
        for c in range(chunks):
            sol_own[c], sol_far[c], solved = run(
                functools.partial(back_kernel, section),
                (above[c], base[c], down_own, down_far, choose, sol_own[c], sol_far[c]),
                [shape(count, F32), shape(count, F32), shape(nodes, BF16)],
                {5: 0, 6: 1},
            )
            above[c] = lax.ppermute(solved, "level", [(section, section - 1)])
    sol_other = [exchanged(value) for value in sol_far]
    upd_other = [exchanged(value) for value in upd_far]
    for c in range(chunks):
        sol_own[c], sol_far[c] = run(
            last_kernel,
            (above[c][:count], exchanged(above[c][count:]), base[c], down_own, sol_own[c], sol_far[c]),
            [shape(count, F32), shape(count, F32)],
            {4: 0, 5: 1},
            products=16,
        )

    def assembled(own, far, other):
        mine = jnp.concatenate(own, axis=1)
        theirs = jnp.where(tier == 0, jnp.concatenate(far, axis=1), jnp.concatenate(other, axis=1))
        return jnp.concatenate([jnp.where(sub == 0, mine, theirs), jnp.where(sub == 0, theirs, mine)], axis=1)

    return assembled(sol_own, sol_far, sol_other)[None], assembled(upd_own, upd_far, upd_other)[None]


def solution(mesh):
    placed = (
        P("level", "sub", "rhs", None),
        P("level", "sub", None, None),
        P("level", "sub", None, None),
        P("level", "sub", None, None),
        P("level", "sub", None, None),
        P("sub", "rhs", None),
        P(),
    )
    return jax.shard_map(
        pair_body if mesh.shape["sub"] == 2 else general_body,
        mesh=mesh,
        in_specs=placed,
        out_specs=(P("level", "sub", "rhs", None), P("level", "sub", "rhs", None)),
        check_vma=False,
    )
```

```python
import functools
import itertools

import jax
import jax.numpy as jnp
from jax import lax
from jax.experimental import pallas as pl
from jax.experimental.pallas import tpu as pltpu
from jax.sharding import PartitionSpec as P

CHUNKS = 2
LOCAL_SWAP = False
VMEM_BYTES = 24 * 2**20

LEVEL, SUB = "level", "sub"
BF16 = jnp.bfloat16
F32 = jnp.float32
IN_VMEM = pl.BlockSpec(memory_space=pltpu.VMEM)
IN_SMEM = pl.BlockSpec(memory_space=pltpu.SMEM)


def dot(left, right):
    return jnp.dot(left, right, preferred_element_type=F32)


def forward_kernel(section, start, rows, info, rhs, incoming, inv, off, kept_f, kept_u, fwd, upd, home, far, total):
    count = inv.shape[0]

    @pl.when(info[count] != section)
    def _():
        fwd[...] = kept_f[...]
        upd[...] = kept_u[...]

    @pl.when(info[count] == section)
    def _():
        total[...] = jnp.zeros_like(total)
        for node in range(count):
            right_side = rhs[node, pl.ds(start, rows), :]
            if incoming is not None:
                right_side = right_side - incoming[node].astype(F32)
            forward = dot(right_side.astype(BF16), inv[node]).astype(BF16)
            fwd[node] = forward
            update = dot(forward, off[node])
            upd[node] = update
            total[info[node]] += update
        home[...] = total[:count]
        far[...] = total[count:].astype(BF16)


def first_kernel(section, start, rows, info, rhs, inv, off, kept_f, kept_u, fwd, upd, home, far, total):
    forward_kernel(section, start, rows, info, rhs, None, inv, off, kept_f, kept_u, fwd, upd, home, far, total)


def top_kernel(section, start, rows, info, rhs, incoming, inv, up_off, up_inv, ancestor, kept_f, kept_s, fwd, sol, sol_bf):
    count = inv.shape[0]

    @pl.when(info[count] != section)
    def _():
        fwd[...] = kept_f[...]
        sol[...] = kept_s[...]

    @pl.when(info[count] == section)
    def _():
        for node in range(count):
            right_side = rhs[node, pl.ds(start, rows), :] - incoming[node].astype(F32)
            forward = dot(right_side.astype(BF16), inv[node]).astype(BF16)
            fwd[node] = forward
            above = dot(ancestor[node, pl.ds(start, rows), :], up_off[node])
            reduced = (forward.astype(F32) - above).astype(BF16)
            solved = dot(reduced, up_inv[node])
            sol[node] = solved
            sol_bf[node] = solved.astype(BF16)


def top_update_kernel(section, start, rows, info, fwd, off, kept_u, upd):
    count = off.shape[0]

    @pl.when(info[count] != section)
    def _():
        upd[...] = kept_u[...]

    @pl.when(info[count] == section)
    def _():
        for node in range(count):
            upd[node] = dot(fwd[node], off[node])


def backward_kernel(section, start, rows, info, fwd, own, partner, up_off, up_inv, kept_s, sol, sol_bf):
    count = up_inv.shape[0]

    @pl.when(info[count] != section)
    def _():
        sol[...] = kept_s[...]

    @pl.when(info[count] == section)
    def _():
        for node in range(count):
            place = info[node]
            at_home = place < count
            slot = jnp.where(at_home, place, place - count)
            above = jnp.where(at_home, own[slot], partner[slot])
            reduced = (fwd[node].astype(F32) - dot(above, up_off[node])).astype(BF16)
            solved = dot(reduced, up_inv[node])
            sol[node] = solved
            sol_bf[node] = solved.astype(BF16)


def call(kernel, section, start, rows, operands, outs, aliases, scratch=(), products=2):
    count = operands[1].shape[0]
    return pl.pallas_call(
        functools.partial(kernel, section, start, rows),
        in_specs=[IN_SMEM] + [IN_VMEM] * (len(operands) - 1),
        out_specs=[IN_VMEM] * len(outs),
        out_shape=outs,
        scratch_shapes=scratch,
        input_output_aliases=aliases,
        compiler_params=pltpu.CompilerParams(vmem_limit_bytes=VMEM_BYTES),
        cost_estimate=pl.CostEstimate(
            flops=products * 2 * count * rows * 256 * 256, bytes_accessed=count * 256 * 256 * 2 * products, transcendentals=0
        ),
    )(*operands)


def swapped(value, section, apart):
    mask = 2**apart
    subs = lax.axis_size(SUB)
    if not LOCAL_SWAP:
        return lax.ppermute(value, SUB, [(i, i ^ mask) for i in range(subs)])
    pairs = [(section * subs + i, section * subs + (i ^ mask)) for i in range(subs)]
    return lax.ppermute(value, (LEVEL, SUB), pairs)


def general_body(rhs, lower_inv, lower_off, upper_inv, upper_off, ancestor, parent):
    levels = lax.axis_size(LEVEL)
    sub_count = lax.axis_size(SUB)
    sub_bits = sub_count.bit_length() - 1
    tier = lax.axis_index(LEVEL)
    sub = lax.axis_index(SUB)
    rhs, lower_inv, lower_off, upper_inv, upper_off = (
        value[0] for value in (rhs, lower_inv, lower_off, upper_inv, upper_off)
    )
    count, all_rows, width = rhs.shape
    rows = all_rows // CHUNKS
    parent_row = lax.dynamic_index_in_dim(parent, jnp.minimum(tier, levels - 2), 0, keepdims=False)
    parent_here = lax.dynamic_slice_in_dim(parent_row, sub * count, count)
    place = parent_here % count + jnp.where(parent_here // count == sub, 0, count)
    info = jnp.concatenate([place, tier[None]]).astype(jnp.int32)

    def shape(dtype):
        return jax.ShapeDtypeStruct((count, rows, width), dtype)

    fwd = [jnp.zeros((count, rows, width), BF16) for _ in range(CHUNKS)]
    upd = [jnp.zeros((count, rows, width), F32) for _ in range(CHUNKS)]
    sol = [jnp.zeros((count, rows, width), F32) for _ in range(CHUNKS)]
    incoming = [None] * CHUNKS
    above = [None] * CHUNKS
    top = levels - 1
    for section in range(top):
        for c in range(CHUNKS):
            if section == 0:
                kernel, operands = first_kernel, (info, rhs, lower_inv, lower_off, fwd[c], upd[c])
            else:
                kernel, operands = forward_kernel, (info, rhs, incoming[c], lower_inv, lower_off, fwd[c], upd[c])
            at = len(operands) - 2
            fwd[c], upd[c], home, far = call(
                kernel, section, c * rows, rows, operands,
                [shape(BF16), shape(F32), shape(F32), shape(BF16)], {at: 0, at + 1: 1},
                [pltpu.VMEM((2 * count, rows, width), F32)],
            )
            received = swapped(far, section, section % sub_bits)
            summed = (home + received.astype(F32)).astype(BF16)
            incoming[c] = lax.ppermute(summed, LEVEL, [(section, section + 1)])
    for c in range(CHUNKS):
        fwd[c], sol[c], solved = call(
            top_kernel, top, c * rows, rows,
            (info, rhs, incoming[c], lower_inv, upper_off, upper_inv, ancestor, fwd[c], sol[c]),
            [shape(BF16), shape(F32), shape(BF16)], {7: 0, 8: 1}, products=3,
        )
        above[c] = lax.ppermute(solved, LEVEL, [(top, top - 1)])
    for c in range(CHUNKS):
        (upd[c],) = call(top_update_kernel, top, c * rows, rows, (info, fwd[c], lower_off, upd[c]), [shape(F32)], {3: 0}, products=1)
    for section in reversed(range(top)):
        for c in range(CHUNKS):
            partner = swapped(above[c], section, section % sub_bits)
            sol[c], solved = call(
                backward_kernel, section, c * rows, rows,
                (info, fwd[c], above[c], partner, upper_off, upper_inv, sol[c]),
                [shape(F32), shape(BF16)], {6: 0},
            )
            if section:
                above[c] = lax.ppermute(solved, LEVEL, [(section, section - 1)])
    return jnp.concatenate(sol, axis=1)[None], jnp.concatenate(upd, axis=1)[None]


NODE_ROWS = 16
LOAD_NODES = 4
SMALL_VMEM_BYTES = 12 * 2**20
IN_ANY = pl.BlockSpec(memory_space=pl.ANY)
IN_HBM = pl.BlockSpec(memory_space=pltpu.HBM)


def rows_of(start):
    return pl.ds(pl.multiple_of(start, NODE_ROWS), NODE_ROWS)


def half_rows(array, sub):
    half = array.shape[1] // 2
    return pl.ds(pl.multiple_of(half * sub, half), half)


def flat(value):
    return value.reshape(value.shape[0] * value.shape[1], value.shape[2])


def pick(select, values):
    high = values.astype(BF16)
    low = (values - high.astype(F32)).astype(BF16)
    return dot(select, high) + dot(select, low)


def on_level(section):
    return pl.when(lax.axis_index(LEVEL) == section)


def off_level(section):
    return pl.when(lax.axis_index(LEVEL) != section)


def keep(section, kept, outs):
    @off_level(section)
    def _():
        for before, after in zip(kept, outs):
            after[...] = before[...]


def fill_tables(parent, select, choose):
    nodes = parent.shape[1]
    size = nodes * NODE_ROWS
    top = lax.axis_size(LEVEL) - 1
    level, shift = lax.axis_index(LEVEL), lax.axis_index(SUB) * (nodes // 2)

    def target(row, axis):
        shape = (nodes, size) if axis else (size, nodes)
        child = lax.broadcasted_iota(jnp.int32, shape, axis) // NODE_ROWS + shift
        child = jnp.where(child >= nodes, child - nodes, child)
        same = child == lax.broadcasted_iota(jnp.int32, shape, 1 - axis)
        row = row - shift
        row = jnp.where(row < 0, row + nodes, row)
        if axis:
            found = dot(row.astype(F32).astype(BF16), same.astype(F32).astype(BF16))
        else:
            found = jnp.sum(jnp.where(same, row.astype(F32), 0.0), axis=1, keepdims=True)
        place = lax.broadcasted_iota(jnp.int32, found.shape, axis)
        return found.astype(jnp.int32) * NODE_ROWS + lax.rem(place, NODE_ROWS)

    up = target(parent[pl.ds(jnp.minimum(level, top - 1), 1), :], 1)
    down = target(parent[pl.ds(jnp.maximum(level - 1, 0), 1), :], 0)
    index = lax.broadcasted_iota(jnp.int32, (size, size), 0)
    select[...] = (index == up).astype(F32).astype(BF16)
    index = lax.broadcasted_iota(jnp.int32, (size, size), 1)
    choose[...] = (index == down).astype(F32).astype(BF16)


def start_kernel(parent, rhs, inv, off, select, choose, rhs_own, rhs_sent, home, swap, merged, *refs):
    *updates, parent_here, inv_here, off_here, sems = refs
    count = inv.shape[0]
    chunks = len(updates) // 2
    size = count * NODE_ROWS
    level, sub = lax.axis_index(LEVEL), lax.axis_index(SUB)
    table = pltpu.make_async_copy(parent, parent_here, sems.at[0, 0])
    mine = pltpu.make_async_copy(rhs.at[:, half_rows(rhs, sub), :], rhs_own, sems.at[0, 1])
    other = pltpu.make_async_copy(rhs.at[:, half_rows(rhs, 1 - sub), :], rhs_sent, sems.at[0, 2])
    table.start()
    loads = []
    for group in range(count // LOAD_NODES):
        here = pl.ds(group * LOAD_NODES, LOAD_NODES)
        loads.append(pltpu.make_async_copy(inv.at[here], inv_here.at[here], sems.at[1, group]))
        loads.append(pltpu.make_async_copy(off.at[here], off_here.at[here], sems.at[2, group]))
        loads[-2].start()
        loads[-1].start()
        if group == 0:
            mine.start()
            other.start()
    table.wait()
    fill_tables(parent_here, select, choose)
    mine.wait()
    other.wait()

    @on_level(0)
    def _():
        for node in range(count):
            if node % LOAD_NODES == 0:
                loads[2 * (node // LOAD_NODES)].wait()
                loads[2 * (node // LOAD_NODES) + 1].wait()
            right_side = jnp.concatenate([rhs_own[node], rhs_sent[node]], axis=0).astype(BF16)
            forward = dot(right_side, inv_here[node]).astype(BF16)
            update = dot(forward, off_here[node])
            for c in range(2 * chunks):
                updates[c][node] = update[NODE_ROWS * c : NODE_ROWS * (c + 1)]
        chosen = select[:, :size]
        for c in range(chunks):
            home[2 * count * c : 2 * count * (c + 1)] = pick(chosen, flat(updates[c][...])).reshape(2 * count, *home.shape[1:])
            sums = pick(chosen, flat(updates[chunks + c][...])).astype(BF16).reshape(2 * count, *home.shape[1:])
            swap[2 * count * c : 2 * count * c + count] = sums[count:]
            swap[2 * count * c + count : 2 * count * (c + 1)] = sums[:count]

    @off_level(0)
    def _():
        for node in range(count):
            if node % LOAD_NODES == 0:
                loads[2 * (node // LOAD_NODES)].wait()
                loads[2 * (node // LOAD_NODES) + 1].wait()
            merged[node] = dot(inv_here[node], off_here[node]).astype(BF16)


def merge_kernel(levels, low_inv, up_inv, up_off, ancestor, packed, *scratch):
    low_here, up_here, off_here, rows, sems = scratch
    count = low_inv.shape[0]
    level, sub = lax.axis_index(LEVEL), lax.axis_index(SUB)

    @pl.when((level == levels[0]) | (level == levels[1]))
    def _():
        loads = []
        for group in range(count // LOAD_NODES):
            here = pl.ds(group * LOAD_NODES, LOAD_NODES)
            loads.append(pltpu.make_async_copy(up_inv.at[here], up_here.at[here], sems.at[1, group]))
            loads.append(pltpu.make_async_copy(low_inv.at[here], low_here.at[here], sems.at[0, group]))
            loads.append(pltpu.make_async_copy(up_off.at[here], off_here.at[here], sems.at[2, group]))
        loads.append(pltpu.make_async_copy(ancestor.at[:, half_rows(ancestor, 1 - sub), :], rows, sems.at[3, 0]))
        for load in loads:
            load.start()
        for node in range(count):
            if node % LOAD_NODES == 0:
                for load in loads[3 * (node // LOAD_NODES) : 3 * (node // LOAD_NODES) + 3]:
                    load.wait()
            packed[node] = dot(low_here[node], up_here[node]).astype(BF16)
            packed[count + node] = dot(off_here[node], up_here[node]).astype(BF16)
        loads[-1].wait()
        packed[2 * count :] = rows[...].reshape(packed.shape[0] - 2 * count, *packed.shape[1:])


def residue_of(c, rhs_own, rhs_far, incoming, node):
    count = rhs_own.shape[0]
    rows = slice(NODE_ROWS * c, NODE_ROWS * (c + 1))
    right_side = rhs_own[node, rows, :] if node < count else rhs_far[node - count, rows, :]
    return (right_side - incoming[node].astype(F32)).astype(BF16)


def tier_role(c, at):
    count = at["rhs_own"].shape[0]
    own, far = at["own", c], at["far", c]
    for node in range(2 * count):
        value = residue_of(c, at["rhs_own"], at["rhs_far"], at["received"], node)
        at["residue", c][node] = value
        if node < count:
            own[node] = dot(value, at["up_own"][node])
        else:
            far[node - count] = dot(value, at["up_far"][node - count])
    updates = jnp.concatenate([flat(own[...]), flat(far[...])], axis=0)
    at["sent"][...] = pick(at["select"][...], updates).astype(BF16).reshape(at["sent"].shape)


def send_solved(c, at):
    if "sent" in at:
        solved = jnp.concatenate([flat(at["sol_own", c][...]), flat(at["sol_far", c][...])], axis=0).astype(BF16)
        at["sent"][...] = dot(at["choose"][...], solved).astype(BF16).reshape(at["sent"].shape)


def top_role(c, at):
    count = at["rhs_own"].shape[0]
    base = at["top_base", c]
    for node in range(2 * count):
        value = residue_of(c, at["rhs_own"], at["rhs_far"], at["received"], node)
        at["residue", c][node] = value
        if node < count:
            at["sol_own", c][node] = dot(value, at["high_own"][node]) - base[node]
        else:
            at["sol_far", c][node - count] = dot(value, at["high_far"][node - count]) - base[node]
    send_solved(c, at)


def back_role(c, at, group="high"):
    count = at["sol_own", c].shape[0]
    base, above = at[group + "_base", c], at["received"]
    own, far = at[group + "_own"], at[group + "_far"]
    for node in range(count):
        at["sol_own", c][node] = base[node] - dot(above[node], own[count + node])
        at["sol_far", c][node] = base[count + node] - dot(above[count + node], far[count + node])
    send_solved(c, at)


def low_back_role(c, at):
    back_role(c, at, "low")


def sum_role(c, at):
    rows = slice(c * at["sent"].shape[0], (c + 1) * at["sent"].shape[0])
    at["sent"][...] = (at["home"][rows] + at["swapped"][rows].astype(F32)).astype(BF16)


ROLES = {"tier": tier_role, "top": top_role, "back": back_role, "low": low_back_role, "sum": sum_role}
READS = {
    "tier": ("rhs_own", "rhs_far", "received", "up_own", "up_far", "select"),
    "top": ("rhs_own", "rhs_far", "received", "high_own", "high_far", "choose", "top_base"),
    "back": ("received", "high_own", "high_far", "choose", "high_base"),
    "low": ("received", "low_own", "low_far", "choose", "low_base"),
    "sum": ("home", "swapped"),
}
WRITES = {
    "tier": ("residue", "own", "far"),
    "top": ("residue", "sol_own", "sol_far"),
    "back": ("sol_own", "sol_far"),
    "low": ("sol_own", "sol_far"),
    "sum": (),
}


def step_kernel(plan, in_keys, out_keys, kept_keys, *refs):
    reads = dict(zip(in_keys, refs))
    kept = dict(zip(kept_keys, refs[len(in_keys) :]))
    outs = dict(zip(out_keys, refs[len(in_keys) + len(kept_keys) :]))
    for level, role, c in plan:
        writes = [(name, c) for name in WRITES[role]]
        keep(level, [kept[key] for key in writes if key in kept], [outs[key] for key in writes if key in kept])
        pl.when(lax.axis_index(LEVEL) == level)(functools.partial(ROLES[role], c, {**reads, **outs}))


def step(plan, state, sends=True):
    nodes = state["nodes"]
    in_keys, out_keys = [], []
    for _, role, c in plan:
        for name in READS[role]:
            key = (name, c) if name.endswith("_base") else name
            if key not in in_keys:
                in_keys.append(key)
        out_keys += [(name, c) for name in WRITES[role]]
    kept_keys = [key for key in out_keys if key in state]
    width = state["rhs_own"].shape[2]
    outs = []
    for name, _ in out_keys:
        of, dtype = (nodes, BF16) if name == "residue" else (nodes // 2, F32)
        outs.append(jax.ShapeDtypeStruct((of, NODE_ROWS, width), dtype))
    aliases = {len(in_keys) + i: out_keys.index(key) for i, key in enumerate(kept_keys)}
    all_outs = out_keys + (["sent"] if sends else [])
    if sends:
        outs.append(jax.ShapeDtypeStruct((nodes, NODE_ROWS, width), BF16))
    operands = [state[key] for key in in_keys + kept_keys]
    results = run(functools.partial(step_kernel, plan, in_keys, all_outs, kept_keys), operands, outs, aliases)
    state.update(zip(out_keys, results))
    return results[-1] if sends else None


def high_base_kernel(section, own, far, *refs):
    chunks = len(refs) // 2
    residue, base = refs[:chunks], refs[chunks:]
    count = residue[0].shape[0] // 2

    @on_level(section)
    def _():
        for c in range(chunks):
            for node in range(count):
                base[c][node] = dot(residue[c][node], own[node])
                base[c][count + node] = dot(residue[c][count + node], far[node])


def low_base_kernel(rhs_own, rhs_far, own, far, *refs):
    chunks = len(refs) // 2
    residue, base = refs[:chunks], refs[chunks:]
    count = rhs_own.shape[0]
    level = lax.axis_index(LEVEL)

    @pl.when(level == 0)
    def _():
        for node in range(count):
            mine = dot(rhs_own[node].astype(BF16), own[node])
            other = dot(rhs_far[node].astype(BF16), far[node])
            for c in range(chunks):
                base[c][node] = mine[NODE_ROWS * c : NODE_ROWS * (c + 1)]
                base[c][count + node] = other[NODE_ROWS * c : NODE_ROWS * (c + 1)]

    @pl.when((level != 0) & (level < lax.axis_size(LEVEL) - 2))
    def _():
        for c in range(chunks):
            for node in range(count):
                base[c][node] = dot(residue[c][node], own[node])
                base[c][count + node] = dot(residue[c][count + node], far[node])


def ancestor_kernel(section, ancestor, own, far, *refs):
    *bases, here, sem = refs
    count, half, _ = here.shape
    sub = lax.axis_index(SUB)

    @on_level(section)
    def _():
        load = pltpu.make_async_copy(ancestor.at[:, half_rows(ancestor, sub), :], here, sem.at[0])
        load.start()
        load.wait()
        for node in range(count):
            per = far.shape[1] // half
            other = far[2 * count + node // per, half * (node % per) : half * (node % per + 1), :]
            mine = dot(here[node], own[count + node])
            other = dot(other, far[count + node])
            for c, base in enumerate(bases):
                base[node] = mine[NODE_ROWS * c : NODE_ROWS * (c + 1)]
                base[count + node] = other[NODE_ROWS * c : NODE_ROWS * (c + 1)]


def top_tier_update_kernel(section, residue, step_own, step_far, kept_o, kept_f, upd_own, upd_far):
    count = step_own.shape[0]
    keep(section, (kept_o, kept_f), (upd_own, upd_far))

    @on_level(section)
    def _():
        for node in range(count):
            upd_own[node] = dot(residue[node], step_own[node])
            upd_far[node] = dot(residue[count + node], step_far[node])


def put(c, own, far, out, sems):
    sub = lax.axis_index(SUB)
    half = out.shape[1] // 2
    first = pltpu.make_async_copy(own, out.at[:, rows_of(half * sub + NODE_ROWS * c), :], sems.at[0])
    second = pltpu.make_async_copy(far, out.at[:, rows_of(half * (1 - sub) + NODE_ROWS * c), :], sems.at[1])
    first.start()
    second.start()
    first.wait()
    second.wait()


def place_kernel(c, here, far, other, *refs):
    out, sems = refs[-2:]
    put(c, here, other, out, sems)


def place_bottom_kernel(c, here, far, other, *refs):
    out, sems = refs[-2:]

    @on_level(0)
    def _():
        put(c, here, far, out, sems)

    @off_level(0)
    def _():
        put(c, here, other, out, sems)


def run(kernel, operands, outs, aliases=None, products=32, whole=None, scratch=(), raw=()):
    in_specs = [IN_HBM] * len(raw) + [IN_VMEM] * len(operands)
    operands = [*(pltpu.with_memory_space_constraint(value, pltpu.HBM) for value in raw), *(pltpu.with_memory_space_constraint(value, pltpu.VMEM) for value in operands)]
    out_specs = [IN_VMEM] * len(outs)
    out_shape = [pltpu.VMEM(out.shape, out.dtype) for out in outs]
    aliases = dict(aliases or {})
    if whole is not None:
        shape, before = whole
        if before is not None:
            aliases[len(operands)] = len(outs)
            operands.append(before)
            in_specs.append(IN_ANY)
        out_shape.append(shape)
        out_specs.append(IN_ANY)
    return pl.pallas_call(
        kernel,
        in_specs=in_specs,
        out_specs=out_specs,
        out_shape=out_shape,
        input_output_aliases=aliases,
        scratch_shapes=scratch,
        compiler_params=pltpu.CompilerParams(vmem_limit_bytes=SMALL_VMEM_BYTES),
        cost_estimate=pl.CostEstimate(
            flops=products * 2 * NODE_ROWS * 256 * 256, bytes_accessed=256 * 256 * 2 * products, transcendentals=0
        ),
    )(*operands)


def exchanged(value):
    return lax.ppermute(value, SUB, [(0, 1), (1, 0)])


def pair_body(rhs, lower_inv, lower_off, upper_inv, upper_off, ancestor, parent):
    levels = lax.axis_size(LEVEL)
    top = levels - 1
    rhs, lower_inv, lower_off, upper_inv, upper_off = (
        value[0] for value in (rhs, lower_inv, lower_off, upper_inv, upper_off)
    )
    count, all_rows, width = rhs.shape
    half = all_rows // 2
    chunks = half // NODE_ROWS
    nodes = 2 * count
    size = nodes * NODE_ROWS

    def shape(of, dtype):
        return jax.ShapeDtypeStruct((of, NODE_ROWS, width), dtype)

    def passed(value, pairs):
        sources = [i for i in range(levels) if i not in dict(pairs)]
        targets = [i for i in range(levels) if i not in [to for _, to in pairs]]
        fill = min(
            (list(zip(sources, order)) for order in itertools.permutations(targets)),
            key=lambda extra: (sum(a == b for a, b in extra), sum(abs(a - b) for a, b in extra)),
        )
        return lax.ppermute(value, LEVEL, pairs + fill)

    def after(value, *earlier):
        return lax.optimization_barrier((value, *earlier))[0]

    matrices = jax.ShapeDtypeStruct(lower_inv.shape, BF16)
    table = jax.ShapeDtypeStruct((size, size), BF16)
    half_shape = jax.ShapeDtypeStruct((count, half, width), F32)
    block = pltpu.VMEM(lower_inv.shape, BF16)
    state = {"nodes": nodes}
    select, choose, rhs_own, rhs_sent, home, swap, up_own, *updates = run(
        start_kernel, (),
        [table, table, half_shape, half_shape, shape(chunks * nodes, F32), shape(chunks * nodes, BF16), matrices]
        + [shape(count, F32)] * (2 * chunks),
        raw=(parent, rhs, lower_inv, lower_off),
        scratch=[pltpu.VMEM(parent.shape, parent.dtype), block, block, pltpu.SemaphoreType.DMA((3, max(count // LOAD_NODES, 3)))],
    )
    state.update(select=select, choose=choose, rhs_own=rhs_own, home=home, up_own=up_own, swapped=exchanged(swap))
    for c in range(chunks):
        state["own", c], state["far", c] = updates[c], updates[chunks + c]

    packed_shape = (2 * count + count * half // width, width, width)
    merge_scratch = [block, block, block, pltpu.VMEM((count, half, width), BF16), pltpu.SemaphoreType.DMA((4, count // LOAD_NODES))]

    def merged(levels_here, sent):
        low, *others = lax.optimization_barrier((lower_inv, upper_inv, upper_off, ancestor, sent))
        return run(
            functools.partial(merge_kernel, levels_here), (), [jax.ShapeDtypeStruct(packed_shape, BF16)],
            raw=(low, *others[:3]), scratch=merge_scratch, products=512,
        )[0]

    whole = jax.ShapeDtypeStruct(rhs.shape, F32)
    sems = [pltpu.SemaphoreType.DMA((2,))]
    update, solved = None, None
    for k in range(2 * top + chunks):
        plan, pairs = [], []
        for c in range(chunks):
            tier = k - c
            if 0 <= tier < top:
                plan.append((tier, "sum" if tier == 0 else "tier", c))
                pairs.append((tier, tier + 1))
            elif tier == top:
                plan.append((top, "top", c))
                pairs.append((top, top - 1))
            elif top < tier <= 2 * top:
                low = 2 * top - tier
                plan.append((low, "back" if low == top - 1 else "low", c))
                if low:
                    pairs.append((low, low - 1))
        sent = step(plan, state, sends=bool(pairs))
        if not pairs:
            break
        received = passed(sent, pairs)
        done = []
        if k == 0:
            state["up_far"] = exchanged(after(up_own, sent))
            state["rhs_far"] = exchanged(after(rhs_sent, sent))
            state["high_own"] = merged((top - 1, top), sent)
            done = [state["high_own"]]
        if k == 1:
            state["high_far"] = exchanged(after(state["high_own"], sent))
        if k == top - 1:
            bases = run(
                functools.partial(ancestor_kernel, top),
                (state["high_own"], state["high_far"]),
                [shape(nodes, F32)] * chunks,
                raw=(after(ancestor, sent),),
                scratch=[pltpu.VMEM((count, half, width), BF16), pltpu.SemaphoreType.DMA((1,))],
            )
            state.update({("top_base", c): bases[c] for c in range(chunks)})
            state["low_own"] = merged((0, 1), sent)
            done = [*bases, state["low_own"]]
        if k == top:
            state["low_far"] = exchanged(after(state["low_own"], sent))
            residues = [state["residue", c] for c in range(chunks)]
            bases = run(
                functools.partial(high_base_kernel, top - 1),
                (after(state["high_own"], sent), state["high_far"], *residues),
                [shape(nodes, F32)] * chunks,
            )
            state.update({("high_base", c): bases[c] for c in range(chunks)})
            done = bases
        if k == top + 1:
            residues = [state["residue", c] for c in range(chunks)]
            bases = run(
                low_base_kernel,
                (after(rhs_own, sent), state["rhs_far"], state["low_own"], state["low_far"], *residues),
                [shape(nodes, F32)] * chunks,
            )
            state.update({("low_base", c): bases[c] for c in range(chunks)})
            done = bases
        if k == top + chunks - 1:
            for c in range(chunks):
                state["own", c], state["far", c] = run(
                    functools.partial(top_tier_update_kernel, top),
                    (after(state["residue", c], sent), state["up_own"], state["up_far"], state["own", c], state["far", c]),
                    [shape(count, F32), shape(count, F32)],
                    {3: 0, 4: 1},
                )
            done = [*done, *(state["far", c] for c in range(chunks))]
        if k == top + chunks:
            upd_other = [exchanged(after(state["far", c], sent)) for c in range(chunks)]
        if k == 2 * top + chunks - 2:
            for c in range(chunks):
                (update,) = run(
                    functools.partial(place_bottom_kernel, c),
                    (state["own", c], after(state["far", c], sent), upd_other[c]),
                    [], whole=(whole, update), scratch=sems, products=1,
                )
            for c in range(chunks - 1):
                (solved,) = run(
                    functools.partial(place_kernel, c),
                    (state["sol_own", c], state["sol_far", c], exchanged(state["sol_far", c])),
                    [], whole=(whole, solved), scratch=sems, products=1,
                )
            done = [update] + ([] if solved is None else [solved])
        if done:
            received, *done = lax.optimization_barrier((received, *done))
            if k == 2 * top + chunks - 2:
                update, solved = done[0], done[1] if chunks > 1 else None
        state["received"] = received
    c = chunks - 1
    (solved,) = run(
        functools.partial(place_kernel, c),
        (state["sol_own", c], state["sol_far", c], exchanged(state["sol_far", c])),
        [], whole=(whole, solved), scratch=sems, products=1,
    )
    return solved[None], update[None]


def solution(mesh):
    placed = (
        P(LEVEL, SUB, "rhs", None),
        P(LEVEL, SUB, None, None),
        P(LEVEL, SUB, None, None),
        P(LEVEL, SUB, None, None),
        P(LEVEL, SUB, None, None),
        P(SUB, "rhs", None),
        P(),
    )
    return jax.shard_map(
        pair_body if mesh.shape[SUB] == 2 else general_body,
        mesh=mesh,
        in_specs=placed,
        out_specs=(P(LEVEL, SUB, "rhs", None), P(LEVEL, SUB, "rhs", None)),
        check_vma=False,
    )
```

```python
import functools
import itertools

import jax
import jax.numpy as jnp
from jax import lax
from jax.experimental import pallas as pl
from jax.experimental.pallas import tpu as pltpu
from jax.sharding import PartitionSpec as P

CHUNKS = 2
LOCAL_SWAP = False
VMEM_BYTES = 24 * 2**20

LEVEL, SUB = "level", "sub"
BF16 = jnp.bfloat16
F32 = jnp.float32
IN_VMEM = pl.BlockSpec(memory_space=pltpu.VMEM)
IN_SMEM = pl.BlockSpec(memory_space=pltpu.SMEM)


def dot(left, right):
    return jnp.dot(left, right, preferred_element_type=F32)


def forward_kernel(section, start, rows, info, rhs, incoming, inv, off, kept_f, kept_u, fwd, upd, home, far, total):
    count = inv.shape[0]

    @pl.when(info[count] != section)
    def _():
        fwd[...] = kept_f[...]
        upd[...] = kept_u[...]

    @pl.when(info[count] == section)
    def _():
        total[...] = jnp.zeros_like(total)
        for node in range(count):
            right_side = rhs[node, pl.ds(start, rows), :]
            if incoming is not None:
                right_side = right_side - incoming[node].astype(F32)
            forward = dot(right_side.astype(BF16), inv[node]).astype(BF16)
            fwd[node] = forward
            update = dot(forward, off[node])
            upd[node] = update
            total[info[node]] += update
        home[...] = total[:count]
        far[...] = total[count:].astype(BF16)


def first_kernel(section, start, rows, info, rhs, inv, off, kept_f, kept_u, fwd, upd, home, far, total):
    forward_kernel(section, start, rows, info, rhs, None, inv, off, kept_f, kept_u, fwd, upd, home, far, total)


def top_kernel(section, start, rows, info, rhs, incoming, inv, up_off, up_inv, ancestor, kept_f, kept_s, fwd, sol, sol_bf):
    count = inv.shape[0]

    @pl.when(info[count] != section)
    def _():
        fwd[...] = kept_f[...]
        sol[...] = kept_s[...]

    @pl.when(info[count] == section)
    def _():
        for node in range(count):
            right_side = rhs[node, pl.ds(start, rows), :] - incoming[node].astype(F32)
            forward = dot(right_side.astype(BF16), inv[node]).astype(BF16)
            fwd[node] = forward
            above = dot(ancestor[node, pl.ds(start, rows), :], up_off[node])
            reduced = (forward.astype(F32) - above).astype(BF16)
            solved = dot(reduced, up_inv[node])
            sol[node] = solved
            sol_bf[node] = solved.astype(BF16)


def top_update_kernel(section, start, rows, info, fwd, off, kept_u, upd):
    count = off.shape[0]

    @pl.when(info[count] != section)
    def _():
        upd[...] = kept_u[...]

    @pl.when(info[count] == section)
    def _():
        for node in range(count):
            upd[node] = dot(fwd[node], off[node])


def backward_kernel(section, start, rows, info, fwd, own, partner, up_off, up_inv, kept_s, sol, sol_bf):
    count = up_inv.shape[0]

    @pl.when(info[count] != section)
    def _():
        sol[...] = kept_s[...]

    @pl.when(info[count] == section)
    def _():
        for node in range(count):
            place = info[node]
            at_home = place < count
            slot = jnp.where(at_home, place, place - count)
            above = jnp.where(at_home, own[slot], partner[slot])
            reduced = (fwd[node].astype(F32) - dot(above, up_off[node])).astype(BF16)
            solved = dot(reduced, up_inv[node])
            sol[node] = solved
            sol_bf[node] = solved.astype(BF16)


def call(kernel, section, start, rows, operands, outs, aliases, scratch=(), products=2):
    count = operands[1].shape[0]
    return pl.pallas_call(
        functools.partial(kernel, section, start, rows),
        in_specs=[IN_SMEM] + [IN_VMEM] * (len(operands) - 1),
        out_specs=[IN_VMEM] * len(outs),
        out_shape=outs,
        scratch_shapes=scratch,
        input_output_aliases=aliases,
        compiler_params=pltpu.CompilerParams(vmem_limit_bytes=VMEM_BYTES),
        cost_estimate=pl.CostEstimate(
            flops=products * 2 * count * rows * 256 * 256, bytes_accessed=count * 256 * 256 * 2 * products, transcendentals=0
        ),
    )(*operands)


def swapped(value, section, apart):
    mask = 2**apart
    subs = lax.axis_size(SUB)
    if not LOCAL_SWAP:
        return lax.ppermute(value, SUB, [(i, i ^ mask) for i in range(subs)])
    pairs = [(section * subs + i, section * subs + (i ^ mask)) for i in range(subs)]
    return lax.ppermute(value, (LEVEL, SUB), pairs)


def general_body(rhs, lower_inv, lower_off, upper_inv, upper_off, ancestor, parent):
    levels = lax.axis_size(LEVEL)
    sub_count = lax.axis_size(SUB)
    sub_bits = sub_count.bit_length() - 1
    tier = lax.axis_index(LEVEL)
    sub = lax.axis_index(SUB)
    rhs, lower_inv, lower_off, upper_inv, upper_off = (
        value[0] for value in (rhs, lower_inv, lower_off, upper_inv, upper_off)
    )
    count, all_rows, width = rhs.shape
    rows = all_rows // CHUNKS
    parent_row = lax.dynamic_index_in_dim(parent, jnp.minimum(tier, levels - 2), 0, keepdims=False)
    parent_here = lax.dynamic_slice_in_dim(parent_row, sub * count, count)
    place = parent_here % count + jnp.where(parent_here // count == sub, 0, count)
    info = jnp.concatenate([place, tier[None]]).astype(jnp.int32)

    def shape(dtype):
        return jax.ShapeDtypeStruct((count, rows, width), dtype)

    fwd = [jnp.zeros((count, rows, width), BF16) for _ in range(CHUNKS)]
    upd = [jnp.zeros((count, rows, width), F32) for _ in range(CHUNKS)]
    sol = [jnp.zeros((count, rows, width), F32) for _ in range(CHUNKS)]
    incoming = [None] * CHUNKS
    above = [None] * CHUNKS
    top = levels - 1
    for section in range(top):
        for c in range(CHUNKS):
            if section == 0:
                kernel, operands = first_kernel, (info, rhs, lower_inv, lower_off, fwd[c], upd[c])
            else:
                kernel, operands = forward_kernel, (info, rhs, incoming[c], lower_inv, lower_off, fwd[c], upd[c])
            at = len(operands) - 2
            fwd[c], upd[c], home, far = call(
                kernel, section, c * rows, rows, operands,
                [shape(BF16), shape(F32), shape(F32), shape(BF16)], {at: 0, at + 1: 1},
                [pltpu.VMEM((2 * count, rows, width), F32)],
            )
            received = swapped(far, section, section % sub_bits)
            summed = (home + received.astype(F32)).astype(BF16)
            incoming[c] = lax.ppermute(summed, LEVEL, [(section, section + 1)])
    for c in range(CHUNKS):
        fwd[c], sol[c], solved = call(
            top_kernel, top, c * rows, rows,
            (info, rhs, incoming[c], lower_inv, upper_off, upper_inv, ancestor, fwd[c], sol[c]),
            [shape(BF16), shape(F32), shape(BF16)], {7: 0, 8: 1}, products=3,
        )
        above[c] = lax.ppermute(solved, LEVEL, [(top, top - 1)])
    for c in range(CHUNKS):
        (upd[c],) = call(top_update_kernel, top, c * rows, rows, (info, fwd[c], lower_off, upd[c]), [shape(F32)], {3: 0}, products=1)
    for section in reversed(range(top)):
        for c in range(CHUNKS):
            partner = swapped(above[c], section, section % sub_bits)
            sol[c], solved = call(
                backward_kernel, section, c * rows, rows,
                (info, fwd[c], above[c], partner, upper_off, upper_inv, sol[c]),
                [shape(F32), shape(BF16)], {6: 0},
            )
            if section:
                above[c] = lax.ppermute(solved, LEVEL, [(section, section - 1)])
    return jnp.concatenate(sol, axis=1)[None], jnp.concatenate(upd, axis=1)[None]


NODE_ROWS = 8
LOAD_NODES = 4
COSTS = [10**9,3*10**10,3*10**10]+[5*10**9]*5
SMALL_VMEM_BYTES = 12 * 2**20
IN_ANY = pl.BlockSpec(memory_space=pl.ANY)
IN_HBM = pl.BlockSpec(memory_space=pltpu.HBM)


def rows_of(start):
    return pl.ds(pl.multiple_of(start, NODE_ROWS), NODE_ROWS)


def half_rows(array, sub):
    half = array.shape[1] // 2
    return pl.ds(pl.multiple_of(half * sub, half), half)


def flat(value):
    return value.reshape(value.shape[0] * value.shape[1], value.shape[2])


def pick(select, values):
    return dot(select, values.astype(BF16))


def on_level(section):
    return pl.when(lax.axis_index(LEVEL) == section)


def off_level(section):
    return pl.when(lax.axis_index(LEVEL) != section)


def keep(section, kept, outs):
    @off_level(section)
    def _():
        for before, after in zip(kept, outs):
            after[...] = before[...]


def fill_tables(parent, select, choose):
    nodes = parent.shape[1]
    size = nodes * NODE_ROWS
    top = lax.axis_size(LEVEL) - 1
    level, shift = lax.axis_index(LEVEL), lax.axis_index(SUB) * (nodes // 2)

    def target(row, axis):
        shape = (nodes, size) if axis else (size, nodes)
        child = lax.broadcasted_iota(jnp.int32, shape, axis) // NODE_ROWS + shift
        child = jnp.where(child >= nodes, child - nodes, child)
        same = child == lax.broadcasted_iota(jnp.int32, shape, 1 - axis)
        row = row - shift
        row = jnp.where(row < 0, row + nodes, row)
        if axis:
            found = dot(row.astype(F32).astype(BF16), same.astype(F32).astype(BF16))
        else:
            found = jnp.sum(jnp.where(same, row.astype(F32), 0.0), axis=1, keepdims=True)
        place = lax.broadcasted_iota(jnp.int32, found.shape, axis)
        return found.astype(jnp.int32) * NODE_ROWS + lax.rem(place, NODE_ROWS)

    up = target(parent[pl.ds(jnp.minimum(level, top - 1), 1), :], 1)
    down = target(parent[pl.ds(jnp.maximum(level - 1, 0), 1), :], 0)
    index = lax.broadcasted_iota(jnp.int32, (size, size), 0)
    select[...] = (index == up).astype(F32).astype(BF16)
    index = lax.broadcasted_iota(jnp.int32, (size, size), 1)
    choose[...] = (index == down).astype(F32).astype(BF16)


def start_kernel(parent, rhs, inv, off, select, choose, rhs_own, rhs_sent, home, swap, merged, *refs):
    *updates, parent_here, inv_here, off_here, sems = refs
    count = inv.shape[0]
    chunks = len(updates) // 2
    size = count * NODE_ROWS
    level, sub = lax.axis_index(LEVEL), lax.axis_index(SUB)
    table = pltpu.make_async_copy(parent, parent_here, sems.at[0, 0])
    mine = pltpu.make_async_copy(rhs.at[:, half_rows(rhs, sub), :], rhs_own, sems.at[0, 1])
    other = pltpu.make_async_copy(rhs.at[:, half_rows(rhs, 1 - sub), :], rhs_sent, sems.at[0, 2])
    table.start()
    loads = []
    for group in range(count // LOAD_NODES):
        here = pl.ds(group * LOAD_NODES, LOAD_NODES)
        loads.append(pltpu.make_async_copy(inv.at[here], inv_here.at[here], sems.at[1, group]))
        loads.append(pltpu.make_async_copy(off.at[here], off_here.at[here], sems.at[2, group]))
        loads[-2].start()
        loads[-1].start()
        if group == 0:
            mine.start()
            other.start()
    table.wait()
    fill_tables(parent_here, select, choose)
    mine.wait()
    other.wait()

    @on_level(0)
    def _():
        for node in range(count):
            if node % LOAD_NODES == 0:
                loads[2 * (node // LOAD_NODES)].wait()
                loads[2 * (node // LOAD_NODES) + 1].wait()
            right_side = jnp.concatenate([rhs_own[node], rhs_sent[node]], axis=0).astype(BF16)
            forward = dot(right_side, inv_here[node]).astype(BF16)
            update = dot(forward, off_here[node])
            for c in range(2 * chunks):
                updates[c][node] = update[NODE_ROWS * c : NODE_ROWS * (c + 1)]
        chosen = select[:, :size]
        for c in range(chunks):
            home[2 * count * c : 2 * count * (c + 1)] = pick(chosen, flat(updates[c][...])).reshape(2 * count, *home.shape[1:])
            sums = pick(chosen, flat(updates[chunks + c][...])).reshape(2 * count, *home.shape[1:]).astype(BF16)
            swap[2 * count * c : 2 * count * c + count] = sums[count:]
            swap[2 * count * c + count : 2 * count * (c + 1)] = sums[:count]

    @off_level(0)
    def _():
        for node in range(count):
            if node % LOAD_NODES == 0:
                loads[2 * (node // LOAD_NODES)].wait()
                loads[2 * (node // LOAD_NODES) + 1].wait()
            merged[node] = dot(inv_here[node], off_here[node]).astype(BF16)


def merge_kernel(low_inv, up_inv, up_off, ancestor, packed, *scratch):
    low_here, up_here, off_here, rows, sems = scratch
    count = low_inv.shape[0]
    sub = lax.axis_index(SUB)
    loads = []
    for group in range(count // LOAD_NODES):
        here = pl.ds(group * LOAD_NODES, LOAD_NODES)
        loads.append(pltpu.make_async_copy(up_inv.at[here], up_here.at[here], sems.at[1, group]))
        loads.append(pltpu.make_async_copy(low_inv.at[here], low_here.at[here], sems.at[0, group]))
        loads.append(pltpu.make_async_copy(up_off.at[here], off_here.at[here], sems.at[2, group]))
    loads.append(pltpu.make_async_copy(ancestor.at[:, half_rows(ancestor, 1 - sub), :], rows, sems.at[3, 0]))
    for load in loads:
        load.start()
    for node in range(count):
        if node % LOAD_NODES == 0:
            for load in loads[3 * (node // LOAD_NODES) : 3 * (node // LOAD_NODES) + 3]:
                load.wait()
        packed[node] = dot(low_here[node], up_here[node]).astype(BF16)
        packed[count + node] = dot(off_here[node], up_here[node]).astype(BF16)
    loads[-1].wait()
    packed[2 * count :] = rows[...].reshape(packed.shape[0] - 2 * count, *packed.shape[1:])


def residue_of(c, rhs_own, rhs_far, incoming, node):
    count = rhs_own.shape[0]
    rows = slice(NODE_ROWS * c, NODE_ROWS * (c + 1))
    right_side = rhs_own[node, rows, :] if node < count else rhs_far[node - count, rows, :]
    return (right_side - incoming[node].astype(F32)).astype(BF16)


def tier_role(c, at):
    count = at["rhs_own"].shape[0]
    own, far = at["own", c], at["far", c]
    for node in range(2 * count):
        value = residue_of(c, at["rhs_own"], at["rhs_far"], at["received"], node)
        at["residue", c][node] = value.astype(F32)
        if node < count:
            own[node] = dot(value, at["up_own"][node])
        else:
            far[node - count] = dot(value, at["up_far"][node - count])
    updates = jnp.concatenate([flat(own[...]), flat(far[...])], axis=0)
    at["sent"][...] = pick(at["select"][...], updates).reshape(at["sent"].shape).astype(BF16)


def send_solved(c, at):
    if "sent" in at:
        solved = jnp.concatenate([flat(at["sol_own", c][...]), flat(at["sol_far", c][...])], axis=0).astype(BF16)
        at["sent"][...] = dot(at["choose"][...], solved).reshape(at["sent"].shape).astype(BF16)


def top_role(c, at):
    count = at["rhs_own"].shape[0]
    base = at["top_base", c]
    for node in range(2 * count):
        value = residue_of(c, at["rhs_own"], at["rhs_far"], at["received"], node)
        at["residue", c][node] = value.astype(F32)
        if node < count:
            at["sol_own", c][node] = dot(value, at["down_own"][node]) - base[node]
        else:
            at["sol_far", c][node - count] = dot(value, at["down_far"][node - count]) - base[node]
    send_solved(c, at)


def back_role(c, at):
    count = at["sol_own", c].shape[0]
    base, above = at["low_base", c], at["received"]
    for node in range(count):
        at["sol_own", c][node] = base[node] - dot(above[node], at["down_own"][count + node])
        at["sol_far", c][node] = base[count + node] - dot(above[count + node], at["down_far"][count + node])
    send_solved(c, at)


def sum_role(c, at):
    rows = slice(c * at["sent"].shape[0], (c + 1) * at["sent"].shape[0])
    at["sent"][...] = (at["home"][rows] + at["swapped"][rows].astype(F32)).astype(BF16)


ROLES = {"tier": tier_role, "top": top_role, "back": back_role, "sum": sum_role}
READS = {
    "tier": ("rhs_own", "rhs_far", "received", "up_own", "up_far", "select"),
    "top": ("rhs_own", "rhs_far", "received", "down_own", "down_far", "choose", "top_base"),
    "back": ("received", "down_own", "down_far", "choose", "low_base"),
    "sum": ("home", "swapped"),
}
WRITES = {
    "tier": ("residue", "own", "far"),
    "top": ("residue", "sol_own", "sol_far"),
    "back": ("sol_own", "sol_far"),
    "sum": (),
}


def step_kernel(plan, in_keys, out_keys, kept_keys, *refs):
    reads = dict(zip(in_keys, refs))
    kept = dict(zip(kept_keys, refs[len(in_keys) :]))
    outs = dict(zip(out_keys, refs[len(in_keys) + len(kept_keys) :]))
    for level, role, c in plan:
        writes = [(name, c) for name in WRITES[role]]
        keep(level, [kept[key] for key in writes if key in kept], [outs[key] for key in writes if key in kept])
        pl.when(lax.axis_index(LEVEL) == level)(functools.partial(ROLES[role], c, {**reads, **outs}))


def step(plan, state, sends=True, flops=10**9):
    nodes = state["nodes"]
    in_keys, out_keys = [], []
    for _, role, c in plan:
        for name in READS[role]:
            key = (name, c) if name.endswith("_base") else name
            if key not in in_keys:
                in_keys.append(key)
        out_keys += [(name, c) for name in WRITES[role]]
    kept_keys = [key for key in out_keys if key in state]
    width = state["rhs_own"].shape[2]
    outs = []
    for name, _ in out_keys:
        of = nodes if name == "residue" else nodes // 2
        outs.append(jax.ShapeDtypeStruct((of, NODE_ROWS, width), F32))
    aliases = {len(in_keys) + i: out_keys.index(key) for i, key in enumerate(kept_keys)}
    all_outs = out_keys + (["sent"] if sends else [])
    if sends:
        outs.append(jax.ShapeDtypeStruct((nodes, NODE_ROWS, width), BF16))
    operands = [state[key] for key in in_keys + kept_keys]
    results = run(functools.partial(step_kernel, plan, in_keys, all_outs, kept_keys), operands, outs, aliases, flops)
    state.update(zip(out_keys, results))
    return results[-1] if sends else None


def rows_together(chunks, node):
    return jnp.concatenate([chunk[node] for chunk in chunks], axis=0).astype(BF16)


def apart(value, chunks, node):
    for c, chunk in enumerate(chunks):
        chunk[node] = value[NODE_ROWS * c : NODE_ROWS * (c + 1)]


def base_kernel(rhs_own, rhs_far, own, far, *refs):
    residue, base = refs[: len(refs) // 2], refs[len(refs) // 2 :]
    count = rhs_own.shape[0]
    level, top = lax.axis_index(LEVEL), lax.axis_size(LEVEL) - 1

    @pl.when(level == 0)
    def _():
        for node in range(count):
            apart(dot(rhs_own[node].astype(BF16), own[node]), base, node)
            apart(dot(rhs_far[node].astype(BF16), far[node]), base, count + node)

    @pl.when((level != 0) & (level != top))
    def _():
        for node in range(count):
            apart(dot(rows_together(residue, node), own[node]), base, node)
            apart(dot(rows_together(residue, count + node), far[node]), base, count + node)


def update_kernel(up_own, up_far, *refs):
    chunks = (len(refs) - 2) // 3
    residue, own_kept, far_kept = (refs[chunks * i : chunks * (i + 1)] for i in range(3))
    upd_own, upd_far = refs[-2:]
    level, top = lax.axis_index(LEVEL), lax.axis_size(LEVEL) - 1

    @pl.when(level == top)
    def _():
        count = up_own.shape[0]
        for node in range(count):
            upd_own[node] = dot(rows_together(residue, node), up_own[node])
            upd_far[node] = dot(rows_together(residue, count + node), up_far[node])

    @pl.when(level != top)
    def _():
        for c in range(chunks):
            rows = slice(NODE_ROWS * c, NODE_ROWS * (c + 1))
            upd_own[:, rows, :] = own_kept[c][...]
            upd_far[:, rows, :] = far_kept[c][...]


def ancestor_kernel(section, ancestor, own, far, *refs):
    *bases, here, sem = refs
    count, half, _ = here.shape
    sub = lax.axis_index(SUB)

    @on_level(section)
    def _():
        load = pltpu.make_async_copy(ancestor.at[:, half_rows(ancestor, sub), :], here, sem.at[0])
        load.start()
        load.wait()
        for node in range(count):
            per = far.shape[1] // half
            other = far[2 * count + node // per, half * (node % per) : half * (node % per + 1), :]
            mine = dot(here[node], own[count + node])
            other = dot(other, far[count + node])
            for c, base in enumerate(bases):
                base[node] = mine[NODE_ROWS * c : NODE_ROWS * (c + 1)]
                base[count + node] = other[NODE_ROWS * c : NODE_ROWS * (c + 1)]


def put(here, other, first, out, sems):
    sub = lax.axis_index(SUB)
    half = out.shape[1] // 2
    copies = []
    for i, (mine, theirs, row) in enumerate(zip(here, other, first)):
        size = mine.shape[1]
        to_mine = pl.ds(pl.multiple_of(half * sub + row, NODE_ROWS), size)
        to_theirs = pl.ds(pl.multiple_of(half * (1 - sub) + row, NODE_ROWS), size)
        copies.append(pltpu.make_async_copy(mine, out.at[:, to_mine, :], sems.at[0, i]))
        copies.append(pltpu.make_async_copy(theirs, out.at[:, to_theirs, :], sems.at[1, i]))
    for copy in copies:
        copy.start()
    for copy in copies:
        copy.wait()


def place_kernel(first, *refs):
    count = len(first)
    put(refs[:count], refs[count : 2 * count], first, *refs[-2:])


def place_bottom_kernel(here, far, other, *refs):
    @on_level(0)
    def _():
        put([here], [far], [0], *refs[-2:])

    @off_level(0)
    def _():
        put([here], [other], [0], *refs[-2:])


def run(kernel, operands, outs, aliases=None, flops=10**9, whole=None, scratch=(), raw=()):
    in_specs = [IN_HBM] * len(raw) + [IN_VMEM] * len(operands)
    operands = [*(pltpu.with_memory_space_constraint(value, pltpu.HBM) for value in raw), *(pltpu.with_memory_space_constraint(value, pltpu.VMEM) for value in operands)]
    out_specs = [IN_VMEM] * len(outs)
    out_shape = [pltpu.VMEM(out.shape, out.dtype) for out in outs]
    aliases = dict(aliases or {})
    if whole is not None:
        shape, before = whole
        if before is not None:
            aliases[len(operands)] = len(outs)
            operands.append(before)
            in_specs.append(IN_ANY)
        out_shape.append(shape)
        out_specs.append(IN_ANY)
    return pl.pallas_call(
        kernel,
        in_specs=in_specs,
        out_specs=out_specs,
        out_shape=out_shape,
        input_output_aliases=aliases,
        scratch_shapes=scratch,
        compiler_params=pltpu.CompilerParams(vmem_limit_bytes=SMALL_VMEM_BYTES),
        cost_estimate=pl.CostEstimate(
            flops=flops, bytes_accessed=10**6, transcendentals=0
        ),
    )(*operands)


def exchanged(value):
    return lax.ppermute(value, SUB, [(0, 1), (1, 0)])


def pair_body(rhs, lower_inv, lower_off, upper_inv, upper_off, ancestor, parent):
    levels = lax.axis_size(LEVEL)
    top = levels - 1
    rhs, lower_inv, lower_off, upper_inv, upper_off = (
        value[0] for value in (rhs, lower_inv, lower_off, upper_inv, upper_off)
    )
    count, all_rows, width = rhs.shape
    half = all_rows // 2
    chunks = half // NODE_ROWS
    nodes = 2 * count
    size = nodes * NODE_ROWS

    def shape(of, dtype):
        return jax.ShapeDtypeStruct((of, NODE_ROWS, width), dtype)

    def passed(value, pairs):
        sources = [i for i in range(levels) if i not in dict(pairs)]
        targets = [i for i in range(levels) if i not in [to for _, to in pairs]]
        fill = min(
            (list(zip(sources, order)) for order in itertools.permutations(targets)),
            key=lambda extra: (sum(a == b for a, b in extra), sum(abs(a - b) for a, b in extra)),
        )
        return lax.ppermute(value, LEVEL, pairs + fill)

    def after(value, *earlier):
        return lax.optimization_barrier((value, *earlier))[0]

    matrices = jax.ShapeDtypeStruct(lower_inv.shape, BF16)
    table = jax.ShapeDtypeStruct((size, size), BF16)
    half_shape = jax.ShapeDtypeStruct((count, half, width), F32)
    block = pltpu.VMEM(lower_inv.shape, BF16)
    state = {"nodes": nodes}
    select, choose, rhs_own, rhs_sent, home, swap, up_own, *updates = run(
        start_kernel, (),
        [table, table, half_shape, half_shape, shape(chunks * nodes, F32), shape(chunks * nodes, BF16), matrices]
        + [shape(count, F32)] * (2 * chunks),
        raw=(parent, rhs, lower_inv, lower_off),
        scratch=[pltpu.VMEM(parent.shape, parent.dtype), block, block, pltpu.SemaphoreType.DMA((3, max(count // LOAD_NODES, 3)))],
    )
    state.update(select=select, choose=choose, rhs_own=rhs_own, home=home, up_own=up_own, swapped=exchanged(swap))
    for c in range(chunks):
        state["own", c], state["far", c] = updates[c], updates[chunks + c]

    packed_shape = (2 * count + count * half // width, width, width)
    merge_scratch = [block, block, block, pltpu.VMEM((count, half, width), BF16), pltpu.SemaphoreType.DMA((4, count // LOAD_NODES))]

    def merged(sent):
        low, *others = lax.optimization_barrier((lower_inv, upper_inv, upper_off, ancestor, sent))
        return run(
            merge_kernel, (), [jax.ShapeDtypeStruct(packed_shape, BF16)],
            raw=(low, *others[:3]), scratch=merge_scratch,
        )[0]

    whole = jax.ShapeDtypeStruct(rhs.shape, F32)

    def sems(pieces):
        return [pltpu.SemaphoreType.DMA((2, pieces))]

    pipes = [list(range(chunks))[i : i + 2] for i in range(0, chunks, 2)]
    received = [None] * len(pipes)
    pace = []
    last = 2 * top + 1
    for k in range(last + 1):
        for p, pipe in enumerate(pipes):
            plan, pairs = [], []
            for j, c in enumerate(pipe):
                tier = k - j
                if 0 <= tier < top:
                    plan.append((tier, "sum" if tier == 0 else "tier", c))
                    pairs.append((tier, tier + 1))
                elif tier == top:
                    plan.append((top, "top", c))
                    pairs.append((top, top - 1))
                elif top < tier <= 2 * top:
                    low = 2 * top - tier
                    plan.append((low, "back", c))
                    if low:
                        pairs.append((low, low - 1))
            if received[p] is not None:
                state["received"] = after(received[p], *pace)
            sent = step(plan, state, bool(pairs), COSTS[k])
            pace = [sent] if pairs else [state["sol_own", pipe[1]]]
            if pairs:
                received[p] = passed(sent, pairs)
            if p == 0 and k == 0:
                state["up_far"] = exchanged(after(up_own, sent))
                state["rhs_far"] = exchanged(after(rhs_sent, sent))
            if p == 0 and k == 1:
                state["down_far"] = exchanged(state["down_own"])
            if p == 0 and k == last:
                (update,) = run(
                    place_bottom_kernel, (upd_own, after(upd_far, *pace), upd_other), [], whole=(whole, None), scratch=sems(1)
                )
                pace = [update]
        if k == 0:
            state["down_own"] = merged(sent)
            pace.append(state["down_own"])
        if k == top - 1:
            bases = run(
                functools.partial(ancestor_kernel, top),
                (state["down_own"], state["down_far"]),
                [shape(nodes, F32)] * chunks,
                raw=(after(ancestor, sent),),
                scratch=[pltpu.VMEM((count, half, width), BF16), pltpu.SemaphoreType.DMA((1,))],
            )
            state.update({("top_base", c): bases[c] for c in range(chunks)})
            pace += bases
        residues = [state["residue", c] for c in range(chunks)] if k >= top else []
        if k == top:
            bases = run(
                base_kernel,
                (after(rhs_own, sent), state["rhs_far"], state["down_own"], state["down_far"], *residues),
                [shape(nodes, F32)] * chunks,
            )
            state.update({("low_base", c): bases[c] for c in range(chunks)})
            pace += bases
        if k == top + 2:
            upd_own, upd_far = run(
                update_kernel,
                (up_own, state["up_far"], *residues, *(state["own", c] for c in range(chunks)), *(state["far", c] for c in range(chunks))),
                [half_shape] * 2,
            )
            upd_other = exchanged(upd_far)
        if k == last:
            (solved,) = run(
                functools.partial(place_kernel, [NODE_ROWS * c for c in range(chunks)]),
                [state["sol_own", c] for c in range(chunks)] + [exchanged(state["sol_far", c]) for c in range(chunks)],
                [], whole=(whole, None), scratch=sems(chunks),
            )
    return solved[None], update[None]


def solution(mesh):
    placed = (
        P(LEVEL, SUB, "rhs", None),
        P(LEVEL, SUB, None, None),
        P(LEVEL, SUB, None, None),
        P(LEVEL, SUB, None, None),
        P(LEVEL, SUB, None, None),
        P(SUB, "rhs", None),
        P(),
    )
    return jax.shard_map(
        pair_body if mesh.shape[SUB] == 2 else general_body,
        mesh=mesh,
        in_specs=placed,
        out_specs=(P(LEVEL, SUB, "rhs", None), P(LEVEL, SUB, "rhs", None)),
        check_vma=False,
    )
```

```python
import functools
import itertools

import jax
import jax.numpy as jnp
from jax import lax
from jax.experimental import pallas as pl
from jax.experimental.pallas import tpu as pltpu
from jax.sharding import PartitionSpec as P

CHUNKS = 2
LOCAL_SWAP = False
VMEM_BYTES = 24 * 2**20

LEVEL, SUB = "level", "sub"
BF16 = jnp.bfloat16
F32 = jnp.float32
IN_VMEM = pl.BlockSpec(memory_space=pltpu.VMEM)
IN_SMEM = pl.BlockSpec(memory_space=pltpu.SMEM)


def dot(left, right):
    return jnp.dot(left, right, preferred_element_type=F32)


def forward_kernel(section, start, rows, info, rhs, incoming, inv, off, kept_f, kept_u, fwd, upd, home, far, total):
    count = inv.shape[0]

    @pl.when(info[count] != section)
    def _():
        fwd[...] = kept_f[...]
        upd[...] = kept_u[...]

    @pl.when(info[count] == section)
    def _():
        total[...] = jnp.zeros_like(total)
        for node in range(count):
            right_side = rhs[node, pl.ds(start, rows), :]
            if incoming is not None:
                right_side = right_side - incoming[node].astype(F32)
            forward = dot(right_side.astype(BF16), inv[node]).astype(BF16)
            fwd[node] = forward
            update = dot(forward, off[node])
            upd[node] = update
            total[info[node]] += update
        home[...] = total[:count]
        far[...] = total[count:].astype(BF16)


def first_kernel(section, start, rows, info, rhs, inv, off, kept_f, kept_u, fwd, upd, home, far, total):
    forward_kernel(section, start, rows, info, rhs, None, inv, off, kept_f, kept_u, fwd, upd, home, far, total)


def top_kernel(section, start, rows, info, rhs, incoming, inv, up_off, up_inv, ancestor, kept_f, kept_s, fwd, sol, sol_bf):
    count = inv.shape[0]

    @pl.when(info[count] != section)
    def _():
        fwd[...] = kept_f[...]
        sol[...] = kept_s[...]

    @pl.when(info[count] == section)
    def _():
        for node in range(count):
            right_side = rhs[node, pl.ds(start, rows), :] - incoming[node].astype(F32)
            forward = dot(right_side.astype(BF16), inv[node]).astype(BF16)
            fwd[node] = forward
            above = dot(ancestor[node, pl.ds(start, rows), :], up_off[node])
            reduced = (forward.astype(F32) - above).astype(BF16)
            solved = dot(reduced, up_inv[node])
            sol[node] = solved
            sol_bf[node] = solved.astype(BF16)


def top_update_kernel(section, start, rows, info, fwd, off, kept_u, upd):
    count = off.shape[0]

    @pl.when(info[count] != section)
    def _():
        upd[...] = kept_u[...]

    @pl.when(info[count] == section)
    def _():
        for node in range(count):
            upd[node] = dot(fwd[node], off[node])


def backward_kernel(section, start, rows, info, fwd, own, partner, up_off, up_inv, kept_s, sol, sol_bf):
    count = up_inv.shape[0]

    @pl.when(info[count] != section)
    def _():
        sol[...] = kept_s[...]

    @pl.when(info[count] == section)
    def _():
        for node in range(count):
            place = info[node]
            at_home = place < count
            slot = jnp.where(at_home, place, place - count)
            above = jnp.where(at_home, own[slot], partner[slot])
            reduced = (fwd[node].astype(F32) - dot(above, up_off[node])).astype(BF16)
            solved = dot(reduced, up_inv[node])
            sol[node] = solved
            sol_bf[node] = solved.astype(BF16)


def call(kernel, section, start, rows, operands, outs, aliases, scratch=(), products=2):
    count = operands[1].shape[0]
    return pl.pallas_call(
        functools.partial(kernel, section, start, rows),
        in_specs=[IN_SMEM] + [IN_VMEM] * (len(operands) - 1),
        out_specs=[IN_VMEM] * len(outs),
        out_shape=outs,
        scratch_shapes=scratch,
        input_output_aliases=aliases,
        compiler_params=pltpu.CompilerParams(vmem_limit_bytes=VMEM_BYTES),
        cost_estimate=pl.CostEstimate(
            flops=products * 2 * count * rows * 256 * 256, bytes_accessed=count * 256 * 256 * 2 * products, transcendentals=0
        ),
    )(*operands)


def swapped(value, section, apart):
    mask = 2**apart
    subs = lax.axis_size(SUB)
    if not LOCAL_SWAP:
        return lax.ppermute(value, SUB, [(i, i ^ mask) for i in range(subs)])
    pairs = [(section * subs + i, section * subs + (i ^ mask)) for i in range(subs)]
    return lax.ppermute(value, (LEVEL, SUB), pairs)


def general_body(rhs, lower_inv, lower_off, upper_inv, upper_off, ancestor, parent):
    levels = lax.axis_size(LEVEL)
    sub_count = lax.axis_size(SUB)
    sub_bits = sub_count.bit_length() - 1
    tier = lax.axis_index(LEVEL)
    sub = lax.axis_index(SUB)
    rhs, lower_inv, lower_off, upper_inv, upper_off = (
        value[0] for value in (rhs, lower_inv, lower_off, upper_inv, upper_off)
    )
    count, all_rows, width = rhs.shape
    rows = all_rows // CHUNKS
    parent_row = lax.dynamic_index_in_dim(parent, jnp.minimum(tier, levels - 2), 0, keepdims=False)
    parent_here = lax.dynamic_slice_in_dim(parent_row, sub * count, count)
    place = parent_here % count + jnp.where(parent_here // count == sub, 0, count)
    info = jnp.concatenate([place, tier[None]]).astype(jnp.int32)

    def shape(dtype):
        return jax.ShapeDtypeStruct((count, rows, width), dtype)

    fwd = [jnp.zeros((count, rows, width), BF16) for _ in range(CHUNKS)]
    upd = [jnp.zeros((count, rows, width), F32) for _ in range(CHUNKS)]
    sol = [jnp.zeros((count, rows, width), F32) for _ in range(CHUNKS)]
    incoming = [None] * CHUNKS
    above = [None] * CHUNKS
    top = levels - 1
    for section in range(top):
        for c in range(CHUNKS):
            if section == 0:
                kernel, operands = first_kernel, (info, rhs, lower_inv, lower_off, fwd[c], upd[c])
            else:
                kernel, operands = forward_kernel, (info, rhs, incoming[c], lower_inv, lower_off, fwd[c], upd[c])
            at = len(operands) - 2
            fwd[c], upd[c], home, far = call(
                kernel, section, c * rows, rows, operands,
                [shape(BF16), shape(F32), shape(F32), shape(BF16)], {at: 0, at + 1: 1},
                [pltpu.VMEM((2 * count, rows, width), F32)],
            )
            received = swapped(far, section, section % sub_bits)
            summed = (home + received.astype(F32)).astype(BF16)
            incoming[c] = lax.ppermute(summed, LEVEL, [(section, section + 1)])
    for c in range(CHUNKS):
        fwd[c], sol[c], solved = call(
            top_kernel, top, c * rows, rows,
            (info, rhs, incoming[c], lower_inv, upper_off, upper_inv, ancestor, fwd[c], sol[c]),
            [shape(BF16), shape(F32), shape(BF16)], {7: 0, 8: 1}, products=3,
        )
        above[c] = lax.ppermute(solved, LEVEL, [(top, top - 1)])
    for c in range(CHUNKS):
        (upd[c],) = call(top_update_kernel, top, c * rows, rows, (info, fwd[c], lower_off, upd[c]), [shape(F32)], {3: 0}, products=1)
    for section in reversed(range(top)):
        for c in range(CHUNKS):
            partner = swapped(above[c], section, section % sub_bits)
            sol[c], solved = call(
                backward_kernel, section, c * rows, rows,
                (info, fwd[c], above[c], partner, upper_off, upper_inv, sol[c]),
                [shape(F32), shape(BF16)], {6: 0},
            )
            if section:
                above[c] = lax.ppermute(solved, LEVEL, [(section, section - 1)])
    return jnp.concatenate(sol, axis=1)[None], jnp.concatenate(upd, axis=1)[None]


NODE_ROWS = 8
LOAD_NODES = 4
COSTS = [10000000000, 30000000000, 30000000000, 5000000000, 5000000000, 5000000000, 5000000000, 5000000000]
SMALL_VMEM_BYTES = 12 * 2**20
IN_ANY = pl.BlockSpec(memory_space=pl.ANY)
IN_HBM = pl.BlockSpec(memory_space=pltpu.HBM)


def rows_of(start):
    return pl.ds(pl.multiple_of(start, NODE_ROWS), NODE_ROWS)


def half_rows(array, sub):
    half = array.shape[1] // 2
    return pl.ds(pl.multiple_of(half * sub, half), half)


def flat(value):
    return value.reshape(value.shape[0] * value.shape[1], value.shape[2])


def pick(select, values):
    return dot(select, values.astype(BF16))


def on_level(section):
    return pl.when(lax.axis_index(LEVEL) == section)


def off_level(section):
    return pl.when(lax.axis_index(LEVEL) != section)


def keep(section, kept, outs):
    @off_level(section)
    def _():
        for before, after in zip(kept, outs):
            after[...] = before[...]


def fill_tables(parent, select, choose):
    nodes = parent.shape[1]
    size = nodes * NODE_ROWS
    top = lax.axis_size(LEVEL) - 1
    level, shift = lax.axis_index(LEVEL), lax.axis_index(SUB) * (nodes // 2)

    def target(row, axis):
        shape = (nodes, size) if axis else (size, nodes)
        child = lax.broadcasted_iota(jnp.int32, shape, axis) // NODE_ROWS + shift
        child = jnp.where(child >= nodes, child - nodes, child)
        same = child == lax.broadcasted_iota(jnp.int32, shape, 1 - axis)
        row = row - shift
        row = jnp.where(row < 0, row + nodes, row)
        if axis:
            found = dot(row.astype(F32).astype(BF16), same.astype(F32).astype(BF16))
        else:
            found = jnp.sum(jnp.where(same, row.astype(F32), 0.0), axis=1, keepdims=True)
        place = lax.broadcasted_iota(jnp.int32, found.shape, axis)
        return found.astype(jnp.int32) * NODE_ROWS + lax.rem(place, NODE_ROWS)

    up = target(parent[pl.ds(jnp.minimum(level, top - 1), 1), :], 1)
    down = target(parent[pl.ds(jnp.maximum(level - 1, 0), 1), :], 0)
    index = lax.broadcasted_iota(jnp.int32, (size, size), 0)
    select[...] = (index == up).astype(F32).astype(BF16)
    index = lax.broadcasted_iota(jnp.int32, (size, size), 1)
    choose[...] = (index == down).astype(F32).astype(BF16)


def start_kernel(parent, rhs, inv, off, select, choose, rhs_own, rhs_sent, home, swap, merged, *refs):
    *updates, parent_here, inv_here, off_here, sems = refs
    count = inv.shape[0]
    chunks = len(updates) // 2
    size = count * NODE_ROWS
    level, sub = lax.axis_index(LEVEL), lax.axis_index(SUB)
    table = pltpu.make_async_copy(parent, parent_here, sems.at[0, 0])
    mine = pltpu.make_async_copy(rhs.at[:, half_rows(rhs, sub), :], rhs_own, sems.at[0, 1])
    other = pltpu.make_async_copy(rhs.at[:, half_rows(rhs, 1 - sub), :], rhs_sent, sems.at[0, 2])
    table.start()
    loads = []
    for group in range(count // LOAD_NODES):
        here = pl.ds(group * LOAD_NODES, LOAD_NODES)
        loads.append(pltpu.make_async_copy(inv.at[here], inv_here.at[here], sems.at[1, group]))
        loads.append(pltpu.make_async_copy(off.at[here], off_here.at[here], sems.at[2, group]))
        loads[-2].start()
        loads[-1].start()
        if group == 0:
            mine.start()
            other.start()
    table.wait()
    fill_tables(parent_here, select, choose)
    mine.wait()
    other.wait()

    @on_level(0)
    def _():
        for node in range(count):
            if node % LOAD_NODES == 0:
                loads[2 * (node // LOAD_NODES)].wait()
                loads[2 * (node // LOAD_NODES) + 1].wait()
            right_side = jnp.concatenate([rhs_own[node], rhs_sent[node]], axis=0).astype(BF16)
            forward = dot(right_side, inv_here[node]).astype(BF16)
            update = dot(forward, off_here[node])
            for c in range(2 * chunks):
                updates[c][node] = update[NODE_ROWS * c : NODE_ROWS * (c + 1)]
        chosen = select[:, :size]
        for c in range(chunks):
            home[2 * count * c : 2 * count * (c + 1)] = pick(chosen, flat(updates[c][...])).reshape(2 * count, *home.shape[1:])
            sums = pick(chosen, flat(updates[chunks + c][...])).reshape(2 * count, *home.shape[1:]).astype(BF16)
            swap[2 * count * c : 2 * count * c + count] = sums[count:]
            swap[2 * count * c + count : 2 * count * (c + 1)] = sums[:count]

    @off_level(0)
    def _():
        for node in range(count):
            if node % LOAD_NODES == 0:
                loads[2 * (node // LOAD_NODES)].wait()
                loads[2 * (node // LOAD_NODES) + 1].wait()
            merged[node] = dot(inv_here[node], off_here[node]).astype(BF16)


def merge_kernel(low_inv, up_inv, up_off, ancestor, packed, *scratch):
    low_here, up_here, off_here, rows, sems = scratch
    count = low_inv.shape[0]
    sub = lax.axis_index(SUB)
    loads = []
    for group in range(count // LOAD_NODES):
        here = pl.ds(group * LOAD_NODES, LOAD_NODES)
        loads.append(pltpu.make_async_copy(up_inv.at[here], up_here.at[here], sems.at[1, group]))
        loads.append(pltpu.make_async_copy(low_inv.at[here], low_here.at[here], sems.at[0, group]))
        loads.append(pltpu.make_async_copy(up_off.at[here], off_here.at[here], sems.at[2, group]))
    loads.append(pltpu.make_async_copy(ancestor.at[:, half_rows(ancestor, 1 - sub), :], rows, sems.at[3, 0]))
    for load in loads:
        load.start()
    for node in range(count):
        if node % LOAD_NODES == 0:
            for load in loads[3 * (node // LOAD_NODES) : 3 * (node // LOAD_NODES) + 3]:
                load.wait()
        packed[node] = dot(low_here[node], up_here[node]).astype(BF16)
        packed[count + node] = dot(off_here[node], up_here[node]).astype(BF16)
    loads[-1].wait()
    packed[2 * count :] = rows[...].reshape(packed.shape[0] - 2 * count, *packed.shape[1:])


def residue_of(c, rhs_own, rhs_far, incoming, node):
    count = rhs_own.shape[0]
    rows = slice(NODE_ROWS * c, NODE_ROWS * (c + 1))
    right_side = rhs_own[node, rows, :] if node < count else rhs_far[node - count, rows, :]
    return (right_side - incoming[node].astype(F32)).astype(BF16)


def tier_role(c, at):
    count = at["rhs_own"].shape[0]
    own, far = at["own", c], at["far", c]
    for node in range(2 * count):
        value = residue_of(c, at["rhs_own"], at["rhs_far"], at["received"], node)
        at["residue", c][node] = value.astype(F32)
        if node < count:
            own[node] = dot(value, at["up_own"][node])
        else:
            far[node - count] = dot(value, at["up_far"][node - count])
    updates = jnp.concatenate([flat(own[...]), flat(far[...])], axis=0)
    at["sent"][...] = pick(at["select"][...], updates).reshape(at["sent"].shape).astype(BF16)


def send_solved(c, at):
    if "sent" in at:
        solved = jnp.concatenate([flat(at["sol_own", c][...]), flat(at["sol_far", c][...])], axis=0).astype(BF16)
        at["sent"][...] = dot(at["choose"][...], solved).reshape(at["sent"].shape).astype(BF16)


def top_role(c, at):
    count = at["rhs_own"].shape[0]
    base = at["top_base", c]
    for node in range(2 * count):
        value = residue_of(c, at["rhs_own"], at["rhs_far"], at["received"], node)
        at["residue", c][node] = value.astype(F32)
        if node < count:
            at["sol_own", c][node] = dot(value, at["down_own"][node]) - base[node]
        else:
            at["sol_far", c][node - count] = dot(value, at["down_far"][node - count]) - base[node]
    send_solved(c, at)


def back_role(c, at):
    count = at["sol_own", c].shape[0]
    base, above = at["low_base", c], at["received"]
    for node in range(count):
        at["sol_own", c][node] = base[node] - dot(above[node], at["down_own"][count + node])
        at["sol_far", c][node] = base[count + node] - dot(above[count + node], at["down_far"][count + node])
    send_solved(c, at)


def back_far_role(c, at):
    base = at["low_base", c]
    count = base.shape[0] // 2
    for node in range(count):
        above = at["received"][count + node]
        at["sol_far", c][node] = base[count + node] - dot(above, at["down_far"][count + node])


def back_own_role(c, at):
    base = at["low_base", c]
    count = base.shape[0] // 2
    for node in range(count):
        at["sol_own", c][node] = base[node] - dot(at["received"][node], at["down_own"][count + node])


def sum_role(c, at):
    rows = slice(c * at["sent"].shape[0], (c + 1) * at["sent"].shape[0])
    at["sent"][...] = (at["home"][rows] + at["swapped"][rows].astype(F32)).astype(BF16)


FAR, OWN = "f", "o"
ROLES = {"tier": tier_role, "top": top_role, "back": back_role, FAR: back_far_role, OWN: back_own_role, "sum": sum_role}
READS = {
    "tier": ("rhs_own", "rhs_far", "received", "up_own", "up_far", "select"),
    "top": ("rhs_own", "rhs_far", "received", "down_own", "down_far", "choose", "top_base"),
    "back": ("received", "down_own", "down_far", "choose", "low_base"),
    FAR: ("received", "down_far", "low_base"),
    OWN: ("received", "down_own", "low_base"),
    "sum": ("home", "swapped"),
}
WRITES = {
    "tier": ("residue", "own", "far"),
    "top": ("residue", "sol_own", "sol_far"),
    "back": ("sol_own", "sol_far"),
    FAR: ("sol_far",),
    OWN: ("sol_own",),
    "sum": (),
}


def step_kernel(plan, in_keys, out_keys, kept_keys, *refs):
    reads = dict(zip(in_keys, refs))
    kept = dict(zip(kept_keys, refs[len(in_keys) :]))
    outs = dict(zip(out_keys, refs[len(in_keys) + len(kept_keys) :]))
    for level, role, c in plan:
        writes = [(name, c) for name in WRITES[role]]
        keep(level, [kept[key] for key in writes if key in kept], [outs[key] for key in writes if key in kept])
        pl.when(lax.axis_index(LEVEL) == level)(functools.partial(ROLES[role], c, {**reads, **outs}))


def step(plan, state, sends=True, flops=10**9):
    nodes = state["nodes"]
    in_keys, out_keys = [], []
    for _, role, c in plan:
        for name in READS[role]:
            key = (name, c) if name.endswith("_base") else name
            if key not in in_keys:
                in_keys.append(key)
        out_keys += [(name, c) for name in WRITES[role]]
    kept_keys = [key for key in out_keys if key in state]
    width = state["rhs_own"].shape[2]
    outs = []
    for name, _ in out_keys:
        of = nodes if name == "residue" else nodes // 2
        outs.append(jax.ShapeDtypeStruct((of, NODE_ROWS, width), F32))
    aliases = {len(in_keys) + i: out_keys.index(key) for i, key in enumerate(kept_keys)}
    all_outs = out_keys + (["sent"] if sends else [])
    if sends:
        outs.append(jax.ShapeDtypeStruct((nodes, NODE_ROWS, width), BF16))
    operands = [state[key] for key in in_keys + kept_keys]
    results = run(functools.partial(step_kernel, plan, in_keys, all_outs, kept_keys), operands, outs, aliases, flops)
    state.update(zip(out_keys, results))
    return results[-1] if sends else None


def rows_together(chunks, node):
    return jnp.concatenate([chunk[node] for chunk in chunks], axis=0).astype(BF16)


def apart(value, chunks, node):
    for c, chunk in enumerate(chunks):
        chunk[node] = value[NODE_ROWS * c : NODE_ROWS * (c + 1)]


def base_kernel(rhs_own, rhs_far, own, far, *refs):
    residue, base = refs[: len(refs) // 2], refs[len(refs) // 2 :]
    count = rhs_own.shape[0]
    level, top = lax.axis_index(LEVEL), lax.axis_size(LEVEL) - 1

    @pl.when(level == 0)
    def _():
        for node in range(count):
            apart(dot(rhs_own[node].astype(BF16), own[node]), base, node)
            apart(dot(rhs_far[node].astype(BF16), far[node]), base, count + node)

    @pl.when((level != 0) & (level != top))
    def _():
        for node in range(count):
            apart(dot(rows_together(residue, node), own[node]), base, node)
            apart(dot(rows_together(residue, count + node), far[node]), base, count + node)


def update_kernel(up_own, up_far, *refs):
    chunks = (len(refs) - 2) // 3
    residue, own_kept, far_kept = (refs[chunks * i : chunks * (i + 1)] for i in range(3))
    upd_own, upd_far = refs[-2:]
    level, top = lax.axis_index(LEVEL), lax.axis_size(LEVEL) - 1

    @pl.when(level == top)
    def _():
        count = up_own.shape[0]
        for node in range(count):
            upd_own[node] = dot(rows_together(residue, node), up_own[node])
            upd_far[node] = dot(rows_together(residue, count + node), up_far[node])

    @pl.when(level != top)
    def _():
        for c in range(chunks):
            rows = slice(NODE_ROWS * c, NODE_ROWS * (c + 1))
            upd_own[:, rows, :] = own_kept[c][...]
            upd_far[:, rows, :] = far_kept[c][...]


def ancestor_kernel(section, ancestor, own, far, *refs):
    *bases, here, sem = refs
    count, half, _ = here.shape
    sub = lax.axis_index(SUB)

    @on_level(section)
    def _():
        load = pltpu.make_async_copy(ancestor.at[:, half_rows(ancestor, sub), :], here, sem.at[0])
        load.start()
        load.wait()
        for node in range(count):
            per = far.shape[1] // half
            other = far[2 * count + node // per, half * (node % per) : half * (node % per + 1), :]
            mine = dot(here[node], own[count + node])
            other = dot(other, far[count + node])
            for c, base in enumerate(bases):
                base[node] = mine[NODE_ROWS * c : NODE_ROWS * (c + 1)]
                base[count + node] = other[NODE_ROWS * c : NODE_ROWS * (c + 1)]


def put(here, other, first, out, sems):
    sub = lax.axis_index(SUB)
    half = out.shape[1] // 2
    copies = []
    for i, (mine, theirs, row) in enumerate(zip(here, other, first)):
        size = mine.shape[1]
        to_mine = pl.ds(pl.multiple_of(half * sub + row, NODE_ROWS), size)
        to_theirs = pl.ds(pl.multiple_of(half * (1 - sub) + row, NODE_ROWS), size)
        copies.append(pltpu.make_async_copy(mine, out.at[:, to_mine, :], sems.at[0, i]))
        copies.append(pltpu.make_async_copy(theirs, out.at[:, to_theirs, :], sems.at[1, i]))
    for copy in copies:
        copy.start()
    for copy in copies:
        copy.wait()


def place_kernel(first, *refs):
    count = len(first)
    put(refs[:count], refs[count : 2 * count], first, *refs[-2:])


def place_bottom_kernel(here, far, other, *refs):
    @on_level(0)
    def _():
        put([here], [far], [0], *refs[-2:])

    @off_level(0)
    def _():
        put([here], [other], [0], *refs[-2:])


def run(kernel, operands, outs, aliases=None, flops=10**9, whole=None, scratch=(), raw=()):
    in_specs = [IN_HBM] * len(raw) + [IN_VMEM] * len(operands)
    operands = [*(pltpu.with_memory_space_constraint(value, pltpu.HBM) for value in raw), *(pltpu.with_memory_space_constraint(value, pltpu.VMEM) for value in operands)]
    out_specs = [IN_VMEM] * len(outs)
    out_shape = [pltpu.VMEM(out.shape, out.dtype) for out in outs]
    aliases = dict(aliases or {})
    if whole is not None:
        shape, before = whole
        if before is not None:
            aliases[len(operands)] = len(outs)
            operands.append(before)
            in_specs.append(IN_ANY)
        out_shape.append(shape)
        out_specs.append(IN_ANY)
    return pl.pallas_call(
        kernel,
        in_specs=in_specs,
        out_specs=out_specs,
        out_shape=out_shape,
        input_output_aliases=aliases,
        scratch_shapes=scratch,
        compiler_params=pltpu.CompilerParams(vmem_limit_bytes=SMALL_VMEM_BYTES),
        cost_estimate=pl.CostEstimate(
            flops=flops, bytes_accessed=10**6, transcendentals=0
        ),
    )(*operands)


def exchanged(value):
    return lax.ppermute(value, SUB, [(0, 1), (1, 0)])


def pair_body(rhs, lower_inv, lower_off, upper_inv, upper_off, ancestor, parent):
    levels = lax.axis_size(LEVEL)
    top = levels - 1
    rhs, lower_inv, lower_off, upper_inv, upper_off = (
        value[0] for value in (rhs, lower_inv, lower_off, upper_inv, upper_off)
    )
    count, all_rows, width = rhs.shape
    half = all_rows // 2
    chunks = half // NODE_ROWS
    nodes = 2 * count
    size = nodes * NODE_ROWS

    def shape(of, dtype):
        return jax.ShapeDtypeStruct((of, NODE_ROWS, width), dtype)

    def passed(value, pairs):
        sources = [i for i in range(levels) if i not in dict(pairs)]
        targets = [i for i in range(levels) if i not in [to for _, to in pairs]]
        fill = min(
            (list(zip(sources, order)) for order in itertools.permutations(targets)),
            key=lambda extra: (sum(a == b for a, b in extra), sum(abs(a - b) for a, b in extra)),
        )
        return lax.ppermute(value, LEVEL, pairs + fill)

    def after(value, *earlier):
        return lax.optimization_barrier((value, *earlier))[0]

    matrices = jax.ShapeDtypeStruct(lower_inv.shape, BF16)
    table = jax.ShapeDtypeStruct((size, size), BF16)
    half_shape = jax.ShapeDtypeStruct((count, half, width), F32)
    block = pltpu.VMEM(lower_inv.shape, BF16)
    state = {"nodes": nodes}
    select, choose, rhs_own, rhs_sent, home, swap, up_own, *updates = run(
        start_kernel, (),
        [table, table, half_shape, half_shape, shape(chunks * nodes, F32), shape(chunks * nodes, BF16), matrices]
        + [shape(count, F32)] * (2 * chunks),
        raw=(parent, rhs, lower_inv, lower_off),
        scratch=[pltpu.VMEM(parent.shape, parent.dtype), block, block, pltpu.SemaphoreType.DMA((3, max(count // LOAD_NODES, 3)))],
    )
    state.update(select=select, choose=choose, rhs_own=rhs_own, home=home, up_own=up_own, swapped=exchanged(swap))
    for c in range(chunks):
        state["own", c], state["far", c] = updates[c], updates[chunks + c]

    packed_shape = (2 * count + count * half // width, width, width)
    merge_scratch = [block, block, block, pltpu.VMEM((count, half, width), BF16), pltpu.SemaphoreType.DMA((4, count // LOAD_NODES))]

    def merged(sent):
        low, *others = lax.optimization_barrier((lower_inv, upper_inv, upper_off, ancestor, sent))
        return run(
            merge_kernel, (), [jax.ShapeDtypeStruct(packed_shape, BF16)],
            raw=(low, *others[:3]), scratch=merge_scratch,
        )[0]

    whole = jax.ShapeDtypeStruct(rhs.shape, F32)

    def sems(pieces):
        return [pltpu.SemaphoreType.DMA((2, pieces))]

    def placed(group, before, *earlier):
        first = after(state["sol_own", group[0]], *earlier) if earlier else state["sol_own", group[0]]
        return run(
            functools.partial(place_kernel, [NODE_ROWS * c for c in group]),
            [first, *(state["sol_own", c] for c in group[1:]), *(other[c] for c in group)],
            [], whole=(whole, before), scratch=sems(len(group)),
        )[0]

    pipes = [list(range(chunks))[i : i + 2] for i in range(0, chunks, 2)]
    received = [None] * len(pipes)
    other = [None] * chunks
    pace = []
    last = 2 * top + 1
    for k in range(last + 1):
        for p, pipe in enumerate(pipes):
            plan, pairs = [], []
            for j, c in enumerate(pipe):
                tier = k - j
                if 0 <= tier < top:
                    plan.append((tier, "sum" if tier == 0 else "tier", c))
                    pairs.append((tier, tier + 1))
                elif tier == top:
                    plan.append((top, "top", c))
                    pairs.append((top, top - 1))
                elif top < tier <= 2 * top:
                    low = 2 * top - tier
                    plan.append((low, "back", c))
                    if low:
                        pairs.append((low, low - 1))
            if received[p] is not None:
                state["received"] = after(received[p], *pace)
            if k == last:
                step([(0, FAR, pipe[-1])], state, False, COSTS[k])
                other[pipe[-1]] = exchanged(state["sol_far", pipe[-1]])
                plan = [(0, OWN, pipe[-1])]
                state["received"] = after(state["received"], state["sol_far", pipe[-1]])
            sent = step(plan, state, bool(pairs), COSTS[k])
            pace = [sent] if pairs else [state["sol_own", pipe[-1]]]
            if pairs:
                received[p] = passed(sent, pairs)
            if p == 0 and k == 0:
                state["up_far"] = exchanged(after(up_own, sent))
                state["rhs_far"] = exchanged(after(rhs_sent, sent))
            if p == 0 and k == 1:
                state["down_far"] = exchanged(state["down_own"])
            if p == 0 and k == last:
                (update,) = run(
                    place_bottom_kernel, (upd_own, after(upd_far, *pace), upd_other), [], whole=(whole, None), scratch=sems(1)
                )
                early = [pipe[0] for pipe in pipes]
                other[early[0]], other[early[1]] = (exchanged(state["sol_far", c]) for c in early)
                solved = placed(early, None, update)
                pace = [solved]
        if k == 0:
            state["down_own"] = merged(sent)
            pace.append(state["down_own"])
        if k == top - 1:
            bases = run(
                functools.partial(ancestor_kernel, top),
                (state["down_own"], state["down_far"]),
                [shape(nodes, F32)] * chunks,
                raw=(after(ancestor, sent),),
                scratch=[pltpu.VMEM((count, half, width), BF16), pltpu.SemaphoreType.DMA((1,))],
            )
            state.update({("top_base", c): bases[c] for c in range(chunks)})
            pace += bases
        residues = [state["residue", c] for c in range(chunks)] if k >= top else []
        if k == top:
            bases = run(
                base_kernel,
                (after(rhs_own, sent), state["rhs_far"], state["down_own"], state["down_far"], *residues),
                [shape(nodes, F32)] * chunks,
            )
            state.update({("low_base", c): bases[c] for c in range(chunks)})
            pace += bases
        if k == top + 2:
            upd_own, upd_far = run(
                update_kernel,
                (up_own, state["up_far"], *residues, *(state["own", c] for c in range(chunks)), *(state["far", c] for c in range(chunks))),
                [half_shape] * 2,
            )
            upd_other = exchanged(upd_far)
    solved = placed([pipe[-1] for pipe in pipes], solved)
    return solved[None], update[None]


def solution(mesh):
    placed = (
        P(LEVEL, SUB, "rhs", None),
        P(LEVEL, SUB, None, None),
        P(LEVEL, SUB, None, None),
        P(LEVEL, SUB, None, None),
        P(LEVEL, SUB, None, None),
        P(SUB, "rhs", None),
        P(),
    )
    return jax.shard_map(
        pair_body if mesh.shape[SUB] == 2 else general_body,
        mesh=mesh,
        in_specs=placed,
        out_specs=(P(LEVEL, SUB, "rhs", None), P(LEVEL, SUB, "rhs", None)),
        check_vma=False,
    )
```

```python
import functools
import itertools

import jax
import jax.numpy as jnp
from jax import lax
from jax.experimental import pallas as pl
from jax.experimental.pallas import tpu as pltpu
from jax.sharding import PartitionSpec as P

CHUNKS = 2
LOCAL_SWAP = False
VMEM_BYTES = 24 * 2**20

LEVEL, SUB = "level", "sub"
BF16 = jnp.bfloat16
F32 = jnp.float32
IN_VMEM = pl.BlockSpec(memory_space=pltpu.VMEM)
IN_SMEM = pl.BlockSpec(memory_space=pltpu.SMEM)


def dot(left, right):
    return jnp.dot(left, right, preferred_element_type=F32)


def forward_kernel(section, start, rows, info, rhs, incoming, inv, off, kept_f, kept_u, fwd, upd, home, far, total):
    count = inv.shape[0]

    @pl.when(info[count] != section)
    def _():
        fwd[...] = kept_f[...]
        upd[...] = kept_u[...]

    @pl.when(info[count] == section)
    def _():
        total[...] = jnp.zeros_like(total)
        for node in range(count):
            right_side = rhs[node, pl.ds(start, rows), :]
            if incoming is not None:
                right_side = right_side - incoming[node].astype(F32)
            forward = dot(right_side.astype(BF16), inv[node]).astype(BF16)
            fwd[node] = forward
            update = dot(forward, off[node])
            upd[node] = update
            total[info[node]] += update
        home[...] = total[:count]
        far[...] = total[count:].astype(BF16)


def first_kernel(section, start, rows, info, rhs, inv, off, kept_f, kept_u, fwd, upd, home, far, total):
    forward_kernel(section, start, rows, info, rhs, None, inv, off, kept_f, kept_u, fwd, upd, home, far, total)


def top_kernel(section, start, rows, info, rhs, incoming, inv, up_off, up_inv, ancestor, kept_f, kept_s, fwd, sol, sol_bf):
    count = inv.shape[0]

    @pl.when(info[count] != section)
    def _():
        fwd[...] = kept_f[...]
        sol[...] = kept_s[...]

    @pl.when(info[count] == section)
    def _():
        for node in range(count):
            right_side = rhs[node, pl.ds(start, rows), :] - incoming[node].astype(F32)
            forward = dot(right_side.astype(BF16), inv[node]).astype(BF16)
            fwd[node] = forward
            above = dot(ancestor[node, pl.ds(start, rows), :], up_off[node])
            reduced = (forward.astype(F32) - above).astype(BF16)
            solved = dot(reduced, up_inv[node])
            sol[node] = solved
            sol_bf[node] = solved.astype(BF16)


def top_update_kernel(section, start, rows, info, fwd, off, kept_u, upd):
    count = off.shape[0]

    @pl.when(info[count] != section)
    def _():
        upd[...] = kept_u[...]

    @pl.when(info[count] == section)
    def _():
        for node in range(count):
            upd[node] = dot(fwd[node], off[node])


def backward_kernel(section, start, rows, info, fwd, own, partner, up_off, up_inv, kept_s, sol, sol_bf):
    count = up_inv.shape[0]

    @pl.when(info[count] != section)
    def _():
        sol[...] = kept_s[...]

    @pl.when(info[count] == section)
    def _():
        for node in range(count):
            place = info[node]
            at_home = place < count
            slot = jnp.where(at_home, place, place - count)
            above = jnp.where(at_home, own[slot], partner[slot])
            reduced = (fwd[node].astype(F32) - dot(above, up_off[node])).astype(BF16)
            solved = dot(reduced, up_inv[node])
            sol[node] = solved
            sol_bf[node] = solved.astype(BF16)


def call(kernel, section, start, rows, operands, outs, aliases, scratch=(), products=2):
    count = operands[1].shape[0]
    return pl.pallas_call(
        functools.partial(kernel, section, start, rows),
        in_specs=[IN_SMEM] + [IN_VMEM] * (len(operands) - 1),
        out_specs=[IN_VMEM] * len(outs),
        out_shape=outs,
        scratch_shapes=scratch,
        input_output_aliases=aliases,
        compiler_params=pltpu.CompilerParams(vmem_limit_bytes=VMEM_BYTES),
        cost_estimate=pl.CostEstimate(
            flops=products * 2 * count * rows * 256 * 256, bytes_accessed=count * 256 * 256 * 2 * products, transcendentals=0
        ),
    )(*operands)


def swapped(value, section, apart):
    mask = 2**apart
    subs = lax.axis_size(SUB)
    if not LOCAL_SWAP:
        return lax.ppermute(value, SUB, [(i, i ^ mask) for i in range(subs)])
    pairs = [(section * subs + i, section * subs + (i ^ mask)) for i in range(subs)]
    return lax.ppermute(value, (LEVEL, SUB), pairs)


def general_body(rhs, lower_inv, lower_off, upper_inv, upper_off, ancestor, parent):
    levels = lax.axis_size(LEVEL)
    sub_count = lax.axis_size(SUB)
    sub_bits = sub_count.bit_length() - 1
    tier = lax.axis_index(LEVEL)
    sub = lax.axis_index(SUB)
    rhs, lower_inv, lower_off, upper_inv, upper_off = (
        value[0] for value in (rhs, lower_inv, lower_off, upper_inv, upper_off)
    )
    count, all_rows, width = rhs.shape
    rows = all_rows // CHUNKS
    parent_row = lax.dynamic_index_in_dim(parent, jnp.minimum(tier, levels - 2), 0, keepdims=False)
    parent_here = lax.dynamic_slice_in_dim(parent_row, sub * count, count)
    place = parent_here % count + jnp.where(parent_here // count == sub, 0, count)
    info = jnp.concatenate([place, tier[None]]).astype(jnp.int32)

    def shape(dtype):
        return jax.ShapeDtypeStruct((count, rows, width), dtype)

    fwd = [jnp.zeros((count, rows, width), BF16) for _ in range(CHUNKS)]
    upd = [jnp.zeros((count, rows, width), F32) for _ in range(CHUNKS)]
    sol = [jnp.zeros((count, rows, width), F32) for _ in range(CHUNKS)]
    incoming = [None] * CHUNKS
    above = [None] * CHUNKS
    top = levels - 1
    for section in range(top):
        for c in range(CHUNKS):
            if section == 0:
                kernel, operands = first_kernel, (info, rhs, lower_inv, lower_off, fwd[c], upd[c])
            else:
                kernel, operands = forward_kernel, (info, rhs, incoming[c], lower_inv, lower_off, fwd[c], upd[c])
            at = len(operands) - 2
            fwd[c], upd[c], home, far = call(
                kernel, section, c * rows, rows, operands,
                [shape(BF16), shape(F32), shape(F32), shape(BF16)], {at: 0, at + 1: 1},
                [pltpu.VMEM((2 * count, rows, width), F32)],
            )
            received = swapped(far, section, section % sub_bits)
            summed = (home + received.astype(F32)).astype(BF16)
            incoming[c] = lax.ppermute(summed, LEVEL, [(section, section + 1)])
    for c in range(CHUNKS):
        fwd[c], sol[c], solved = call(
            top_kernel, top, c * rows, rows,
            (info, rhs, incoming[c], lower_inv, upper_off, upper_inv, ancestor, fwd[c], sol[c]),
            [shape(BF16), shape(F32), shape(BF16)], {7: 0, 8: 1}, products=3,
        )
        above[c] = lax.ppermute(solved, LEVEL, [(top, top - 1)])
    for c in range(CHUNKS):
        (upd[c],) = call(top_update_kernel, top, c * rows, rows, (info, fwd[c], lower_off, upd[c]), [shape(F32)], {3: 0}, products=1)
    for section in reversed(range(top)):
        for c in range(CHUNKS):
            partner = swapped(above[c], section, section % sub_bits)
            sol[c], solved = call(
                backward_kernel, section, c * rows, rows,
                (info, fwd[c], above[c], partner, upper_off, upper_inv, sol[c]),
                [shape(F32), shape(BF16)], {6: 0},
            )
            if section:
                above[c] = lax.ppermute(solved, LEVEL, [(section, section - 1)])
    return jnp.concatenate(sol, axis=1)[None], jnp.concatenate(upd, axis=1)[None]


NODE_ROWS = 8
CROSS, OTHER, BELOW, LAST = "c", "o", "b", "l"
LOAD_NODES = 4
COSTS = [10000000000, 30000000000, 30000000000, 5000000000, 5000000000, 5000000000, 5000000000, 5000000000]
SMALL_VMEM_BYTES = 12 * 2**20
IN_ANY = pl.BlockSpec(memory_space=pl.ANY)
IN_HBM = pl.BlockSpec(memory_space=pltpu.HBM)


def rows_of(start):
    return pl.ds(pl.multiple_of(start, NODE_ROWS), NODE_ROWS)


def half_rows(array, sub):
    half = array.shape[1] // 2
    return pl.ds(pl.multiple_of(half * sub, half), half)


def flat(value):
    return value.reshape(value.shape[0] * value.shape[1], value.shape[2])


def pick(select, values):
    return dot(select, values.astype(BF16))


def on_level(section):
    return pl.when(lax.axis_index(LEVEL) == section)


def off_level(section):
    return pl.when(lax.axis_index(LEVEL) != section)


def keep(section, kept, outs):
    @off_level(section)
    def _():
        for before, after in zip(kept, outs):
            after[...] = before[...]


def fill_tables(parent, select, choose):
    nodes = parent.shape[1]
    size = nodes * NODE_ROWS
    top = lax.axis_size(LEVEL) - 1
    level, shift = lax.axis_index(LEVEL), lax.axis_index(SUB) * (nodes // 2)

    def target(row, axis):
        shape = (nodes, size) if axis else (size, nodes)
        child = lax.broadcasted_iota(jnp.int32, shape, axis) // NODE_ROWS + shift
        child = jnp.where(child >= nodes, child - nodes, child)
        same = child == lax.broadcasted_iota(jnp.int32, shape, 1 - axis)
        row = row - shift
        row = jnp.where(row < 0, row + nodes, row)
        if axis:
            found = dot(row.astype(F32).astype(BF16), same.astype(F32).astype(BF16))
        else:
            found = jnp.sum(jnp.where(same, row.astype(F32), 0.0), axis=1, keepdims=True)
        place = lax.broadcasted_iota(jnp.int32, found.shape, axis)
        return found.astype(jnp.int32) * NODE_ROWS + lax.rem(place, NODE_ROWS)

    up = target(parent[pl.ds(jnp.minimum(level, top - 1), 1), :], 1)
    down = target(parent[pl.ds(jnp.maximum(level - 1, 0), 1), :], 0)
    index = lax.broadcasted_iota(jnp.int32, (size, size), 0)
    select[...] = (index == up).astype(F32).astype(BF16)
    index = lax.broadcasted_iota(jnp.int32, (size, size), 1)
    choose[...] = (index == down).astype(F32).astype(BF16)


def start_kernel(parent, rhs, inv, off, select, choose, rhs_own, rhs_sent, home, swap, merged, *refs):
    *updates, parent_here, inv_here, off_here, sems = refs
    count = inv.shape[0]
    chunks = len(updates) // 2
    size = count * NODE_ROWS
    level, sub = lax.axis_index(LEVEL), lax.axis_index(SUB)
    table = pltpu.make_async_copy(parent, parent_here, sems.at[0, 0])
    mine = pltpu.make_async_copy(rhs.at[:, half_rows(rhs, sub), :], rhs_own, sems.at[0, 1])
    other = pltpu.make_async_copy(rhs.at[:, half_rows(rhs, 1 - sub), :], rhs_sent, sems.at[0, 2])
    table.start()
    loads = []
    for group in range(count // LOAD_NODES):
        here = pl.ds(group * LOAD_NODES, LOAD_NODES)
        loads.append(pltpu.make_async_copy(inv.at[here], inv_here.at[here], sems.at[1, group]))
        loads.append(pltpu.make_async_copy(off.at[here], off_here.at[here], sems.at[2, group]))
        loads[-2].start()
        loads[-1].start()
        if group == 0:
            mine.start()
            other.start()
    table.wait()
    fill_tables(parent_here, select, choose)
    mine.wait()
    other.wait()

    @on_level(0)
    def _():
        for node in range(count):
            if node % LOAD_NODES == 0:
                loads[2 * (node // LOAD_NODES)].wait()
                loads[2 * (node // LOAD_NODES) + 1].wait()
            right_side = jnp.concatenate([rhs_own[node], rhs_sent[node]], axis=0).astype(BF16)
            forward = dot(right_side, inv_here[node]).astype(BF16)
            update = dot(forward, off_here[node])
            for c in range(2 * chunks):
                updates[c][node] = update[NODE_ROWS * c : NODE_ROWS * (c + 1)]
        chosen = select[:, :size]
        for c in range(chunks):
            home[2 * count * c : 2 * count * (c + 1)] = pick(chosen, flat(updates[c][...])).reshape(2 * count, *home.shape[1:])
            sums = pick(chosen, flat(updates[chunks + c][...])).reshape(2 * count, *home.shape[1:]).astype(BF16)
            swap[2 * count * c : 2 * count * c + count] = sums[count:]
            swap[2 * count * c + count : 2 * count * (c + 1)] = sums[:count]

    @off_level(0)
    def _():
        for node in range(count):
            if node % LOAD_NODES == 0:
                loads[2 * (node // LOAD_NODES)].wait()
                loads[2 * (node // LOAD_NODES) + 1].wait()
            merged[node] = dot(inv_here[node], off_here[node]).astype(BF16)


def merge_kernel(low_inv, up_inv, up_off, ancestor, packed, *scratch):
    low_here, up_here, off_here, rows, sems = scratch
    count = low_inv.shape[0]
    sub = lax.axis_index(SUB)
    loads = []
    for group in range(count // LOAD_NODES):
        here = pl.ds(group * LOAD_NODES, LOAD_NODES)
        loads.append(pltpu.make_async_copy(up_inv.at[here], up_here.at[here], sems.at[1, group]))
        loads.append(pltpu.make_async_copy(low_inv.at[here], low_here.at[here], sems.at[0, group]))
        loads.append(pltpu.make_async_copy(up_off.at[here], off_here.at[here], sems.at[2, group]))
    loads.append(pltpu.make_async_copy(ancestor.at[:, half_rows(ancestor, 1 - sub), :], rows, sems.at[3, 0]))
    for load in loads:
        load.start()
    for node in range(count):
        if node % LOAD_NODES == 0:
            for load in loads[3 * (node // LOAD_NODES) : 3 * (node // LOAD_NODES) + 3]:
                load.wait()
        packed[node] = dot(low_here[node], up_here[node]).astype(BF16)
        packed[count + node] = dot(off_here[node], up_here[node]).astype(BF16)
    loads[-1].wait()
    packed[2 * count :] = rows[...].reshape(packed.shape[0] - 2 * count, *packed.shape[1:])


def residue_of(c, rhs_own, rhs_far, incoming, node):
    count = rhs_own.shape[0]
    rows = slice(NODE_ROWS * c, NODE_ROWS * (c + 1))
    right_side = rhs_own[node, rows, :] if node < count else rhs_far[node - count, rows, :]
    return (right_side - incoming[node].astype(F32)).astype(BF16)


def tier_role(c, at):
    count = at["rhs_own"].shape[0]
    own, far = at["own", c], at["far", c]
    for node in range(2 * count):
        value = residue_of(c, at["rhs_own"], at["rhs_far"], at["received"], node)
        at["residue", c][node] = value.astype(F32)
        if node < count:
            own[node] = dot(value, at["up_own"][node])
        else:
            far[node - count] = dot(value, at["up_far"][node - count])
    updates = jnp.concatenate([flat(own[...]), flat(far[...])], axis=0)
    at["sent"][...] = pick(at["select"][...], updates).reshape(at["sent"].shape).astype(BF16)


def send_solved(c, at):
    if "sent" in at:
        solved = jnp.concatenate([flat(at["sol_own", c][...]), flat(at["sol_far", c][...])], axis=0).astype(BF16)
        rows = dot(at["choose"][...], solved)
        rows = rows.reshape(rows.shape[0] // NODE_ROWS, NODE_ROWS, rows.shape[1]).astype(BF16)
        at["sent"][...] = rows[: at["sent"].shape[0]]
        if CROSS in at:
            at[CROSS][...] = rows[at["sent"].shape[0] :]


def top_role(c, at):
    count = at["rhs_own"].shape[0]
    base = at["top_base", c]
    for node in range(2 * count):
        value = residue_of(c, at["rhs_own"], at["rhs_far"], at["received"], node)
        at["residue", c][node] = value.astype(F32)
        if node < count:
            at["sol_own", c][node] = dot(value, at["down_own"][node]) - base[node]
        else:
            at["sol_far", c][node - count] = dot(value, at["down_far"][node - count]) - base[node]
    send_solved(c, at)


def back_role(c, at):
    count = at["sol_own", c].shape[0]
    base, above = at["low_base", c], at["received"]
    for node in range(count):
        at["sol_own", c][node] = base[node] - dot(above[node], at["down_own"][count + node])
        at["sol_far", c][node] = base[count + node] - dot(above[count + node], at["down_far"][count + node])
    send_solved(c, at)


def last_role(c, at):
    count = at["sol_own", c].shape[0]
    for node in range(count):
        above = jnp.concatenate([at["received"][node].astype(F32), at[CROSS][node].astype(F32)], axis=0)
        solved = dot(above.astype(BF16), at["down_own"][count + node])
        at["sol_own", c][node] = at["low_base", c][node] - solved[:NODE_ROWS]
        at[OTHER, c][node] = at[BELOW][node] - solved[NODE_ROWS:]


def sum_role(c, at):
    rows = slice(c * at["sent"].shape[0], (c + 1) * at["sent"].shape[0])
    at["sent"][...] = (at["home"][rows] + at["swapped"][rows].astype(F32)).astype(BF16)


ROLES = {"tier": tier_role, "top": top_role, "back": back_role, LAST: last_role, "sum": sum_role}
READS = {
    "tier": ("rhs_own", "rhs_far", "received", "up_own", "up_far", "select"),
    "top": ("rhs_own", "rhs_far", "received", "down_own", "down_far", "choose", "top_base"),
    "back": ("received", "down_own", "down_far", "choose", "low_base"),
    LAST: ("received", CROSS, "down_own", "low_base", BELOW),
    "sum": ("home", "swapped"),
}
WRITES = {
    "tier": ("residue", "own", "far"),
    "top": ("residue", "sol_own", "sol_far"),
    "back": ("sol_own", "sol_far"),
    LAST: ("sol_own", OTHER),
    "sum": (),
}


def step_kernel(plan, in_keys, out_keys, kept_keys, *refs):
    reads = dict(zip(in_keys, refs))
    kept = dict(zip(kept_keys, refs[len(in_keys) :]))
    outs = dict(zip(out_keys, refs[len(in_keys) + len(kept_keys) :]))
    for level, role, c in plan:
        writes = [(name, c) for name in WRITES[role]]
        keep(level, [kept[key] for key in writes if key in kept], [outs[key] for key in writes if key in kept])
        pl.when(lax.axis_index(LEVEL) == level)(functools.partial(ROLES[role], c, {**reads, **outs}))


def step(plan, state, sends=1, flops=10**9):
    nodes = state["nodes"]
    in_keys, out_keys = [], []
    for _, role, c in plan:
        for name in READS[role]:
            key = (name, c) if name.endswith("_base") else name
            if key not in in_keys:
                in_keys.append(key)
        out_keys += [(name, c) for name in WRITES[role]]
    kept_keys = [key for key in out_keys if key in state]
    width = state["rhs_own"].shape[2]
    outs = []
    for name, _ in out_keys:
        of = nodes if name == "residue" else nodes // 2
        outs.append(jax.ShapeDtypeStruct((of, NODE_ROWS, width), F32))
    aliases = {len(in_keys) + i: out_keys.index(key) for i, key in enumerate(kept_keys)}
    all_outs = out_keys + ["sent", CROSS][:sends]
    outs += [jax.ShapeDtypeStruct((nodes // max(sends, 1), NODE_ROWS, width), BF16)] * sends
    operands = [state[key] for key in in_keys + kept_keys]
    results = run(functools.partial(step_kernel, plan, in_keys, all_outs, kept_keys), operands, outs, aliases, flops)
    state.update(zip(out_keys, results))
    return results[len(out_keys) :]


def rows_together(chunks, node):
    return jnp.concatenate([chunk[node] for chunk in chunks], axis=0).astype(BF16)


def apart(value, chunks, node):
    for c, chunk in enumerate(chunks):
        chunk[node] = value[NODE_ROWS * c : NODE_ROWS * (c + 1)]


def base_kernel(rhs_own, rhs_far, rhs_sent, own, far, *refs):
    *refs, below = refs
    residue, base = refs[: len(refs) // 2], refs[len(refs) // 2 :]
    count = rhs_own.shape[0]
    level, top = lax.axis_index(LEVEL), lax.axis_size(LEVEL) - 1

    @pl.when(level == 0)
    def _():
        for node in range(count):
            both = jnp.concatenate([rhs_own[node], rhs_sent[node, -NODE_ROWS:, :]], axis=0).astype(BF16)
            solved = dot(both, own[node])
            apart(solved, base, node)
            below[node] = solved[-NODE_ROWS:]
            apart(dot(rhs_far[node].astype(BF16), far[node]), base, count + node)

    @pl.when((level != 0) & (level != top))
    def _():
        for node in range(count):
            apart(dot(rows_together(residue, node), own[node]), base, node)
            apart(dot(rows_together(residue, count + node), far[node]), base, count + node)


def update_kernel(up_own, up_far, *refs):
    chunks = (len(refs) - 2) // 3
    residue, own_kept, far_kept = (refs[chunks * i : chunks * (i + 1)] for i in range(3))
    upd_own, upd_far = refs[-2:]
    level, top = lax.axis_index(LEVEL), lax.axis_size(LEVEL) - 1

    @pl.when(level == top)
    def _():
        count = up_own.shape[0]
        for node in range(count):
            upd_own[node] = dot(rows_together(residue, node), up_own[node])
            upd_far[node] = dot(rows_together(residue, count + node), up_far[node])

    @pl.when(level != top)
    def _():
        for c in range(chunks):
            rows = slice(NODE_ROWS * c, NODE_ROWS * (c + 1))
            upd_own[:, rows, :] = own_kept[c][...]
            upd_far[:, rows, :] = far_kept[c][...]


def ancestor_kernel(section, ancestor, own, far, *refs):
    *bases, here, sem = refs
    count, half, _ = here.shape
    sub = lax.axis_index(SUB)

    @on_level(section)
    def _():
        load = pltpu.make_async_copy(ancestor.at[:, half_rows(ancestor, sub), :], here, sem.at[0])
        load.start()
        load.wait()
        for node in range(count):
            per = far.shape[1] // half
            other = far[2 * count + node // per, half * (node % per) : half * (node % per + 1), :]
            mine = dot(here[node], own[count + node])
            other = dot(other, far[count + node])
            for c, base in enumerate(bases):
                base[node] = mine[NODE_ROWS * c : NODE_ROWS * (c + 1)]
                base[count + node] = other[NODE_ROWS * c : NODE_ROWS * (c + 1)]


def put(here, other, first, out, sems):
    sub = lax.axis_index(SUB)
    half = out.shape[1] // 2
    copies = []
    for i, (mine, theirs, row) in enumerate(zip(here, other, first)):
        size = mine.shape[1]
        to_mine = pl.ds(pl.multiple_of(half * sub + row, NODE_ROWS), size)
        to_theirs = pl.ds(pl.multiple_of(half * (1 - sub) + row, NODE_ROWS), size)
        copies.append(pltpu.make_async_copy(mine, out.at[:, to_mine, :], sems.at[0, i]))
        copies.append(pltpu.make_async_copy(theirs, out.at[:, to_theirs, :], sems.at[1, i]))
    for copy in copies:
        copy.start()
    for copy in copies:
        copy.wait()


def place_kernel(first, *refs):
    count = len(first)
    put(refs[:count], refs[count : 2 * count], first, *refs[-2:])


def place_bottom_kernel(here, far, other, *refs):
    @on_level(0)
    def _():
        put([here], [far], [0], *refs[-2:])

    @off_level(0)
    def _():
        put([here], [other], [0], *refs[-2:])


def run(kernel, operands, outs, aliases=None, flops=10**9, whole=None, scratch=(), raw=()):
    in_specs = [IN_HBM] * len(raw) + [IN_VMEM] * len(operands)
    operands = [*(pltpu.with_memory_space_constraint(value, pltpu.HBM) for value in raw), *(pltpu.with_memory_space_constraint(value, pltpu.VMEM) for value in operands)]
    out_specs = [IN_VMEM] * len(outs)
    out_shape = [pltpu.VMEM(out.shape, out.dtype) for out in outs]
    aliases = dict(aliases or {})
    if whole is not None:
        shape, before = whole
        if before is not None:
            aliases[len(operands)] = len(outs)
            operands.append(before)
            in_specs.append(IN_ANY)
        out_shape.append(shape)
        out_specs.append(IN_ANY)
    return pl.pallas_call(
        kernel,
        in_specs=in_specs,
        out_specs=out_specs,
        out_shape=out_shape,
        input_output_aliases=aliases,
        scratch_shapes=scratch,
        compiler_params=pltpu.CompilerParams(vmem_limit_bytes=SMALL_VMEM_BYTES),
        cost_estimate=pl.CostEstimate(
            flops=flops, bytes_accessed=10**6, transcendentals=0
        ),
    )(*operands)


def exchanged(value):
    return lax.ppermute(value, SUB, [(0, 1), (1, 0)])


def pair_body(rhs, lower_inv, lower_off, upper_inv, upper_off, ancestor, parent):
    levels = lax.axis_size(LEVEL)
    top = levels - 1
    rhs, lower_inv, lower_off, upper_inv, upper_off = (
        value[0] for value in (rhs, lower_inv, lower_off, upper_inv, upper_off)
    )
    count, all_rows, width = rhs.shape
    half = all_rows // 2
    chunks = half // NODE_ROWS
    nodes = 2 * count
    size = nodes * NODE_ROWS

    def shape(of, dtype):
        return jax.ShapeDtypeStruct((of, NODE_ROWS, width), dtype)

    def passed(value, pairs, cross=False):
        sources = [i for i in range(levels) if i not in dict(pairs)]
        targets = [i for i in range(levels) if i not in [to for _, to in pairs]]
        fill = min(
            (list(zip(sources, order)) for order in itertools.permutations(targets)),
            key=lambda extra: (sum(a == b for a, b in extra), sum(abs(a - b) for a, b in extra)),
        )
        if cross:
            pairs = [(2 * a + s, 2 * b + 1 - s) for a, b in pairs + fill for s in range(2)]
            return lax.ppermute(value, (LEVEL, SUB), pairs)
        return lax.ppermute(value, LEVEL, pairs + fill)

    def after(value, *earlier):
        return lax.optimization_barrier((value, *earlier))[0]

    matrices = jax.ShapeDtypeStruct(lower_inv.shape, BF16)
    table = jax.ShapeDtypeStruct((size, size), BF16)
    half_shape = jax.ShapeDtypeStruct((count, half, width), F32)
    block = pltpu.VMEM(lower_inv.shape, BF16)
    state = {"nodes": nodes}
    select, choose, rhs_own, rhs_sent, home, swap, up_own, *updates = run(
        start_kernel, (),
        [table, table, half_shape, half_shape, shape(chunks * nodes, F32), shape(chunks * nodes, BF16), matrices]
        + [shape(count, F32)] * (2 * chunks),
        raw=(parent, rhs, lower_inv, lower_off),
        scratch=[pltpu.VMEM(parent.shape, parent.dtype), block, block, pltpu.SemaphoreType.DMA((3, max(count // LOAD_NODES, 3)))],
    )
    state.update(select=select, choose=choose, rhs_own=rhs_own, home=home, up_own=up_own, swapped=exchanged(swap))
    for c in range(chunks):
        state["own", c], state["far", c] = updates[c], updates[chunks + c]

    packed_shape = (2 * count + count * half // width, width, width)
    merge_scratch = [block, block, block, pltpu.VMEM((count, half, width), BF16), pltpu.SemaphoreType.DMA((4, count // LOAD_NODES))]

    def merged(sent):
        low, *others = lax.optimization_barrier((lower_inv, upper_inv, upper_off, ancestor, sent))
        return run(
            merge_kernel, (), [jax.ShapeDtypeStruct(packed_shape, BF16)],
            raw=(low, *others[:3]), scratch=merge_scratch,
        )[0]

    whole = jax.ShapeDtypeStruct(rhs.shape, F32)

    def sems(pieces):
        return [pltpu.SemaphoreType.DMA((2, pieces))]

    def placed(group, before, *earlier):
        first = after(state["sol_own", group[0]], *earlier) if earlier else state["sol_own", group[0]]
        return run(
            functools.partial(place_kernel, [NODE_ROWS * c for c in group]),
            [first, *(state["sol_own", c] for c in group[1:]), *(other[c] for c in group)],
            [], whole=(whole, before), scratch=sems(len(group)),
        )[0]

    pipes = [list(range(chunks))[i : i + 2] for i in range(0, chunks, 2)]
    received = [None] * len(pipes)
    other = [None] * chunks
    pace = []
    last = 2 * top + 1
    for k in range(last + 1):
        for p, pipe in enumerate(pipes):
            plan, pairs = [], []
            for j, c in enumerate(pipe):
                tier = k - j
                if 0 <= tier < top:
                    plan.append((tier, "sum" if tier == 0 else "tier", c))
                    pairs.append((tier, tier + 1))
                elif tier == top:
                    plan.append((top, "top", c))
                    pairs.append((top, top - 1))
                elif top < tier <= 2 * top:
                    low = 2 * top - tier
                    plan.append((low, "back", c))
                    if low:
                        pairs.append((low, low - 1))
            if received[p] is not None:
                state["received"] = after(received[p], *pace)
            split = k == last - 1 and p == len(pipes) - 1
            if k == last and p == len(pipes) - 1:
                state[CROSS], state[OTHER, pipe[-1]] = cross, other[pipe[-1]]
                plan = [(0, LAST, pipe[-1])]
            sent, *sent_cross = step(plan, state, 2 if split else bool(pairs), COSTS[k]) or [None]
            if k == last and p == len(pipes) - 1:
                other[pipe[-1]] = state[OTHER, pipe[-1]]
            elif k == last:
                other[pipe[-1]] = exchanged(state["sol_far", pipe[-1]])
            if split:
                cross = passed(sent_cross[0], pairs, cross=True)
                other[pipe[-1]] = exchanged(state["sol_far", pipe[-1]])
            pace = [sent] if pairs else [state["sol_own", pipe[-1]]]
            if pairs:
                received[p] = passed(sent, pairs)
            if p == 0 and k == 0:
                state["up_far"] = exchanged(after(up_own, sent))
                state["rhs_far"] = exchanged(after(rhs_sent, sent))
            if p == 0 and k == 1:
                state["down_far"] = exchanged(state["down_own"])
            if p == 0 and k == last:
                (update,) = run(
                    place_bottom_kernel, (upd_own, after(upd_far, *pace), upd_other), [], whole=(whole, None), scratch=sems(1)
                )
                early = [pipe[0] for pipe in pipes]
                other[early[0]], other[early[1]] = (exchanged(state["sol_far", c]) for c in early)
                solved = placed(early, None, update)
                pace = [solved]
        if k == 0:
            state["down_own"] = merged(sent)
            pace.append(state["down_own"])
        if k == top - 1:
            bases = run(
                functools.partial(ancestor_kernel, top),
                (state["down_own"], state["down_far"]),
                [shape(nodes, F32)] * chunks,
                raw=(after(ancestor, sent),),
                scratch=[pltpu.VMEM((count, half, width), BF16), pltpu.SemaphoreType.DMA((1,))],
            )
            state.update({("top_base", c): bases[c] for c in range(chunks)})
            pace += bases
        residues = [state["residue", c] for c in range(chunks)] if k >= top else []
        if k == top:
            *bases, state[BELOW] = run(
                base_kernel,
                (after(rhs_own, sent), state["rhs_far"], rhs_sent, state["down_own"], state["down_far"], *residues),
                [shape(nodes, F32)] * chunks + [shape(count, F32)],
            )
            state.update({("low_base", c): bases[c] for c in range(chunks)})
            pace += bases
        if k == top + 2:
            upd_own, upd_far = run(
                update_kernel,
                (up_own, state["up_far"], *residues, *(state["own", c] for c in range(chunks)), *(state["far", c] for c in range(chunks))),
                [half_shape] * 2,
            )
            upd_other = exchanged(upd_far)
    solved = placed([pipe[-1] for pipe in pipes], solved)
    return solved[None], update[None]


def solution(mesh):
    placed = (
        P(LEVEL, SUB, "rhs", None),
        P(LEVEL, SUB, None, None),
        P(LEVEL, SUB, None, None),
        P(LEVEL, SUB, None, None),
        P(LEVEL, SUB, None, None),
        P(SUB, "rhs", None),
        P(),
    )
    return jax.shard_map(
        pair_body if mesh.shape[SUB] == 2 else general_body,
        mesh=mesh,
        in_specs=placed,
        out_specs=(P(LEVEL, SUB, "rhs", None), P(LEVEL, SUB, "rhs", None)),
        check_vma=False,
    )
```

```python
import functools
import itertools

import jax
import jax.numpy as jnp
from jax import lax
from jax.experimental import pallas as pl
from jax.experimental.pallas import tpu as pltpu
from jax.sharding import PartitionSpec as P

CHUNKS = 2
LOCAL_SWAP = False
VMEM_BYTES = 24 * 2**20

LEVEL, SUB = "level", "sub"
BF16 = jnp.bfloat16
F32 = jnp.float32
IN_VMEM = pl.BlockSpec(memory_space=pltpu.VMEM)
IN_SMEM = pl.BlockSpec(memory_space=pltpu.SMEM)


def dot(left, right):
    return jnp.dot(left, right, preferred_element_type=F32)


def forward_kernel(section, start, rows, info, rhs, incoming, inv, off, kept_f, kept_u, fwd, upd, home, far, total):
    count = inv.shape[0]

    @pl.when(info[count] != section)
    def _():
        fwd[...] = kept_f[...]
        upd[...] = kept_u[...]

    @pl.when(info[count] == section)
    def _():
        total[...] = jnp.zeros_like(total)
        for node in range(count):
            right_side = rhs[node, pl.ds(start, rows), :]
            if incoming is not None:
                right_side = right_side - incoming[node].astype(F32)
            forward = dot(right_side.astype(BF16), inv[node]).astype(BF16)
            fwd[node] = forward
            update = dot(forward, off[node])
            upd[node] = update
            total[info[node]] += update
        home[...] = total[:count]
        far[...] = total[count:].astype(BF16)


def first_kernel(section, start, rows, info, rhs, inv, off, kept_f, kept_u, fwd, upd, home, far, total):
    forward_kernel(section, start, rows, info, rhs, None, inv, off, kept_f, kept_u, fwd, upd, home, far, total)


def top_kernel(section, start, rows, info, rhs, incoming, inv, up_off, up_inv, ancestor, kept_f, kept_s, fwd, sol, sol_bf):
    count = inv.shape[0]

    @pl.when(info[count] != section)
    def _():
        fwd[...] = kept_f[...]
        sol[...] = kept_s[...]

    @pl.when(info[count] == section)
    def _():
        for node in range(count):
            right_side = rhs[node, pl.ds(start, rows), :] - incoming[node].astype(F32)
            forward = dot(right_side.astype(BF16), inv[node]).astype(BF16)
            fwd[node] = forward
            above = dot(ancestor[node, pl.ds(start, rows), :], up_off[node])
            reduced = (forward.astype(F32) - above).astype(BF16)
            solved = dot(reduced, up_inv[node])
            sol[node] = solved
            sol_bf[node] = solved.astype(BF16)


def top_update_kernel(section, start, rows, info, fwd, off, kept_u, upd):
    count = off.shape[0]

    @pl.when(info[count] != section)
    def _():
        upd[...] = kept_u[...]

    @pl.when(info[count] == section)
    def _():
        for node in range(count):
            upd[node] = dot(fwd[node], off[node])


def backward_kernel(section, start, rows, info, fwd, own, partner, up_off, up_inv, kept_s, sol, sol_bf):
    count = up_inv.shape[0]

    @pl.when(info[count] != section)
    def _():
        sol[...] = kept_s[...]

    @pl.when(info[count] == section)
    def _():
        for node in range(count):
            place = info[node]
            at_home = place < count
            slot = jnp.where(at_home, place, place - count)
            above = jnp.where(at_home, own[slot], partner[slot])
            reduced = (fwd[node].astype(F32) - dot(above, up_off[node])).astype(BF16)
            solved = dot(reduced, up_inv[node])
            sol[node] = solved
            sol_bf[node] = solved.astype(BF16)


def call(kernel, section, start, rows, operands, outs, aliases, scratch=(), products=2):
    count = operands[1].shape[0]
    return pl.pallas_call(
        functools.partial(kernel, section, start, rows),
        in_specs=[IN_SMEM] + [IN_VMEM] * (len(operands) - 1),
        out_specs=[IN_VMEM] * len(outs),
        out_shape=outs,
        scratch_shapes=scratch,
        input_output_aliases=aliases,
        compiler_params=pltpu.CompilerParams(vmem_limit_bytes=VMEM_BYTES),
        cost_estimate=pl.CostEstimate(
            flops=products * 2 * count * rows * 256 * 256, bytes_accessed=count * 256 * 256 * 2 * products, transcendentals=0
        ),
    )(*operands)


def swapped(value, section, apart):
    mask = 2**apart
    subs = lax.axis_size(SUB)
    if not LOCAL_SWAP:
        return lax.ppermute(value, SUB, [(i, i ^ mask) for i in range(subs)])
    pairs = [(section * subs + i, section * subs + (i ^ mask)) for i in range(subs)]
    return lax.ppermute(value, (LEVEL, SUB), pairs)


def general_body(rhs, lower_inv, lower_off, upper_inv, upper_off, ancestor, parent):
    levels = lax.axis_size(LEVEL)
    sub_count = lax.axis_size(SUB)
    sub_bits = sub_count.bit_length() - 1
    tier = lax.axis_index(LEVEL)
    sub = lax.axis_index(SUB)
    rhs, lower_inv, lower_off, upper_inv, upper_off = (
        value[0] for value in (rhs, lower_inv, lower_off, upper_inv, upper_off)
    )
    count, all_rows, width = rhs.shape
    rows = all_rows // CHUNKS
    parent_row = lax.dynamic_index_in_dim(parent, jnp.minimum(tier, levels - 2), 0, keepdims=False)
    parent_here = lax.dynamic_slice_in_dim(parent_row, sub * count, count)
    place = parent_here % count + jnp.where(parent_here // count == sub, 0, count)
    info = jnp.concatenate([place, tier[None]]).astype(jnp.int32)

    def shape(dtype):
        return jax.ShapeDtypeStruct((count, rows, width), dtype)

    fwd = [jnp.zeros((count, rows, width), BF16) for _ in range(CHUNKS)]
    upd = [jnp.zeros((count, rows, width), F32) for _ in range(CHUNKS)]
    sol = [jnp.zeros((count, rows, width), F32) for _ in range(CHUNKS)]
    incoming = [None] * CHUNKS
    above = [None] * CHUNKS
    top = levels - 1
    for section in range(top):
        for c in range(CHUNKS):
            if section == 0:
                kernel, operands = first_kernel, (info, rhs, lower_inv, lower_off, fwd[c], upd[c])
            else:
                kernel, operands = forward_kernel, (info, rhs, incoming[c], lower_inv, lower_off, fwd[c], upd[c])
            at = len(operands) - 2
            fwd[c], upd[c], home, far = call(
                kernel, section, c * rows, rows, operands,
                [shape(BF16), shape(F32), shape(F32), shape(BF16)], {at: 0, at + 1: 1},
                [pltpu.VMEM((2 * count, rows, width), F32)],
            )
            received = swapped(far, section, section % sub_bits)
            summed = (home + received.astype(F32)).astype(BF16)
            incoming[c] = lax.ppermute(summed, LEVEL, [(section, section + 1)])
    for c in range(CHUNKS):
        fwd[c], sol[c], solved = call(
            top_kernel, top, c * rows, rows,
            (info, rhs, incoming[c], lower_inv, upper_off, upper_inv, ancestor, fwd[c], sol[c]),
            [shape(BF16), shape(F32), shape(BF16)], {7: 0, 8: 1}, products=3,
        )
        above[c] = lax.ppermute(solved, LEVEL, [(top, top - 1)])
    for c in range(CHUNKS):
        (upd[c],) = call(top_update_kernel, top, c * rows, rows, (info, fwd[c], lower_off, upd[c]), [shape(F32)], {3: 0}, products=1)
    for section in reversed(range(top)):
        for c in range(CHUNKS):
            partner = swapped(above[c], section, section % sub_bits)
            sol[c], solved = call(
                backward_kernel, section, c * rows, rows,
                (info, fwd[c], above[c], partner, upper_off, upper_inv, sol[c]),
                [shape(F32), shape(BF16)], {6: 0},
            )
            if section:
                above[c] = lax.ppermute(solved, LEVEL, [(section, section - 1)])
    return jnp.concatenate(sol, axis=1)[None], jnp.concatenate(upd, axis=1)[None]


NODE_ROWS = 8
CROSS, OTHER, BELOW, LAST = "c", "o", "b", "l"
LOAD_NODES = 4
COSTS = [30000000000, 30000000000, 30000000000, 5000000000, 5000000000, 5000000000, 5000000000, 5000000000]
SMALL_VMEM_BYTES = 12 * 2**20
IN_ANY = pl.BlockSpec(memory_space=pl.ANY)
IN_HBM = pl.BlockSpec(memory_space=pltpu.HBM)


def rows_of(start):
    return pl.ds(pl.multiple_of(start, NODE_ROWS), NODE_ROWS)


def half_rows(array, sub):
    half = array.shape[1] // 2
    return pl.ds(pl.multiple_of(half * sub, half), half)


def flat(value):
    return value.reshape(value.shape[0] * value.shape[1], value.shape[2])


def pick(select, values):
    return dot(select, values.astype(BF16))


def on_level(section):
    return pl.when(lax.axis_index(LEVEL) == section)


def off_level(section):
    return pl.when(lax.axis_index(LEVEL) != section)


def keep(section, kept, outs):
    @off_level(section)
    def _():
        for before, after in zip(kept, outs):
            after[...] = before[...]


def fill_tables(parent, select, choose):
    nodes = parent.shape[1]
    size = nodes * NODE_ROWS
    top = lax.axis_size(LEVEL) - 1
    level, shift = lax.axis_index(LEVEL), lax.axis_index(SUB) * (nodes // 2)

    def target(row, axis):
        shape = (nodes, size) if axis else (size, nodes)
        child = lax.broadcasted_iota(jnp.int32, shape, axis) // NODE_ROWS + shift
        child = jnp.where(child >= nodes, child - nodes, child)
        same = child == lax.broadcasted_iota(jnp.int32, shape, 1 - axis)
        row = row - shift
        row = jnp.where(row < 0, row + nodes, row)
        if axis:
            found = dot(row.astype(F32).astype(BF16), same.astype(F32).astype(BF16))
        else:
            found = jnp.sum(jnp.where(same, row.astype(F32), 0.0), axis=1, keepdims=True)
        place = lax.broadcasted_iota(jnp.int32, found.shape, axis)
        return found.astype(jnp.int32) * NODE_ROWS + lax.rem(place, NODE_ROWS)

    up = target(parent[pl.ds(jnp.minimum(level, top - 1), 1), :], 1)
    down = target(parent[pl.ds(jnp.maximum(level - 1, 0), 1), :], 0)
    index = lax.broadcasted_iota(jnp.int32, (size, size), 0)
    select[...] = (index == up).astype(F32).astype(BF16)
    index = lax.broadcasted_iota(jnp.int32, (size, size), 1)
    choose[...] = (index == down).astype(F32).astype(BF16)


def start_kernel(parent, rhs, inv, off, select, choose, rhs_own, rhs_sent, home, swap_first, swap_rest, merged, *refs):
    *updates, parent_here, inv_here, off_here, sems = refs
    count = inv.shape[0]
    chunks = len(updates) // 2
    size = count * NODE_ROWS
    level, sub = lax.axis_index(LEVEL), lax.axis_index(SUB)
    table = pltpu.make_async_copy(parent, parent_here, sems.at[0, 0])
    mine = pltpu.make_async_copy(rhs.at[:, half_rows(rhs, sub), :], rhs_own, sems.at[0, 1])
    other = pltpu.make_async_copy(rhs.at[:, half_rows(rhs, 1 - sub), :], rhs_sent, sems.at[0, 2])
    table.start()
    loads = []
    for group in range(count // LOAD_NODES):
        here = pl.ds(group * LOAD_NODES, LOAD_NODES)
        loads.append(pltpu.make_async_copy(inv.at[here], inv_here.at[here], sems.at[1, group]))
        loads.append(pltpu.make_async_copy(off.at[here], off_here.at[here], sems.at[2, group]))
        loads[-2].start()
        loads[-1].start()
        if group == 0:
            mine.start()
            other.start()
    table.wait()
    fill_tables(parent_here, select, choose)
    mine.wait()
    other.wait()

    @on_level(0)
    def _():
        for node in range(count):
            if node % LOAD_NODES == 0:
                loads[2 * (node // LOAD_NODES)].wait()
                loads[2 * (node // LOAD_NODES) + 1].wait()
            right_side = jnp.concatenate([rhs_own[node], rhs_sent[node]], axis=0).astype(BF16)
            forward = dot(right_side, inv_here[node]).astype(BF16)
            update = dot(forward, off_here[node])
            for c in range(2 * chunks):
                updates[c][node] = update[NODE_ROWS * c : NODE_ROWS * (c + 1)]
        chosen = select[:, :size]
        for c in range(chunks):
            home[2 * count * c : 2 * count * (c + 1)] = pick(chosen, flat(updates[c][...])).reshape(2 * count, *home.shape[1:])
            sums = pick(chosen, flat(updates[chunks + c][...])).reshape(2 * count, *home.shape[1:]).astype(BF16)
            swap, at = (swap_first, swap_rest)[c % 2], 2 * count * (c // 2)
            swap[at : at + count] = sums[count:]
            swap[at + count : at + 2 * count] = sums[:count]

    @off_level(0)
    def _():
        for node in range(count):
            if node % LOAD_NODES == 0:
                loads[2 * (node // LOAD_NODES)].wait()
                loads[2 * (node // LOAD_NODES) + 1].wait()
            merged[node] = dot(inv_here[node], off_here[node]).astype(BF16)


def merge_kernel(low_inv, up_inv, up_off, ancestor, packed, *scratch):
    low_here, up_here, off_here, rows, sems = scratch
    count = low_inv.shape[0]
    sub = lax.axis_index(SUB)
    loads = []
    for group in range(count // LOAD_NODES):
        here = pl.ds(group * LOAD_NODES, LOAD_NODES)
        loads.append(pltpu.make_async_copy(up_inv.at[here], up_here.at[here], sems.at[1, group]))
        loads.append(pltpu.make_async_copy(low_inv.at[here], low_here.at[here], sems.at[0, group]))
        loads.append(pltpu.make_async_copy(up_off.at[here], off_here.at[here], sems.at[2, group]))
    loads.append(pltpu.make_async_copy(ancestor.at[:, half_rows(ancestor, 1 - sub), :], rows, sems.at[3, 0]))
    for load in loads:
        load.start()
    for node in range(count):
        if node % LOAD_NODES == 0:
            for load in loads[3 * (node // LOAD_NODES) : 3 * (node // LOAD_NODES) + 3]:
                load.wait()
        packed[node] = dot(low_here[node], up_here[node]).astype(BF16)
        packed[count + node] = dot(off_here[node], up_here[node]).astype(BF16)
    loads[-1].wait()
    packed[2 * count :] = rows[...].reshape(packed.shape[0] - 2 * count, *packed.shape[1:])


def residue_of(c, rhs_own, rhs_far, incoming, node):
    count = rhs_own.shape[0]
    rows = slice(NODE_ROWS * c, NODE_ROWS * (c + 1))
    right_side = rhs_own[node, rows, :] if node < count else rhs_far[node - count, rows, :]
    return (right_side - incoming[node].astype(F32)).astype(BF16)


def tier_role(c, at):
    count = at["rhs_own"].shape[0]
    own, far = at["own", c], at["far", c]
    for node in range(2 * count):
        value = residue_of(c, at["rhs_own"], at["rhs_far"], at["received"], node)
        at["residue", c][node] = value.astype(F32)
        if node < count:
            own[node] = dot(value, at["up_own"][node])
        else:
            far[node - count] = dot(value, at["up_far"][node - count])
    updates = jnp.concatenate([flat(own[...]), flat(far[...])], axis=0)
    at["sent"][...] = pick(at["select"][...], updates).reshape(at["sent"].shape).astype(BF16)


def send_solved(c, at):
    if "sent" in at:
        solved = jnp.concatenate([flat(at["sol_own", c][...]), flat(at["sol_far", c][...])], axis=0).astype(BF16)
        rows = dot(at["choose"][...], solved)
        rows = rows.reshape(rows.shape[0] // NODE_ROWS, NODE_ROWS, rows.shape[1]).astype(BF16)
        at["sent"][...] = rows[: at["sent"].shape[0]]
        if CROSS in at:
            at[CROSS][...] = rows[at["sent"].shape[0] :]


def top_role(c, at):
    count = at["rhs_own"].shape[0]
    base = at["top_base", c]
    for node in range(2 * count):
        value = residue_of(c, at["rhs_own"], at["rhs_far"], at["received"], node)
        at["residue", c][node] = value.astype(F32)
        if node < count:
            at["sol_own", c][node] = dot(value, at["down_own"][node]) - base[node]
        else:
            at["sol_far", c][node - count] = dot(value, at["down_far"][node - count]) - base[node]
    send_solved(c, at)


def back_role(c, at):
    count = at["sol_own", c].shape[0]
    base, above = at["low_base", c], at["received"]
    for node in range(count):
        at["sol_own", c][node] = base[node] - dot(above[node], at["down_own"][count + node])
        at["sol_far", c][node] = base[count + node] - dot(above[count + node], at["down_far"][count + node])
    send_solved(c, at)


def last_role(c, at):
    count = at["sol_own", c].shape[0]
    for node in range(count):
        above = jnp.concatenate([at["received"][node].astype(F32), at[CROSS][node].astype(F32)], axis=0)
        solved = dot(above.astype(BF16), at["down_own"][count + node])
        at["sol_own", c][node] = at["low_base", c][node] - solved[:NODE_ROWS]
        at[OTHER, c][node] = at[BELOW][node] - solved[NODE_ROWS:]


def sum_role(c, at):
    nodes = at["sent"].shape[0]
    home = at["home"][c * nodes : (c + 1) * nodes]
    partner = at["swapped"][c // 2 * nodes : (c // 2 + 1) * nodes]
    at["sent"][...] = (home + partner.astype(F32)).astype(BF16)


ROLES = {"tier": tier_role, "top": top_role, "back": back_role, LAST: last_role, "sum": sum_role}
READS = {
    "tier": ("rhs_own", "rhs_far", "received", "up_own", "up_far", "select"),
    "top": ("rhs_own", "rhs_far", "received", "down_own", "down_far", "choose", "top_base"),
    "back": ("received", "down_own", "down_far", "choose", "low_base"),
    LAST: ("received", CROSS, "down_own", "low_base", BELOW),
    "sum": ("home", "swapped"),
}
WRITES = {
    "tier": ("residue", "own", "far"),
    "top": ("residue", "sol_own", "sol_far"),
    "back": ("sol_own", "sol_far"),
    LAST: ("sol_own", OTHER),
    "sum": (),
}


def step_kernel(plan, in_keys, out_keys, kept_keys, *refs):
    reads = dict(zip(in_keys, refs))
    kept = dict(zip(kept_keys, refs[len(in_keys) :]))
    outs = dict(zip(out_keys, refs[len(in_keys) + len(kept_keys) :]))
    for level, role, c in plan:
        writes = [(name, c) for name in WRITES[role]]
        keep(level, [kept[key] for key in writes if key in kept], [outs[key] for key in writes if key in kept])
        pl.when(lax.axis_index(LEVEL) == level)(functools.partial(ROLES[role], c, {**reads, **outs}))


def step(plan, state, sends=1, flops=10**9):
    nodes = state["nodes"]
    in_keys, out_keys = [], []
    for _, role, c in plan:
        for name in READS[role]:
            key = (name, c) if name.endswith("_base") else name
            if key not in in_keys:
                in_keys.append(key)
        out_keys += [(name, c) for name in WRITES[role]]
    kept_keys = [key for key in out_keys if key in state]
    width = state["rhs_own"].shape[2]
    outs = []
    for name, _ in out_keys:
        of = nodes if name == "residue" else nodes // 2
        outs.append(jax.ShapeDtypeStruct((of, NODE_ROWS, width), F32))
    aliases = {len(in_keys) + i: out_keys.index(key) for i, key in enumerate(kept_keys)}
    all_outs = out_keys + ["sent", CROSS][:sends]
    outs += [jax.ShapeDtypeStruct((nodes // max(sends, 1), NODE_ROWS, width), BF16)] * sends
    operands = [state[key] for key in in_keys + kept_keys]
    results = run(functools.partial(step_kernel, plan, in_keys, all_outs, kept_keys), operands, outs, aliases, flops)
    state.update(zip(out_keys, results))
    return results[len(out_keys) :]


def rows_together(chunks, node):
    return jnp.concatenate([chunk[node] for chunk in chunks], axis=0).astype(BF16)


def apart(value, chunks, node):
    for c, chunk in enumerate(chunks):
        chunk[node] = value[NODE_ROWS * c : NODE_ROWS * (c + 1)]


def base_kernel(rhs_own, rhs_far, rhs_sent, own, far, *refs):
    *refs, below = refs
    residue, base = refs[: len(refs) // 2], refs[len(refs) // 2 :]
    count = rhs_own.shape[0]
    level, top = lax.axis_index(LEVEL), lax.axis_size(LEVEL) - 1

    @pl.when(level == 0)
    def _():
        for node in range(count):
            both = jnp.concatenate([rhs_own[node], rhs_sent[node, -NODE_ROWS:, :]], axis=0).astype(BF16)
            solved = dot(both, own[node])
            apart(solved, base, node)
            below[node] = solved[-NODE_ROWS:]
            apart(dot(rhs_far[node].astype(BF16), far[node]), base, count + node)

    @pl.when((level != 0) & (level != top))
    def _():
        for node in range(count):
            apart(dot(rows_together(residue, node), own[node]), base, node)
            apart(dot(rows_together(residue, count + node), far[node]), base, count + node)


def update_kernel(up_own, up_far, *refs):
    chunks = (len(refs) - 2) // 3
    residue, own_kept, far_kept = (refs[chunks * i : chunks * (i + 1)] for i in range(3))
    upd_own, upd_far = refs[-2:]
    level, top = lax.axis_index(LEVEL), lax.axis_size(LEVEL) - 1

    @pl.when(level == top)
    def _():
        count = up_own.shape[0]
        for node in range(count):
            upd_own[node] = dot(rows_together(residue, node), up_own[node])
            upd_far[node] = dot(rows_together(residue, count + node), up_far[node])

    @pl.when(level != top)
    def _():
        for c in range(chunks):
            rows = slice(NODE_ROWS * c, NODE_ROWS * (c + 1))
            upd_own[:, rows, :] = own_kept[c][...]
            upd_far[:, rows, :] = far_kept[c][...]


def ancestor_kernel(section, ancestor, own, far, *refs):
    *bases, here, sem = refs
    count, half, _ = here.shape
    sub = lax.axis_index(SUB)

    @on_level(section)
    def _():
        load = pltpu.make_async_copy(ancestor.at[:, half_rows(ancestor, sub), :], here, sem.at[0])
        load.start()
        load.wait()
        for node in range(count):
            per = far.shape[1] // half
            other = far[2 * count + node // per, half * (node % per) : half * (node % per + 1), :]
            mine = dot(here[node], own[count + node])
            other = dot(other, far[count + node])
            for c, base in enumerate(bases):
                base[node] = mine[NODE_ROWS * c : NODE_ROWS * (c + 1)]
                base[count + node] = other[NODE_ROWS * c : NODE_ROWS * (c + 1)]


def put(here, other, first, out, sems):
    sub = lax.axis_index(SUB)
    half = out.shape[1] // 2
    copies = []
    for i, (mine, theirs, row) in enumerate(zip(here, other, first)):
        size = mine.shape[1]
        to_mine = pl.ds(pl.multiple_of(half * sub + row, NODE_ROWS), size)
        to_theirs = pl.ds(pl.multiple_of(half * (1 - sub) + row, NODE_ROWS), size)
        copies.append(pltpu.make_async_copy(mine, out.at[:, to_mine, :], sems.at[0, i]))
        copies.append(pltpu.make_async_copy(theirs, out.at[:, to_theirs, :], sems.at[1, i]))
    for copy in copies:
        copy.start()
    for copy in copies:
        copy.wait()


def place_kernel(first, *refs):
    count = len(first)
    put(refs[:count], refs[count : 2 * count], first, *refs[-2:])


def place_bottom_kernel(here, far, other, *refs):
    @on_level(0)
    def _():
        put([here], [far], [0], *refs[-2:])

    @off_level(0)
    def _():
        put([here], [other], [0], *refs[-2:])


def run(kernel, operands, outs, aliases=None, flops=10**9, whole=None, scratch=(), raw=()):
    in_specs = [IN_HBM] * len(raw) + [IN_VMEM] * len(operands)
    operands = [*(pltpu.with_memory_space_constraint(value, pltpu.HBM) for value in raw), *(pltpu.with_memory_space_constraint(value, pltpu.VMEM) for value in operands)]
    out_specs = [IN_VMEM] * len(outs)
    out_shape = [pltpu.VMEM(out.shape, out.dtype) for out in outs]
    aliases = dict(aliases or {})
    if whole is not None:
        shape, before = whole
        if before is not None:
            aliases[len(operands)] = len(outs)
            operands.append(before)
            in_specs.append(IN_ANY)
        out_shape.append(shape)
        out_specs.append(IN_ANY)
    return pl.pallas_call(
        kernel,
        in_specs=in_specs,
        out_specs=out_specs,
        out_shape=out_shape,
        input_output_aliases=aliases,
        scratch_shapes=scratch,
        compiler_params=pltpu.CompilerParams(vmem_limit_bytes=SMALL_VMEM_BYTES),
        cost_estimate=pl.CostEstimate(
            flops=flops, bytes_accessed=10**6, transcendentals=0
        ),
    )(*operands)


def exchanged(value):
    return lax.ppermute(value, SUB, [(0, 1), (1, 0)])


def pair_body(rhs, lower_inv, lower_off, upper_inv, upper_off, ancestor, parent):
    levels = lax.axis_size(LEVEL)
    top = levels - 1
    rhs, lower_inv, lower_off, upper_inv, upper_off = (
        value[0] for value in (rhs, lower_inv, lower_off, upper_inv, upper_off)
    )
    count, all_rows, width = rhs.shape
    half = all_rows // 2
    chunks = half // NODE_ROWS
    nodes = 2 * count
    size = nodes * NODE_ROWS

    def shape(of, dtype):
        return jax.ShapeDtypeStruct((of, NODE_ROWS, width), dtype)

    def passed(value, pairs, cross=False):
        sources = [i for i in range(levels) if i not in dict(pairs)]
        targets = [i for i in range(levels) if i not in [to for _, to in pairs]]
        fill = min(
            (list(zip(sources, order)) for order in itertools.permutations(targets)),
            key=lambda extra: (sum(a == b for a, b in extra), sum(abs(a - b) for a, b in extra)),
        )
        if cross:
            pairs = [(2 * a + s, 2 * b + 1 - s) for a, b in pairs + fill for s in range(2)]
            return lax.ppermute(value, (LEVEL, SUB), pairs)
        return lax.ppermute(value, LEVEL, pairs + fill)

    def after(value, *earlier):
        return lax.optimization_barrier((value, *earlier))[0]

    matrices = jax.ShapeDtypeStruct(lower_inv.shape, BF16)
    table = jax.ShapeDtypeStruct((size, size), BF16)
    half_shape = jax.ShapeDtypeStruct((count, half, width), F32)
    block = pltpu.VMEM(lower_inv.shape, BF16)
    state = {"nodes": nodes}
    select, choose, rhs_own, rhs_sent, home, swap_first, swap_rest, up_own, *updates = run(
        start_kernel, (),
        [table, table, half_shape, half_shape, shape(chunks * nodes, F32)] + [shape(chunks // 2 * nodes, BF16)] * 2 + [matrices]
        + [shape(count, F32)] * (2 * chunks),
        raw=(parent, rhs, lower_inv, lower_off),
        scratch=[pltpu.VMEM(parent.shape, parent.dtype), block, block, pltpu.SemaphoreType.DMA((3, max(count // LOAD_NODES, 3)))],
    )
    state.update(select=select, choose=choose, rhs_own=rhs_own, home=home, up_own=up_own)
    swapped = [exchanged(swap_first), exchanged(swap_rest)]
    for c in range(chunks):
        state["own", c], state["far", c] = updates[c], updates[chunks + c]

    packed_shape = (2 * count + count * half // width, width, width)
    merge_scratch = [block, block, block, pltpu.VMEM((count, half, width), BF16), pltpu.SemaphoreType.DMA((4, count // LOAD_NODES))]

    def merged(sent):
        low, *others = lax.optimization_barrier((lower_inv, upper_inv, upper_off, ancestor, sent))
        return run(
            merge_kernel, (), [jax.ShapeDtypeStruct(packed_shape, BF16)],
            raw=(low, *others[:3]), scratch=merge_scratch,
        )[0]

    whole = jax.ShapeDtypeStruct(rhs.shape, F32)

    def sems(pieces):
        return [pltpu.SemaphoreType.DMA((2, pieces))]

    def placed(group, before, *earlier):
        first = after(state["sol_own", group[0]], *earlier) if earlier else state["sol_own", group[0]]
        return run(
            functools.partial(place_kernel, [NODE_ROWS * c for c in group]),
            [first, *(state["sol_own", c] for c in group[1:]), *(other[c] for c in group)],
            [], whole=(whole, before), scratch=sems(len(group)),
        )[0]

    pipes = [list(range(chunks))[i : i + 2] for i in range(0, chunks, 2)]
    received = [None] * len(pipes)
    other = [None] * chunks
    pace = []
    last = 2 * top + 1
    for k in range(last + 1):
        for p, pipe in enumerate(pipes):
            plan, pairs = [], []
            for j, c in enumerate(pipe):
                tier = k - j
                if 0 <= tier < top:
                    plan.append((tier, "sum" if tier == 0 else "tier", c))
                    pairs.append((tier, tier + 1))
                elif tier == top:
                    plan.append((top, "top", c))
                    pairs.append((top, top - 1))
                elif top < tier <= 2 * top:
                    low = 2 * top - tier
                    plan.append((low, "back", c))
                    if low:
                        pairs.append((low, low - 1))
            if k < len(pipe):
                state["swapped"] = swapped[k]
            if received[p] is not None:
                state["received"] = after(received[p], *pace)
            split = k == last - 1 and p == len(pipes) - 1
            if k == last and p == len(pipes) - 1:
                state[CROSS], state[OTHER, pipe[-1]] = cross, other[pipe[-1]]
                plan = [(0, LAST, pipe[-1])]
            sent, *sent_cross = step(plan, state, 2 if split else bool(pairs), COSTS[k]) or [None]
            if k == last and p == len(pipes) - 1:
                other[pipe[-1]] = state[OTHER, pipe[-1]]
            elif k == last:
                other[pipe[-1]] = exchanged(state["sol_far", pipe[-1]])
            if split:
                cross = passed(sent_cross[0], pairs, cross=True)
                other[pipe[-1]] = exchanged(state["sol_far", pipe[-1]])
            pace = [sent] if pairs else [state["sol_own", pipe[-1]]]
            if pairs:
                received[p] = passed(sent, pairs)
            if p == 0 and k == 0:
                state["up_far"] = exchanged(after(up_own, sent))
                state["rhs_far"] = exchanged(after(rhs_sent, sent))
            if p == 0 and k == 1:
                state["down_far"] = exchanged(state["down_own"])
            if p == 0 and k == last:
                (update,) = run(
                    place_bottom_kernel, (upd_own, after(upd_far, *pace), upd_other), [], whole=(whole, None), scratch=sems(1)
                )
                early = [pipe[0] for pipe in pipes]
                other[early[0]], other[early[1]] = (exchanged(state["sol_far", c]) for c in early)
                solved = placed(early, None, update)
                pace = [solved]
        if k == 0:
            state["down_own"] = merged(sent)
            pace.append(state["down_own"])
        if k == top - 1:
            bases = run(
                functools.partial(ancestor_kernel, top),
                (state["down_own"], state["down_far"]),
                [shape(nodes, F32)] * chunks,
                raw=(after(ancestor, sent),),
                scratch=[pltpu.VMEM((count, half, width), BF16), pltpu.SemaphoreType.DMA((1,))],
            )
            state.update({("top_base", c): bases[c] for c in range(chunks)})
            pace += bases
        residues = [state["residue", c] for c in range(chunks)] if k >= top else []
        if k == top:
            *bases, state[BELOW] = run(
                base_kernel,
                (after(rhs_own, sent), state["rhs_far"], rhs_sent, state["down_own"], state["down_far"], *residues),
                [shape(nodes, F32)] * chunks + [shape(count, F32)],
            )
            state.update({("low_base", c): bases[c] for c in range(chunks)})
            pace += bases
        if k == top + 2:
            upd_own, upd_far = run(
                update_kernel,
                (up_own, state["up_far"], *residues, *(state["own", c] for c in range(chunks)), *(state["far", c] for c in range(chunks))),
                [half_shape] * 2,
            )
            upd_other = exchanged(upd_far)
    solved = placed([pipe[-1] for pipe in pipes], solved)
    return solved[None], update[None]


def solution(mesh):
    placed = (
        P(LEVEL, SUB, "rhs", None),
        P(LEVEL, SUB, None, None),
        P(LEVEL, SUB, None, None),
        P(LEVEL, SUB, None, None),
        P(LEVEL, SUB, None, None),
        P(SUB, "rhs", None),
        P(),
    )
    return jax.shard_map(
        pair_body if mesh.shape[SUB] == 2 else general_body,
        mesh=mesh,
        in_specs=placed,
        out_specs=(P(LEVEL, SUB, "rhs", None), P(LEVEL, SUB, "rhs", None)),
        check_vma=False,
    )
```

```python
import functools
import itertools

import jax
import jax.numpy as jnp
from jax import lax
from jax.experimental import pallas as pl
from jax.experimental.pallas import tpu as pltpu
from jax.sharding import PartitionSpec as P

CHUNKS = 2
LOCAL_SWAP = False
VMEM_BYTES = 24 * 2**20

LEVEL, SUB = "level", "sub"
BF16 = jnp.bfloat16
F32 = jnp.float32
IN_VMEM = pl.BlockSpec(memory_space=pltpu.VMEM)
IN_SMEM = pl.BlockSpec(memory_space=pltpu.SMEM)


def dot(left, right):
    return jnp.dot(left, right, preferred_element_type=F32)


def forward_kernel(section, start, rows, info, rhs, incoming, inv, off, kept_f, kept_u, fwd, upd, home, far, total):
    count = inv.shape[0]

    @pl.when(info[count] != section)
    def _():
        fwd[...] = kept_f[...]
        upd[...] = kept_u[...]

    @pl.when(info[count] == section)
    def _():
        total[...] = jnp.zeros_like(total)
        for node in range(count):
            right_side = rhs[node, pl.ds(start, rows), :]
            if incoming is not None:
                right_side = right_side - incoming[node].astype(F32)
            forward = dot(right_side.astype(BF16), inv[node]).astype(BF16)
            fwd[node] = forward
            update = dot(forward, off[node])
            upd[node] = update
            total[info[node]] += update
        home[...] = total[:count]
        far[...] = total[count:].astype(BF16)


def first_kernel(section, start, rows, info, rhs, inv, off, kept_f, kept_u, fwd, upd, home, far, total):
    forward_kernel(section, start, rows, info, rhs, None, inv, off, kept_f, kept_u, fwd, upd, home, far, total)


def top_kernel(section, start, rows, info, rhs, incoming, inv, up_off, up_inv, ancestor, kept_f, kept_s, fwd, sol, sol_bf):
    count = inv.shape[0]

    @pl.when(info[count] != section)
    def _():
        fwd[...] = kept_f[...]
        sol[...] = kept_s[...]

    @pl.when(info[count] == section)
    def _():
        for node in range(count):
            right_side = rhs[node, pl.ds(start, rows), :] - incoming[node].astype(F32)
            forward = dot(right_side.astype(BF16), inv[node]).astype(BF16)
            fwd[node] = forward
            above = dot(ancestor[node, pl.ds(start, rows), :], up_off[node])
            reduced = (forward.astype(F32) - above).astype(BF16)
            solved = dot(reduced, up_inv[node])
            sol[node] = solved
            sol_bf[node] = solved.astype(BF16)


def top_update_kernel(section, start, rows, info, fwd, off, kept_u, upd):
    count = off.shape[0]

    @pl.when(info[count] != section)
    def _():
        upd[...] = kept_u[...]

    @pl.when(info[count] == section)
    def _():
        for node in range(count):
            upd[node] = dot(fwd[node], off[node])


def backward_kernel(section, start, rows, info, fwd, own, partner, up_off, up_inv, kept_s, sol, sol_bf):
    count = up_inv.shape[0]

    @pl.when(info[count] != section)
    def _():
        sol[...] = kept_s[...]

    @pl.when(info[count] == section)
    def _():
        for node in range(count):
            place = info[node]
            at_home = place < count
            slot = jnp.where(at_home, place, place - count)
            above = jnp.where(at_home, own[slot], partner[slot])
            reduced = (fwd[node].astype(F32) - dot(above, up_off[node])).astype(BF16)
            solved = dot(reduced, up_inv[node])
            sol[node] = solved
            sol_bf[node] = solved.astype(BF16)


def call(kernel, section, start, rows, operands, outs, aliases, scratch=(), products=2):
    count = operands[1].shape[0]
    return pl.pallas_call(
        functools.partial(kernel, section, start, rows),
        in_specs=[IN_SMEM] + [IN_VMEM] * (len(operands) - 1),
        out_specs=[IN_VMEM] * len(outs),
        out_shape=outs,
        scratch_shapes=scratch,
        input_output_aliases=aliases,
        compiler_params=pltpu.CompilerParams(vmem_limit_bytes=VMEM_BYTES),
        cost_estimate=pl.CostEstimate(
            flops=products * 2 * count * rows * 256 * 256, bytes_accessed=count * 256 * 256 * 2 * products, transcendentals=0
        ),
    )(*operands)


def swapped(value, section, apart):
    mask = 2**apart
    subs = lax.axis_size(SUB)
    if not LOCAL_SWAP:
        return lax.ppermute(value, SUB, [(i, i ^ mask) for i in range(subs)])
    pairs = [(section * subs + i, section * subs + (i ^ mask)) for i in range(subs)]
    return lax.ppermute(value, (LEVEL, SUB), pairs)


def general_body(rhs, lower_inv, lower_off, upper_inv, upper_off, ancestor, parent):
    levels = lax.axis_size(LEVEL)
    sub_count = lax.axis_size(SUB)
    sub_bits = sub_count.bit_length() - 1
    tier = lax.axis_index(LEVEL)
    sub = lax.axis_index(SUB)
    rhs, lower_inv, lower_off, upper_inv, upper_off = (
        value[0] for value in (rhs, lower_inv, lower_off, upper_inv, upper_off)
    )
    count, all_rows, width = rhs.shape
    rows = all_rows // CHUNKS
    parent_row = lax.dynamic_index_in_dim(parent, jnp.minimum(tier, levels - 2), 0, keepdims=False)
    parent_here = lax.dynamic_slice_in_dim(parent_row, sub * count, count)
    place = parent_here % count + jnp.where(parent_here // count == sub, 0, count)
    info = jnp.concatenate([place, tier[None]]).astype(jnp.int32)

    def shape(dtype):
        return jax.ShapeDtypeStruct((count, rows, width), dtype)

    fwd = [jnp.zeros((count, rows, width), BF16) for _ in range(CHUNKS)]
    upd = [jnp.zeros((count, rows, width), F32) for _ in range(CHUNKS)]
    sol = [jnp.zeros((count, rows, width), F32) for _ in range(CHUNKS)]
    incoming = [None] * CHUNKS
    above = [None] * CHUNKS
    top = levels - 1
    for section in range(top):
        for c in range(CHUNKS):
            if section == 0:
                kernel, operands = first_kernel, (info, rhs, lower_inv, lower_off, fwd[c], upd[c])
            else:
                kernel, operands = forward_kernel, (info, rhs, incoming[c], lower_inv, lower_off, fwd[c], upd[c])
            at = len(operands) - 2
            fwd[c], upd[c], home, far = call(
                kernel, section, c * rows, rows, operands,
                [shape(BF16), shape(F32), shape(F32), shape(BF16)], {at: 0, at + 1: 1},
                [pltpu.VMEM((2 * count, rows, width), F32)],
            )
            received = swapped(far, section, section % sub_bits)
            summed = (home + received.astype(F32)).astype(BF16)
            incoming[c] = lax.ppermute(summed, LEVEL, [(section, section + 1)])
    for c in range(CHUNKS):
        fwd[c], sol[c], solved = call(
            top_kernel, top, c * rows, rows,
            (info, rhs, incoming[c], lower_inv, upper_off, upper_inv, ancestor, fwd[c], sol[c]),
            [shape(BF16), shape(F32), shape(BF16)], {7: 0, 8: 1}, products=3,
        )
        above[c] = lax.ppermute(solved, LEVEL, [(top, top - 1)])
    for c in range(CHUNKS):
        (upd[c],) = call(top_update_kernel, top, c * rows, rows, (info, fwd[c], lower_off, upd[c]), [shape(F32)], {3: 0}, products=1)
    for section in reversed(range(top)):
        for c in range(CHUNKS):
            partner = swapped(above[c], section, section % sub_bits)
            sol[c], solved = call(
                backward_kernel, section, c * rows, rows,
                (info, fwd[c], above[c], partner, upper_off, upper_inv, sol[c]),
                [shape(F32), shape(BF16)], {6: 0},
            )
            if section:
                above[c] = lax.ppermute(solved, LEVEL, [(section, section - 1)])
    return jnp.concatenate(sol, axis=1)[None], jnp.concatenate(upd, axis=1)[None]


NODE_ROWS = 8
CROSS, OTHER, BELOW, LAST = "c", "o", "b", "l"
LOAD_NODES = 4
COSTS = [30000000000, 30000000000, 30000000000, 5000000000, 5000000000, 5000000000, 5000000000, 5000000000]
SMALL_VMEM_BYTES = 12 * 2**20
IN_ANY = pl.BlockSpec(memory_space=pl.ANY)
IN_HBM = pl.BlockSpec(memory_space=pltpu.HBM)


def rows_of(start):
    return pl.ds(pl.multiple_of(start, NODE_ROWS), NODE_ROWS)


def half_rows(array, sub):
    half = array.shape[1] // 2
    return pl.ds(pl.multiple_of(half * sub, half), half)


def flat(value):
    return value.reshape(value.shape[0] * value.shape[1], value.shape[2])


def pick(select, values):
    return dot(select, values.astype(BF16))


def on_level(section):
    return pl.when(lax.axis_index(LEVEL) == section)


def off_level(section):
    return pl.when(lax.axis_index(LEVEL) != section)


def keep(section, kept, outs):
    @off_level(section)
    def _():
        for before, after in zip(kept, outs):
            after[...] = before[...]


def fill_tables(parent, select, choose):
    nodes = parent.shape[1]
    size = nodes * NODE_ROWS
    top = lax.axis_size(LEVEL) - 1
    level, shift = lax.axis_index(LEVEL), lax.axis_index(SUB) * (nodes // 2)

    def target(row, axis):
        shape = (nodes, size) if axis else (size, nodes)
        child = lax.broadcasted_iota(jnp.int32, shape, axis) // NODE_ROWS + shift
        child = jnp.where(child >= nodes, child - nodes, child)
        same = child == lax.broadcasted_iota(jnp.int32, shape, 1 - axis)
        row = row - shift
        row = jnp.where(row < 0, row + nodes, row)
        if axis:
            found = dot(row.astype(F32).astype(BF16), same.astype(F32).astype(BF16))
        else:
            found = jnp.sum(jnp.where(same, row.astype(F32), 0.0), axis=1, keepdims=True)
        place = lax.broadcasted_iota(jnp.int32, found.shape, axis)
        return found.astype(jnp.int32) * NODE_ROWS + lax.rem(place, NODE_ROWS)

    up = target(parent[pl.ds(jnp.minimum(level, top - 1), 1), :], 1)
    down = target(parent[pl.ds(jnp.maximum(level - 1, 0), 1), :], 0)
    index = lax.broadcasted_iota(jnp.int32, (size, size), 0)
    select[...] = (index == up).astype(F32).astype(BF16)
    index = lax.broadcasted_iota(jnp.int32, (size, size), 1)
    choose[...] = (index == down).astype(F32).astype(BF16)


def start_kernel(parent, rhs, inv, off, select, choose, rhs_own, rhs_sent, home, swap_first, swap_rest, merged, *refs):
    *updates, parent_here, inv_here, off_here, sems = refs
    count = inv.shape[0]
    chunks = len(updates) // 2
    size = count * NODE_ROWS
    level, sub = lax.axis_index(LEVEL), lax.axis_index(SUB)
    table = pltpu.make_async_copy(parent, parent_here, sems.at[0, 0])
    mine = pltpu.make_async_copy(rhs.at[:, half_rows(rhs, sub), :], rhs_own, sems.at[0, 1])
    other = pltpu.make_async_copy(rhs.at[:, half_rows(rhs, 1 - sub), :], rhs_sent, sems.at[0, 2])
    table.start()
    loads = []
    for group in range(count // LOAD_NODES):
        here = pl.ds(group * LOAD_NODES, LOAD_NODES)
        loads.append(pltpu.make_async_copy(inv.at[here], inv_here.at[here], sems.at[1, group]))
        loads.append(pltpu.make_async_copy(off.at[here], off_here.at[here], sems.at[2, group]))
        loads[-2].start()
        loads[-1].start()
        if group == 0:
            mine.start()
            other.start()
    table.wait()
    fill_tables(parent_here, select, choose)
    mine.wait()
    other.wait()

    @on_level(0)
    def _():
        for node in range(count):
            if node % LOAD_NODES == 0:
                loads[2 * (node // LOAD_NODES)].wait()
                loads[2 * (node // LOAD_NODES) + 1].wait()
            right_side = jnp.concatenate([rhs_own[node], rhs_sent[node]], axis=0).astype(BF16)
            forward = dot(right_side, inv_here[node]).astype(BF16)
            update = dot(forward, off_here[node])
            for c in range(2 * chunks):
                updates[c][node] = update[NODE_ROWS * c : NODE_ROWS * (c + 1)]
        chosen = select[:, :size]
        for c in range(chunks):
            home[2 * count * c : 2 * count * (c + 1)] = pick(chosen, flat(updates[c][...])).reshape(2 * count, *home.shape[1:])
            sums = pick(chosen, flat(updates[chunks + c][...])).reshape(2 * count, *home.shape[1:]).astype(BF16)
            swap, at = (swap_first, swap_rest)[c % 2], 2 * count * (c // 2)
            swap[at : at + count] = sums[count:]
            swap[at + count : at + 2 * count] = sums[:count]

    @off_level(0)
    def _():
        for node in range(count):
            if node % LOAD_NODES == 0:
                loads[2 * (node // LOAD_NODES)].wait()
                loads[2 * (node // LOAD_NODES) + 1].wait()
            merged[node] = dot(inv_here[node], off_here[node]).astype(BF16)


def merge_kernel(low_inv, up_inv, up_off, ancestor, packed, *scratch):
    low_here, up_here, off_here, rows, sems = scratch
    count = low_inv.shape[0]
    sub = lax.axis_index(SUB)
    loads = []
    for group in range(count // LOAD_NODES):
        here = pl.ds(group * LOAD_NODES, LOAD_NODES)
        loads.append(pltpu.make_async_copy(up_inv.at[here], up_here.at[here], sems.at[1, group]))
        loads.append(pltpu.make_async_copy(low_inv.at[here], low_here.at[here], sems.at[0, group]))
        loads.append(pltpu.make_async_copy(up_off.at[here], off_here.at[here], sems.at[2, group]))
    loads.append(pltpu.make_async_copy(ancestor.at[:, half_rows(ancestor, 1 - sub), :], rows, sems.at[3, 0]))
    for load in loads:
        load.start()
    for node in range(count):
        if node % LOAD_NODES == 0:
            for load in loads[3 * (node // LOAD_NODES) : 3 * (node // LOAD_NODES) + 3]:
                load.wait()
        packed[node] = dot(low_here[node], up_here[node]).astype(BF16)
        packed[count + node] = dot(off_here[node], up_here[node]).astype(BF16)
    loads[-1].wait()
    packed[2 * count :] = rows[...].reshape(packed.shape[0] - 2 * count, *packed.shape[1:])


def residue_of(c, rhs_own, rhs_far, incoming, node):
    count = rhs_own.shape[0]
    rows = slice(NODE_ROWS * c, NODE_ROWS * (c + 1))
    right_side = rhs_own[node, rows, :] if node < count else rhs_far[node - count, rows, :]
    return (right_side - incoming[node].astype(F32)).astype(BF16)


def tier_role(c, at):
    count = at["rhs_own"].shape[0]
    own, far = at["own", c], at["far", c]
    for node in range(2 * count):
        value = residue_of(c, at["rhs_own"], at["rhs_far"], at["received"], node)
        at["residue", c][node] = value.astype(F32)
        if node < count:
            own[node] = dot(value, at["up_own"][node])
        else:
            far[node - count] = dot(value, at["up_far"][node - count])
    updates = jnp.concatenate([flat(own[...]), flat(far[...])], axis=0)
    at["sent"][...] = pick(at["select"][...], updates).reshape(at["sent"].shape).astype(BF16)


def send_solved(c, at):
    if "sent" in at:
        solved = jnp.concatenate([flat(at["sol_own", c][...]), flat(at["sol_far", c][...])], axis=0).astype(BF16)
        rows = dot(at["choose"][...], solved)
        rows = rows.reshape(rows.shape[0] // NODE_ROWS, NODE_ROWS, rows.shape[1]).astype(BF16)
        at["sent"][...] = rows[: at["sent"].shape[0]]
        if CROSS in at:
            at[CROSS][...] = rows[at["sent"].shape[0] :]


def top_role(c, at):
    count = at["rhs_own"].shape[0]
    base = at["top_base", c]
    for node in range(2 * count):
        value = residue_of(c, at["rhs_own"], at["rhs_far"], at["received"], node)
        at["residue", c][node] = value.astype(F32)
        if node < count:
            at["sol_own", c][node] = dot(value, at["down_own"][node]) - base[node]
        else:
            at["sol_far", c][node - count] = dot(value, at["down_far"][node - count]) - base[node]
    send_solved(c, at)


def back_role(c, at):
    count = at["sol_own", c].shape[0]
    base, above = at["low_base", c], at["received"]
    for node in range(count):
        at["sol_own", c][node] = base[node] - dot(above[node], at["down_own"][count + node])
        at["sol_far", c][node] = base[count + node] - dot(above[count + node], at["down_far"][count + node])
    send_solved(c, at)


def last_role(c, at):
    count = at["sol_own", c].shape[0]
    for node in range(count):
        above = jnp.concatenate([at["received"][node].astype(F32), at[CROSS][node].astype(F32)], axis=0)
        solved = dot(above.astype(BF16), at["down_own"][count + node])
        at["sol_own", c][node] = at["low_base", c][node] - solved[:NODE_ROWS]
        at[OTHER, c][node] = at[BELOW][node] - solved[NODE_ROWS:]


def sum_role(c, at):
    nodes = at["sent"].shape[0]
    home = at["home"][c * nodes : (c + 1) * nodes]
    partner = at["swapped"][c // 2 * nodes : (c // 2 + 1) * nodes]
    at["sent"][...] = (home + partner.astype(F32)).astype(BF16)


ROLES = {"tier": tier_role, "top": top_role, "back": back_role, LAST: last_role, "sum": sum_role}
READS = {
    "tier": ("rhs_own", "rhs_far", "received", "up_own", "up_far", "select"),
    "top": ("rhs_own", "rhs_far", "received", "down_own", "down_far", "choose", "top_base"),
    "back": ("received", "down_own", "down_far", "choose", "low_base"),
    LAST: ("received", CROSS, "down_own", "low_base", BELOW),
    "sum": ("home", "swapped"),
}
WRITES = {
    "tier": ("residue", "own", "far"),
    "top": ("residue", "sol_own", "sol_far"),
    "back": ("sol_own", "sol_far"),
    LAST: ("sol_own", OTHER),
    "sum": (),
}


def step_kernel(plan, in_keys, out_keys, kept_keys, *refs):
    reads = dict(zip(in_keys, refs))
    kept = dict(zip(kept_keys, refs[len(in_keys) :]))
    outs = dict(zip(out_keys, refs[len(in_keys) + len(kept_keys) :]))
    for level, role, c in plan:
        writes = [(name, c) for name in WRITES[role]]
        keep(level, [kept[key] for key in writes if key in kept], [outs[key] for key in writes if key in kept])
        pl.when(lax.axis_index(LEVEL) == level)(functools.partial(ROLES[role], c, {**reads, **outs}))


def step(plan, state, sends=1, flops=10**9):
    nodes = state["nodes"]
    in_keys, out_keys = [], []
    for _, role, c in plan:
        for name in READS[role]:
            key = (name, c) if name.endswith("_base") else name
            if key not in in_keys:
                in_keys.append(key)
        out_keys += [(name, c) for name in WRITES[role]]
    kept_keys = [key for key in out_keys if key in state]
    width = state["rhs_own"].shape[2]
    outs = []
    for name, _ in out_keys:
        of = nodes if name == "residue" else nodes // 2
        outs.append(jax.ShapeDtypeStruct((of, NODE_ROWS, width), F32))
    aliases = {len(in_keys) + i: out_keys.index(key) for i, key in enumerate(kept_keys)}
    all_outs = out_keys + ["sent", CROSS][:sends]
    outs += [jax.ShapeDtypeStruct((nodes // max(sends, 1), NODE_ROWS, width), BF16)] * sends
    operands = [state[key] for key in in_keys + kept_keys]
    results = run(functools.partial(step_kernel, plan, in_keys, all_outs, kept_keys), operands, outs, aliases, flops)
    state.update(zip(out_keys, results))
    return results[len(out_keys) :]


def rows_together(chunks, node):
    return jnp.concatenate([chunk[node] for chunk in chunks], axis=0).astype(BF16)


def apart(value, chunks, node):
    for c, chunk in enumerate(chunks):
        chunk[node] = value[NODE_ROWS * c : NODE_ROWS * (c + 1)]


def base_kernel(rhs_own, rhs_far, rhs_sent, own, far, *refs):
    *refs, below = refs
    residue, base = refs[: len(refs) // 2], refs[len(refs) // 2 :]
    count = rhs_own.shape[0]
    level, top = lax.axis_index(LEVEL), lax.axis_size(LEVEL) - 1

    @pl.when(level == 0)
    def _():
        for node in range(count):
            both = jnp.concatenate([rhs_own[node], rhs_sent[node, -NODE_ROWS:, :]], axis=0).astype(BF16)
            solved = dot(both, own[node])
            apart(solved, base, node)
            below[node] = solved[-NODE_ROWS:]
            apart(dot(rhs_far[node].astype(BF16), far[node]), base, count + node)

    @pl.when((level != 0) & (level != top))
    def _():
        for node in range(count):
            apart(dot(rows_together(residue, node), own[node]), base, node)
            apart(dot(rows_together(residue, count + node), far[node]), base, count + node)


def update_kernel(up_own, up_far, *refs):
    chunks = (len(refs) - 2) // 3
    residue, own_kept, far_kept = (refs[chunks * i : chunks * (i + 1)] for i in range(3))
    upd_own, upd_far = refs[-2:]
    level, top = lax.axis_index(LEVEL), lax.axis_size(LEVEL) - 1

    @pl.when(level == top)
    def _():
        count = up_own.shape[0]
        for node in range(count):
            upd_own[node] = dot(rows_together(residue, node), up_own[node])
            upd_far[node] = dot(rows_together(residue, count + node), up_far[node])

    @pl.when(level != top)
    def _():
        for c in range(chunks):
            rows = slice(NODE_ROWS * c, NODE_ROWS * (c + 1))
            upd_own[:, rows, :] = own_kept[c][...]
            upd_far[:, rows, :] = far_kept[c][...]


def ancestor_kernel(section, ancestor, own, far, *refs):
    *bases, here, sem = refs
    count, half, _ = here.shape
    sub = lax.axis_index(SUB)

    @on_level(section)
    def _():
        load = pltpu.make_async_copy(ancestor.at[:, half_rows(ancestor, sub), :], here, sem.at[0])
        load.start()
        load.wait()
        for node in range(count):
            per = far.shape[1] // half
            other = far[2 * count + node // per, half * (node % per) : half * (node % per + 1), :]
            mine = dot(here[node], own[count + node])
            other = dot(other, far[count + node])
            for c, base in enumerate(bases):
                base[node] = mine[NODE_ROWS * c : NODE_ROWS * (c + 1)]
                base[count + node] = other[NODE_ROWS * c : NODE_ROWS * (c + 1)]


def put(here, other, first, out, sems):
    sub = lax.axis_index(SUB)
    half = out.shape[1] // 2
    copies = []
    for i, (mine, theirs, row) in enumerate(zip(here, other, first)):
        size = mine.shape[1]
        to_mine = pl.ds(pl.multiple_of(half * sub + row, NODE_ROWS), size)
        to_theirs = pl.ds(pl.multiple_of(half * (1 - sub) + row, NODE_ROWS), size)
        copies.append(pltpu.make_async_copy(mine, out.at[:, to_mine, :], sems.at[0, i]))
        copies.append(pltpu.make_async_copy(theirs, out.at[:, to_theirs, :], sems.at[1, i]))
    for copy in copies:
        copy.start()
    for copy in copies:
        copy.wait()


def place_kernel(first, *refs):
    count = len(first)
    put(refs[:count], refs[count : 2 * count], first, *refs[-2:])


def place_bottom_kernel(here, far, other, *refs):
    @on_level(0)
    def _():
        put([here], [far], [0], *refs[-2:])

    @off_level(0)
    def _():
        put([here], [other], [0], *refs[-2:])


def run(kernel, operands, outs, aliases=None, flops=10**9, whole=None, scratch=(), raw=()):
    in_specs = [IN_HBM] * len(raw) + [IN_VMEM] * len(operands)
    operands = [*(pltpu.with_memory_space_constraint(value, pltpu.HBM) for value in raw), *(pltpu.with_memory_space_constraint(value, pltpu.VMEM) for value in operands)]
    out_specs = [IN_VMEM] * len(outs)
    out_shape = [pltpu.VMEM(out.shape, out.dtype) for out in outs]
    aliases = dict(aliases or {})
    if whole is not None:
        shape, before = whole
        if before is not None:
            aliases[len(operands)] = len(outs)
            operands.append(before)
            in_specs.append(IN_ANY)
        out_shape.append(shape)
        out_specs.append(IN_ANY)
    return pl.pallas_call(
        kernel,
        in_specs=in_specs,
        out_specs=out_specs,
        out_shape=out_shape,
        input_output_aliases=aliases,
        scratch_shapes=scratch,
        compiler_params=pltpu.CompilerParams(vmem_limit_bytes=SMALL_VMEM_BYTES),
        cost_estimate=pl.CostEstimate(
            flops=flops, bytes_accessed=10**6, transcendentals=0
        ),
    )(*operands)


def exchanged(value):
    return lax.ppermute(value, SUB, [(0, 1), (1, 0)])


def pair_body(rhs, lower_inv, lower_off, upper_inv, upper_off, ancestor, parent):
    levels = lax.axis_size(LEVEL)
    top = levels - 1
    rhs, lower_inv, lower_off, upper_inv, upper_off = (
        value[0] for value in (rhs, lower_inv, lower_off, upper_inv, upper_off)
    )
    count, all_rows, width = rhs.shape
    half = all_rows // 2
    chunks = half // NODE_ROWS
    nodes = 2 * count
    size = nodes * NODE_ROWS

    def shape(of, dtype):
        return jax.ShapeDtypeStruct((of, NODE_ROWS, width), dtype)

    def passed(value, pairs, cross=False):
        sources = [i for i in range(levels) if i not in dict(pairs)]
        targets = [i for i in range(levels) if i not in [to for _, to in pairs]]
        fill = min(
            (list(zip(sources, order)) for order in itertools.permutations(targets)),
            key=lambda extra: (sum(a == b for a, b in extra), sum((a ^ b) == levels - 1 for a, b in extra), sum((b, a) in pairs + extra for a, b in extra)),
        )
        if cross:
            pairs = [(2 * a + s, 2 * b + 1 - s) for a, b in pairs + fill for s in range(2)]
            return lax.ppermute(value, (LEVEL, SUB), pairs)
        return lax.ppermute(value, LEVEL, pairs + fill)

    def after(value, *earlier):
        return lax.optimization_barrier((value, *earlier))[0]

    matrices = jax.ShapeDtypeStruct(lower_inv.shape, BF16)
    table = jax.ShapeDtypeStruct((size, size), BF16)
    half_shape = jax.ShapeDtypeStruct((count, half, width), F32)
    block = pltpu.VMEM(lower_inv.shape, BF16)
    state = {"nodes": nodes}
    select, choose, rhs_own, rhs_sent, home, swap_first, swap_rest, up_own, *updates = run(
        start_kernel, (),
        [table, table, half_shape, half_shape, shape(chunks * nodes, F32)] + [shape(chunks // 2 * nodes, BF16)] * 2 + [matrices]
        + [shape(count, F32)] * (2 * chunks),
        raw=(parent, rhs, lower_inv, lower_off),
        scratch=[pltpu.VMEM(parent.shape, parent.dtype), block, block, pltpu.SemaphoreType.DMA((3, max(count // LOAD_NODES, 3)))],
    )
    state.update(select=select, choose=choose, rhs_own=rhs_own, home=home, up_own=up_own)
    swapped = [exchanged(swap_first), exchanged(swap_rest)]
    for c in range(chunks):
        state["own", c], state["far", c] = updates[c], updates[chunks + c]

    packed_shape = (2 * count + count * half // width, width, width)
    merge_scratch = [block, block, block, pltpu.VMEM((count, half, width), BF16), pltpu.SemaphoreType.DMA((4, count // LOAD_NODES))]

    def merged(sent):
        low, *others = lax.optimization_barrier((lower_inv, upper_inv, upper_off, ancestor, sent))
        return run(
            merge_kernel, (), [jax.ShapeDtypeStruct(packed_shape, BF16)],
            raw=(low, *others[:3]), scratch=merge_scratch,
        )[0]

    whole = jax.ShapeDtypeStruct(rhs.shape, F32)

    def sems(pieces):
        return [pltpu.SemaphoreType.DMA((2, pieces))]

    def placed(group, before, *earlier):
        first = after(state["sol_own", group[0]], *earlier) if earlier else state["sol_own", group[0]]
        return run(
            functools.partial(place_kernel, [NODE_ROWS * c for c in group]),
            [first, *(state["sol_own", c] for c in group[1:]), *(other[c] for c in group)],
            [], whole=(whole, before), scratch=sems(len(group)),
        )[0]

    pipes = [list(range(chunks))[i : i + 2] for i in range(0, chunks, 2)]
    received = [None] * len(pipes)
    other = [None] * chunks
    pace = []
    last = 2 * top + 1
    for k in range(last + 1):
        for p, pipe in enumerate(pipes):
            plan, pairs = [], []
            for j, c in enumerate(pipe):
                tier = k - j
                if 0 <= tier < top:
                    plan.append((tier, "sum" if tier == 0 else "tier", c))
                    pairs.append((tier, tier + 1))
                elif tier == top:
                    plan.append((top, "top", c))
                    pairs.append((top, top - 1))
                elif top < tier <= 2 * top:
                    low = 2 * top - tier
                    plan.append((low, "back", c))
                    if low:
                        pairs.append((low, low - 1))
            if k < len(pipe):
                state["swapped"] = swapped[k]
            if received[p] is not None:
                state["received"] = after(received[p], *pace)
            split = k == last - 1 and p == len(pipes) - 1
            if k == last and p == len(pipes) - 1:
                state[CROSS], state[OTHER, pipe[-1]] = cross, other[pipe[-1]]
                plan = [(0, LAST, pipe[-1])]
            sent, *sent_cross = step(plan, state, 2 if split else bool(pairs), COSTS[k]) or [None]
            if k == last and p == len(pipes) - 1:
                other[pipe[-1]] = state[OTHER, pipe[-1]]
            elif k == last:
                other[pipe[-1]] = exchanged(state["sol_far", pipe[-1]])
            if split:
                cross = passed(sent_cross[0], pairs, cross=True)
                other[pipe[-1]] = exchanged(state["sol_far", pipe[-1]])
            pace = [sent] if pairs else [state["sol_own", pipe[-1]]]
            if pairs:
                received[p] = passed(sent, pairs)
            if p == 0 and k == 0:
                state["up_far"] = exchanged(after(up_own, sent))
                state["rhs_far"] = exchanged(after(rhs_sent, sent))
            if p == 0 and k == 1:
                state["down_far"] = exchanged(state["down_own"])
            if p == 0 and k == last:
                (update,) = run(
                    place_bottom_kernel, (upd_own, after(upd_far, *pace), upd_other), [], whole=(whole, None), scratch=sems(1)
                )
                early = [pipe[0] for pipe in pipes]
                other[early[0]], other[early[1]] = (exchanged(state["sol_far", c]) for c in early)
                solved = placed(early, None, update)
                pace = [solved]
        if k == 0:
            state["down_own"] = merged(sent)
            pace.append(state["down_own"])
        if k == top - 1:
            bases = run(
                functools.partial(ancestor_kernel, top),
                (state["down_own"], state["down_far"]),
                [shape(nodes, F32)] * chunks,
                raw=(after(ancestor, sent),),
                scratch=[pltpu.VMEM((count, half, width), BF16), pltpu.SemaphoreType.DMA((1,))],
            )
            state.update({("top_base", c): bases[c] for c in range(chunks)})
            pace += bases
        residues = [state["residue", c] for c in range(chunks)] if k >= top else []
        if k == top:
            *bases, state[BELOW] = run(
                base_kernel,
                (after(rhs_own, sent), state["rhs_far"], rhs_sent, state["down_own"], state["down_far"], *residues),
                [shape(nodes, F32)] * chunks + [shape(count, F32)],
            )
            state.update({("low_base", c): bases[c] for c in range(chunks)})
            pace += bases
        if k == top + 2:
            upd_own, upd_far = run(
                update_kernel,
                (up_own, state["up_far"], *residues, *(state["own", c] for c in range(chunks)), *(state["far", c] for c in range(chunks))),
                [half_shape] * 2,
            )
            upd_other = exchanged(upd_far)
    solved = placed([pipe[-1] for pipe in pipes], solved)
    return solved[None], update[None]


def solution(mesh):
    placed = (
        P(LEVEL, SUB, "rhs", None),
        P(LEVEL, SUB, None, None),
        P(LEVEL, SUB, None, None),
        P(LEVEL, SUB, None, None),
        P(LEVEL, SUB, None, None),
        P(SUB, "rhs", None),
        P(),
    )
    return jax.shard_map(
        pair_body if mesh.shape[SUB] == 2 else general_body,
        mesh=mesh,
        in_specs=placed,
        out_specs=(P(LEVEL, SUB, "rhs", None), P(LEVEL, SUB, "rhs", None)),
        check_vma=False,
    )
```

```python
import functools
import itertools

import jax
import jax.numpy as jnp
from jax import lax
from jax.experimental import pallas as pl
from jax.experimental.pallas import tpu as pltpu
from jax.sharding import PartitionSpec as P

CHUNKS = 2
LOCAL_SWAP = False
VMEM_BYTES = 24 * 2**20

LEVEL, SUB = "level", "sub"
BF16 = jnp.bfloat16
F32 = jnp.float32
IN_VMEM = pl.BlockSpec(memory_space=pltpu.VMEM)
IN_SMEM = pl.BlockSpec(memory_space=pltpu.SMEM)


def dot(left, right):
    return jnp.dot(left, right, preferred_element_type=F32)


def forward_kernel(section, start, rows, info, rhs, incoming, inv, off, kept_f, kept_u, fwd, upd, home, far, total):
    count = inv.shape[0]

    @pl.when(info[count] != section)
    def _():
        fwd[...] = kept_f[...]
        upd[...] = kept_u[...]

    @pl.when(info[count] == section)
    def _():
        total[...] = jnp.zeros_like(total)
        for node in range(count):
            right_side = rhs[node, pl.ds(start, rows), :]
            if incoming is not None:
                right_side = right_side - incoming[node].astype(F32)
            forward = dot(right_side.astype(BF16), inv[node]).astype(BF16)
            fwd[node] = forward
            update = dot(forward, off[node])
            upd[node] = update
            total[info[node]] += update
        home[...] = total[:count]
        far[...] = total[count:].astype(BF16)


def first_kernel(section, start, rows, info, rhs, inv, off, kept_f, kept_u, fwd, upd, home, far, total):
    forward_kernel(section, start, rows, info, rhs, None, inv, off, kept_f, kept_u, fwd, upd, home, far, total)


def top_kernel(section, start, rows, info, rhs, incoming, inv, up_off, up_inv, ancestor, kept_f, kept_s, fwd, sol, sol_bf):
    count = inv.shape[0]

    @pl.when(info[count] != section)
    def _():
        fwd[...] = kept_f[...]
        sol[...] = kept_s[...]

    @pl.when(info[count] == section)
    def _():
        for node in range(count):
            right_side = rhs[node, pl.ds(start, rows), :] - incoming[node].astype(F32)
            forward = dot(right_side.astype(BF16), inv[node]).astype(BF16)
            fwd[node] = forward
            above = dot(ancestor[node, pl.ds(start, rows), :], up_off[node])
            reduced = (forward.astype(F32) - above).astype(BF16)
            solved = dot(reduced, up_inv[node])
            sol[node] = solved
            sol_bf[node] = solved.astype(BF16)


def top_update_kernel(section, start, rows, info, fwd, off, kept_u, upd):
    count = off.shape[0]

    @pl.when(info[count] != section)
    def _():
        upd[...] = kept_u[...]

    @pl.when(info[count] == section)
    def _():
        for node in range(count):
            upd[node] = dot(fwd[node], off[node])


def backward_kernel(section, start, rows, info, fwd, own, partner, up_off, up_inv, kept_s, sol, sol_bf):
    count = up_inv.shape[0]

    @pl.when(info[count] != section)
    def _():
        sol[...] = kept_s[...]

    @pl.when(info[count] == section)
    def _():
        for node in range(count):
            place = info[node]
            at_home = place < count
            slot = jnp.where(at_home, place, place - count)
            above = jnp.where(at_home, own[slot], partner[slot])
            reduced = (fwd[node].astype(F32) - dot(above, up_off[node])).astype(BF16)
            solved = dot(reduced, up_inv[node])
            sol[node] = solved
            sol_bf[node] = solved.astype(BF16)


def call(kernel, section, start, rows, operands, outs, aliases, scratch=(), products=2):
    count = operands[1].shape[0]
    return pl.pallas_call(
        functools.partial(kernel, section, start, rows),
        in_specs=[IN_SMEM] + [IN_VMEM] * (len(operands) - 1),
        out_specs=[IN_VMEM] * len(outs),
        out_shape=outs,
        scratch_shapes=scratch,
        input_output_aliases=aliases,
        compiler_params=pltpu.CompilerParams(vmem_limit_bytes=VMEM_BYTES),
        cost_estimate=pl.CostEstimate(
            flops=products * 2 * count * rows * 256 * 256, bytes_accessed=count * 256 * 256 * 2 * products, transcendentals=0
        ),
    )(*operands)


def swapped(value, section, apart):
    mask = 2**apart
    subs = lax.axis_size(SUB)
    if not LOCAL_SWAP:
        return lax.ppermute(value, SUB, [(i, i ^ mask) for i in range(subs)])
    pairs = [(section * subs + i, section * subs + (i ^ mask)) for i in range(subs)]
    return lax.ppermute(value, (LEVEL, SUB), pairs)


def general_body(rhs, lower_inv, lower_off, upper_inv, upper_off, ancestor, parent):
    levels = lax.axis_size(LEVEL)
    sub_count = lax.axis_size(SUB)
    sub_bits = sub_count.bit_length() - 1
    tier = lax.axis_index(LEVEL)
    sub = lax.axis_index(SUB)
    rhs, lower_inv, lower_off, upper_inv, upper_off = (
        value[0] for value in (rhs, lower_inv, lower_off, upper_inv, upper_off)
    )
    count, all_rows, width = rhs.shape
    rows = all_rows // CHUNKS
    parent_row = lax.dynamic_index_in_dim(parent, jnp.minimum(tier, levels - 2), 0, keepdims=False)
    parent_here = lax.dynamic_slice_in_dim(parent_row, sub * count, count)
    place = parent_here % count + jnp.where(parent_here // count == sub, 0, count)
    info = jnp.concatenate([place, tier[None]]).astype(jnp.int32)

    def shape(dtype):
        return jax.ShapeDtypeStruct((count, rows, width), dtype)

    fwd = [jnp.zeros((count, rows, width), BF16) for _ in range(CHUNKS)]
    upd = [jnp.zeros((count, rows, width), F32) for _ in range(CHUNKS)]
    sol = [jnp.zeros((count, rows, width), F32) for _ in range(CHUNKS)]
    incoming = [None] * CHUNKS
    above = [None] * CHUNKS
    top = levels - 1
    for section in range(top):
        for c in range(CHUNKS):
            if section == 0:
                kernel, operands = first_kernel, (info, rhs, lower_inv, lower_off, fwd[c], upd[c])
            else:
                kernel, operands = forward_kernel, (info, rhs, incoming[c], lower_inv, lower_off, fwd[c], upd[c])
            at = len(operands) - 2
            fwd[c], upd[c], home, far = call(
                kernel, section, c * rows, rows, operands,
                [shape(BF16), shape(F32), shape(F32), shape(BF16)], {at: 0, at + 1: 1},
                [pltpu.VMEM((2 * count, rows, width), F32)],
            )
            received = swapped(far, section, section % sub_bits)
            summed = (home + received.astype(F32)).astype(BF16)
            incoming[c] = lax.ppermute(summed, LEVEL, [(section, section + 1)])
    for c in range(CHUNKS):
        fwd[c], sol[c], solved = call(
            top_kernel, top, c * rows, rows,
            (info, rhs, incoming[c], lower_inv, upper_off, upper_inv, ancestor, fwd[c], sol[c]),
            [shape(BF16), shape(F32), shape(BF16)], {7: 0, 8: 1}, products=3,
        )
        above[c] = lax.ppermute(solved, LEVEL, [(top, top - 1)])
    for c in range(CHUNKS):
        (upd[c],) = call(top_update_kernel, top, c * rows, rows, (info, fwd[c], lower_off, upd[c]), [shape(F32)], {3: 0}, products=1)
    for section in reversed(range(top)):
        for c in range(CHUNKS):
            partner = swapped(above[c], section, section % sub_bits)
            sol[c], solved = call(
                backward_kernel, section, c * rows, rows,
                (info, fwd[c], above[c], partner, upper_off, upper_inv, sol[c]),
                [shape(F32), shape(BF16)], {6: 0},
            )
            if section:
                above[c] = lax.ppermute(solved, LEVEL, [(section, section - 1)])
    return jnp.concatenate(sol, axis=1)[None], jnp.concatenate(upd, axis=1)[None]


NODE_ROWS = 8
CROSS, OTHER, BELOW, LAST = "c", "o", "b", "l"
LOAD_NODES = 4
COSTS = [30000000000, 10000000000, 30000000000, 5000000000, 5000000000, 5000000000, 5000000000, 5000000000]
SMALL_VMEM_BYTES = 12 * 2**20
IN_ANY = pl.BlockSpec(memory_space=pl.ANY)
IN_HBM = pl.BlockSpec(memory_space=pltpu.HBM)


def rows_of(start):
    return pl.ds(pl.multiple_of(start, NODE_ROWS), NODE_ROWS)


def half_rows(array, sub):
    half = array.shape[1] // 2
    return pl.ds(pl.multiple_of(half * sub, half), half)


def flat(value):
    return value.reshape(value.shape[0] * value.shape[1], value.shape[2])


def pick(select, values):
    return dot(select, values.astype(BF16))


def on_level(section):
    return pl.when(lax.axis_index(LEVEL) == section)


def off_level(section):
    return pl.when(lax.axis_index(LEVEL) != section)


def keep(section, kept, outs):
    @off_level(section)
    def _():
        for before, after in zip(kept, outs):
            after[...] = before[...]


def fill_tables(parent, select, choose):
    nodes = parent.shape[1]
    size = nodes * NODE_ROWS
    top = lax.axis_size(LEVEL) - 1
    level, shift = lax.axis_index(LEVEL), lax.axis_index(SUB) * (nodes // 2)

    def target(row, axis):
        shape = (nodes, size) if axis else (size, nodes)
        child = lax.broadcasted_iota(jnp.int32, shape, axis) // NODE_ROWS + shift
        child = jnp.where(child >= nodes, child - nodes, child)
        same = child == lax.broadcasted_iota(jnp.int32, shape, 1 - axis)
        row = row - shift
        row = jnp.where(row < 0, row + nodes, row)
        if axis:
            found = dot(row.astype(F32).astype(BF16), same.astype(F32).astype(BF16))
        else:
            found = jnp.sum(jnp.where(same, row.astype(F32), 0.0), axis=1, keepdims=True)
        place = lax.broadcasted_iota(jnp.int32, found.shape, axis)
        return found.astype(jnp.int32) * NODE_ROWS + lax.rem(place, NODE_ROWS)

    up = target(parent[pl.ds(jnp.minimum(level, top - 1), 1), :], 1)
    down = target(parent[pl.ds(jnp.maximum(level - 1, 0), 1), :], 0)
    index = lax.broadcasted_iota(jnp.int32, (size, size), 0)
    select[...] = (index == up).astype(F32).astype(BF16)
    index = lax.broadcasted_iota(jnp.int32, (size, size), 1)
    choose[...] = (index == down).astype(F32).astype(BF16)


def start_kernel(parent, rhs, inv, off, select, choose, rhs_own, rhs_sent, home, swap_first, swap_rest, merged, *refs):
    *updates, parent_here, inv_here, off_here, sems = refs
    count = inv.shape[0]
    chunks = len(updates) // 2
    size = count * NODE_ROWS
    level, sub = lax.axis_index(LEVEL), lax.axis_index(SUB)
    table = pltpu.make_async_copy(parent, parent_here, sems.at[0, 0])
    mine = pltpu.make_async_copy(rhs.at[:, half_rows(rhs, sub), :], rhs_own, sems.at[0, 1])
    other = pltpu.make_async_copy(rhs.at[:, half_rows(rhs, 1 - sub), :], rhs_sent, sems.at[0, 2])
    table.start()
    loads = []
    for group in range(count // LOAD_NODES):
        here = pl.ds(group * LOAD_NODES, LOAD_NODES)
        loads.append(pltpu.make_async_copy(inv.at[here], inv_here.at[here], sems.at[1, group]))
        loads.append(pltpu.make_async_copy(off.at[here], off_here.at[here], sems.at[2, group]))
        loads[-2].start()
        loads[-1].start()
        if group == 0:
            mine.start()
            other.start()
    table.wait()
    fill_tables(parent_here, select, choose)
    mine.wait()
    other.wait()

    @on_level(0)
    def _():
        for node in range(count):
            if node % LOAD_NODES == 0:
                loads[2 * (node // LOAD_NODES)].wait()
                loads[2 * (node // LOAD_NODES) + 1].wait()
            right_side = jnp.concatenate([rhs_own[node], rhs_sent[node]], axis=0).astype(BF16)
            forward = dot(right_side, inv_here[node]).astype(BF16)
            update = dot(forward, off_here[node])
            for c in range(2 * chunks):
                updates[c][node] = update[NODE_ROWS * c : NODE_ROWS * (c + 1)]
        chosen = select[:, :size]
        for c in range(chunks):
            home[2 * count * c : 2 * count * (c + 1)] = pick(chosen, flat(updates[c][...])).reshape(2 * count, *home.shape[1:])
            sums = pick(chosen, flat(updates[chunks + c][...])).reshape(2 * count, *home.shape[1:]).astype(BF16)
            swap, at = (swap_first, swap_rest)[c % 2], 2 * count * (c // 2)
            swap[at : at + count] = sums[count:]
            swap[at + count : at + 2 * count] = sums[:count]

    @off_level(0)
    def _():
        for node in range(count):
            if node % LOAD_NODES == 0:
                loads[2 * (node // LOAD_NODES)].wait()
                loads[2 * (node // LOAD_NODES) + 1].wait()
            merged[node] = dot(inv_here[node], off_here[node]).astype(BF16)


def merge_kernel(low_inv, up_inv, up_off, ancestor, packed, *scratch):
    low_here, up_here, off_here, rows, sems = scratch
    count = low_inv.shape[0]
    sub = lax.axis_index(SUB)
    loads = []
    for group in range(count // LOAD_NODES):
        here = pl.ds(group * LOAD_NODES, LOAD_NODES)
        loads.append(pltpu.make_async_copy(up_inv.at[here], up_here.at[here], sems.at[1, group]))
        loads.append(pltpu.make_async_copy(low_inv.at[here], low_here.at[here], sems.at[0, group]))
        loads.append(pltpu.make_async_copy(up_off.at[here], off_here.at[here], sems.at[2, group]))
    loads.append(pltpu.make_async_copy(ancestor.at[:, half_rows(ancestor, 1 - sub), :], rows, sems.at[3, 0]))
    for load in loads:
        load.start()
    for node in range(count):
        if node % LOAD_NODES == 0:
            for load in loads[3 * (node // LOAD_NODES) : 3 * (node // LOAD_NODES) + 3]:
                load.wait()
        packed[node] = dot(low_here[node], up_here[node]).astype(BF16)
        packed[count + node] = dot(off_here[node], up_here[node]).astype(BF16)
    loads[-1].wait()
    packed[2 * count :] = rows[...].reshape(packed.shape[0] - 2 * count, *packed.shape[1:])


def residue_of(c, rhs_own, rhs_far, incoming, node):
    count = rhs_own.shape[0]
    rows = slice(NODE_ROWS * c, NODE_ROWS * (c + 1))
    right_side = rhs_own[node, rows, :] if node < count else rhs_far[node - count, rows, :]
    return (right_side - incoming[node].astype(F32)).astype(BF16)


def tier_role(c, at):
    count = at["rhs_own"].shape[0]
    own, far = at["own", c], at["far", c]
    for node in range(2 * count):
        value = residue_of(c, at["rhs_own"], at["rhs_far"], at["received"], node)
        at["residue", c][node] = value.astype(F32)
        if node < count:
            own[node] = dot(value, at["up_own"][node])
        else:
            far[node - count] = dot(value, at["up_far"][node - count])
    updates = jnp.concatenate([flat(own[...]), flat(far[...])], axis=0)
    at["sent"][...] = pick(at["select"][...], updates).reshape(at["sent"].shape).astype(BF16)


def send_solved(c, at):
    if "sent" in at:
        solved = jnp.concatenate([flat(at["sol_own", c][...]), flat(at["sol_far", c][...])], axis=0).astype(BF16)
        rows = dot(at["choose"][...], solved)
        rows = rows.reshape(rows.shape[0] // NODE_ROWS, NODE_ROWS, rows.shape[1]).astype(BF16)
        at["sent"][...] = rows[: at["sent"].shape[0]]
        if CROSS in at:
            at[CROSS][...] = rows[at["sent"].shape[0] :]


def top_role(c, at):
    count = at["rhs_own"].shape[0]
    base = at["top_base", c]
    for node in range(2 * count):
        value = residue_of(c, at["rhs_own"], at["rhs_far"], at["received"], node)
        at["residue", c][node] = value.astype(F32)
        if node < count:
            at["sol_own", c][node] = dot(value, at["down_own"][node]) - base[node]
        else:
            at["sol_far", c][node - count] = dot(value, at["down_far"][node - count]) - base[node]
    send_solved(c, at)


def back_role(c, at):
    count = at["sol_own", c].shape[0]
    base, above = at["low_base", c], at["received"]
    for node in range(count):
        at["sol_own", c][node] = base[node] - dot(above[node], at["down_own"][count + node])
        at["sol_far", c][node] = base[count + node] - dot(above[count + node], at["down_far"][count + node])
    send_solved(c, at)


def last_role(c, at):
    count = at["sol_own", c].shape[0]
    for node in range(count):
        above = jnp.concatenate([at["received"][node].astype(F32), at[CROSS][node].astype(F32)], axis=0)
        solved = dot(above.astype(BF16), at["down_own"][count + node])
        at["sol_own", c][node] = at["low_base", c][node] - solved[:NODE_ROWS]
        at[OTHER, c][node] = at[BELOW][node] - solved[NODE_ROWS:]


def sum_role(c, at):
    nodes = at["sent"].shape[0]
    home = at["home"][c * nodes : (c + 1) * nodes]
    partner = at["swapped"][c // 2 * nodes : (c // 2 + 1) * nodes]
    at["sent"][...] = (home + partner.astype(F32)).astype(BF16)


ROLES = {"tier": tier_role, "top": top_role, "back": back_role, LAST: last_role, "sum": sum_role}
READS = {
    "tier": ("rhs_own", "rhs_far", "received", "up_own", "up_far", "select"),
    "top": ("rhs_own", "rhs_far", "received", "down_own", "down_far", "choose", "top_base"),
    "back": ("received", "down_own", "down_far", "choose", "low_base"),
    LAST: ("received", CROSS, "down_own", "low_base", BELOW),
    "sum": ("home", "swapped"),
}
WRITES = {
    "tier": ("residue", "own", "far"),
    "top": ("residue", "sol_own", "sol_far"),
    "back": ("sol_own", "sol_far"),
    LAST: ("sol_own", OTHER),
    "sum": (),
}


def step_kernel(plan, in_keys, out_keys, kept_keys, *refs):
    reads = dict(zip(in_keys, refs))
    kept = dict(zip(kept_keys, refs[len(in_keys) :]))
    outs = dict(zip(out_keys, refs[len(in_keys) + len(kept_keys) :]))
    for level, role, c in plan:
        writes = [(name, c) for name in WRITES[role]]
        keep(level, [kept[key] for key in writes if key in kept], [outs[key] for key in writes if key in kept])
        pl.when(lax.axis_index(LEVEL) == level)(functools.partial(ROLES[role], c, {**reads, **outs}))


def step(plan, state, sends=1, flops=10**9):
    nodes = state["nodes"]
    in_keys, out_keys = [], []
    for _, role, c in plan:
        for name in READS[role]:
            key = (name, c) if name.endswith("_base") else name
            if key not in in_keys:
                in_keys.append(key)
        out_keys += [(name, c) for name in WRITES[role]]
    kept_keys = [key for key in out_keys if key in state]
    width = state["rhs_own"].shape[2]
    outs = []
    for name, _ in out_keys:
        of = nodes if name == "residue" else nodes // 2
        outs.append(jax.ShapeDtypeStruct((of, NODE_ROWS, width), F32))
    aliases = {len(in_keys) + i: out_keys.index(key) for i, key in enumerate(kept_keys)}
    all_outs = out_keys + ["sent", CROSS][:sends]
    outs += [jax.ShapeDtypeStruct((nodes // max(sends, 1), NODE_ROWS, width), BF16)] * sends
    operands = [state[key] for key in in_keys + kept_keys]
    results = run(functools.partial(step_kernel, plan, in_keys, all_outs, kept_keys), operands, outs, aliases, flops)
    state.update(zip(out_keys, results))
    return results[len(out_keys) :]


def rows_together(chunks, node):
    return jnp.concatenate([chunk[node] for chunk in chunks], axis=0).astype(BF16)


def apart(value, chunks, node):
    for c, chunk in enumerate(chunks):
        chunk[node] = value[NODE_ROWS * c : NODE_ROWS * (c + 1)]


def base_kernel(rhs_own, rhs_far, rhs_sent, own, far, *refs):
    *refs, below = refs
    residue, base = refs[: len(refs) // 2], refs[len(refs) // 2 :]
    count = rhs_own.shape[0]
    level, top = lax.axis_index(LEVEL), lax.axis_size(LEVEL) - 1

    @pl.when(level == 0)
    def _():
        for node in range(count):
            both = jnp.concatenate([rhs_own[node], rhs_sent[node, -NODE_ROWS:, :]], axis=0).astype(BF16)
            solved = dot(both, own[node])
            apart(solved, base, node)
            below[node] = solved[-NODE_ROWS:]
            apart(dot(rhs_far[node].astype(BF16), far[node]), base, count + node)

    @pl.when((level != 0) & (level != top))
    def _():
        for node in range(count):
            apart(dot(rows_together(residue, node), own[node]), base, node)
            apart(dot(rows_together(residue, count + node), far[node]), base, count + node)


def update_kernel(up_own, up_far, *refs):
    chunks = (len(refs) - 2) // 3
    residue, own_kept, far_kept = (refs[chunks * i : chunks * (i + 1)] for i in range(3))
    upd_own, upd_far = refs[-2:]
    level, top = lax.axis_index(LEVEL), lax.axis_size(LEVEL) - 1

    @pl.when(level == top)
    def _():
        count = up_own.shape[0]
        for node in range(count):
            upd_own[node] = dot(rows_together(residue, node), up_own[node])
            upd_far[node] = dot(rows_together(residue, count + node), up_far[node])

    @pl.when(level != top)
    def _():
        for c in range(chunks):
            rows = slice(NODE_ROWS * c, NODE_ROWS * (c + 1))
            upd_own[:, rows, :] = own_kept[c][...]
            upd_far[:, rows, :] = far_kept[c][...]


def ancestor_kernel(section, ancestor, own, far, *refs):
    *bases, here, sem = refs
    count, half, _ = here.shape
    sub = lax.axis_index(SUB)

    @on_level(section)
    def _():
        load = pltpu.make_async_copy(ancestor.at[:, half_rows(ancestor, sub), :], here, sem.at[0])
        load.start()
        load.wait()
        for node in range(count):
            per = far.shape[1] // half
            other = far[2 * count + node // per, half * (node % per) : half * (node % per + 1), :]
            mine = dot(here[node], own[count + node])
            other = dot(other, far[count + node])
            for c, base in enumerate(bases):
                base[node] = mine[NODE_ROWS * c : NODE_ROWS * (c + 1)]
                base[count + node] = other[NODE_ROWS * c : NODE_ROWS * (c + 1)]


def put(here, other, first, out, sems):
    sub = lax.axis_index(SUB)
    half = out.shape[1] // 2
    copies = []
    for i, (mine, theirs, row) in enumerate(zip(here, other, first)):
        size = mine.shape[1]
        to_mine = pl.ds(pl.multiple_of(half * sub + row, NODE_ROWS), size)
        to_theirs = pl.ds(pl.multiple_of(half * (1 - sub) + row, NODE_ROWS), size)
        copies.append(pltpu.make_async_copy(mine, out.at[:, to_mine, :], sems.at[0, i]))
        copies.append(pltpu.make_async_copy(theirs, out.at[:, to_theirs, :], sems.at[1, i]))
    for copy in copies:
        copy.start()
    for copy in copies:
        copy.wait()


def place_kernel(first, *refs):
    count = len(first)
    put(refs[:count], refs[count : 2 * count], first, *refs[-2:])


def place_bottom_kernel(here, far, other, *refs):
    @on_level(0)
    def _():
        put([here], [far], [0], *refs[-2:])

    @off_level(0)
    def _():
        put([here], [other], [0], *refs[-2:])


def run(kernel, operands, outs, aliases=None, flops=10**9, whole=None, scratch=(), raw=()):
    in_specs = [IN_HBM] * len(raw) + [IN_VMEM] * len(operands)
    operands = [*(pltpu.with_memory_space_constraint(value, pltpu.HBM) for value in raw), *(pltpu.with_memory_space_constraint(value, pltpu.VMEM) for value in operands)]
    out_specs = [IN_VMEM] * len(outs)
    out_shape = [pltpu.VMEM(out.shape, out.dtype) for out in outs]
    aliases = dict(aliases or {})
    if whole is not None:
        shape, before = whole
        if before is not None:
            aliases[len(operands)] = len(outs)
            operands.append(before)
            in_specs.append(IN_ANY)
        out_shape.append(shape)
        out_specs.append(IN_ANY)
    return pl.pallas_call(
        kernel,
        in_specs=in_specs,
        out_specs=out_specs,
        out_shape=out_shape,
        input_output_aliases=aliases,
        scratch_shapes=scratch,
        compiler_params=pltpu.CompilerParams(vmem_limit_bytes=SMALL_VMEM_BYTES),
        cost_estimate=pl.CostEstimate(
            flops=flops, bytes_accessed=10**6, transcendentals=0
        ),
    )(*operands)


def exchanged(value):
    return lax.ppermute(value, SUB, [(0, 1), (1, 0)])


def pair_body(rhs, lower_inv, lower_off, upper_inv, upper_off, ancestor, parent):
    levels = lax.axis_size(LEVEL)
    top = levels - 1
    rhs, lower_inv, lower_off, upper_inv, upper_off = (
        value[0] for value in (rhs, lower_inv, lower_off, upper_inv, upper_off)
    )
    count, all_rows, width = rhs.shape
    half = all_rows // 2
    chunks = half // NODE_ROWS
    nodes = 2 * count
    size = nodes * NODE_ROWS

    def shape(of, dtype):
        return jax.ShapeDtypeStruct((of, NODE_ROWS, width), dtype)

    def passed(value, pairs, cross=False):
        sources = [i for i in range(levels) if i not in dict(pairs)]
        targets = [i for i in range(levels) if i not in [to for _, to in pairs]]
        fill = min(
            (list(zip(sources, order)) for order in itertools.permutations(targets)),
            key=lambda extra: (sum(a == b for a, b in extra), sum((a ^ b) == levels - 1 for a, b in extra), sum((b, a) in pairs + extra for a, b in extra)),
        )
        if cross:
            pairs = [(2 * a + s, 2 * b + 1 - s) for a, b in pairs + fill for s in range(2)]
            return lax.ppermute(value, (LEVEL, SUB), pairs)
        return lax.ppermute(value, LEVEL, pairs + fill)

    def after(value, *earlier):
        return lax.optimization_barrier((value, *earlier))[0]

    matrices = jax.ShapeDtypeStruct(lower_inv.shape, BF16)
    table = jax.ShapeDtypeStruct((size, size), BF16)
    half_shape = jax.ShapeDtypeStruct((count, half, width), F32)
    block = pltpu.VMEM(lower_inv.shape, BF16)
    state = {"nodes": nodes}
    select, choose, rhs_own, rhs_sent, home, swap_first, swap_rest, up_own, *updates = run(
        start_kernel, (),
        [table, table, half_shape, half_shape, shape(chunks * nodes, F32)] + [shape(chunks // 2 * nodes, BF16)] * 2 + [matrices]
        + [shape(count, F32)] * (2 * chunks),
        raw=(parent, rhs, lower_inv, lower_off),
        scratch=[pltpu.VMEM(parent.shape, parent.dtype), block, block, pltpu.SemaphoreType.DMA((3, max(count // LOAD_NODES, 3)))],
    )
    state.update(select=select, choose=choose, rhs_own=rhs_own, home=home, up_own=up_own)
    swapped = [exchanged(swap_first), exchanged(swap_rest)]
    for c in range(chunks):
        state["own", c], state["far", c] = updates[c], updates[chunks + c]

    packed_shape = (2 * count + count * half // width, width, width)
    merge_scratch = [block, block, block, pltpu.VMEM((count, half, width), BF16), pltpu.SemaphoreType.DMA((4, count // LOAD_NODES))]

    def merged(sent):
        low, *others = lax.optimization_barrier((lower_inv, upper_inv, upper_off, ancestor, sent))
        return run(
            merge_kernel, (), [jax.ShapeDtypeStruct(packed_shape, BF16)],
            raw=(low, *others[:3]), scratch=merge_scratch,
        )[0]

    whole = jax.ShapeDtypeStruct(rhs.shape, F32)

    def sems(pieces):
        return [pltpu.SemaphoreType.DMA((2, pieces))]

    def placed(group, before, *earlier):
        first = after(state["sol_own", group[0]], *earlier) if earlier else state["sol_own", group[0]]
        return run(
            functools.partial(place_kernel, [NODE_ROWS * c for c in group]),
            [first, *(state["sol_own", c] for c in group[1:]), *(other[c] for c in group)],
            [], whole=(whole, before), scratch=sems(len(group)),
        )[0]

    pipes = [list(range(chunks))[i : i + 2] for i in range(0, chunks, 2)]
    received = [None] * len(pipes)
    other = [None] * chunks
    pace = []
    last = 2 * top + 1
    for k in range(last + 1):
        for p, pipe in enumerate(pipes):
            plan, pairs = [], []
            for j, c in enumerate(pipe):
                tier = k - j
                if 0 <= tier < top:
                    plan.append((tier, "sum" if tier == 0 else "tier", c))
                    pairs.append((tier, tier + 1))
                elif tier == top:
                    plan.append((top, "top", c))
                    pairs.append((top, top - 1))
                elif top < tier <= 2 * top:
                    low = 2 * top - tier
                    plan.append((low, "back", c))
                    if low:
                        pairs.append((low, low - 1))
            if k < len(pipe):
                state["swapped"] = swapped[k]
            if received[p] is not None:
                state["received"] = after(received[p], *pace)
            split = k == last - 1 and p == len(pipes) - 1
            if k == last and p == len(pipes) - 1:
                state[CROSS], state[OTHER, pipe[-1]] = cross, other[pipe[-1]]
                plan = [(0, LAST, pipe[-1])]
            sent, *sent_cross = step(plan, state, 2 if split else bool(pairs), COSTS[k]) or [None]
            if k == last and p == len(pipes) - 1:
                other[pipe[-1]] = state[OTHER, pipe[-1]]
            elif k == last:
                other[pipe[-1]] = exchanged(state["sol_far", pipe[-1]])
            if split:
                cross = passed(sent_cross[0], pairs, cross=True)
                other[pipe[-1]] = exchanged(state["sol_far", pipe[-1]])
            pace = [sent] if pairs else [state["sol_own", pipe[-1]]]
            if pairs:
                received[p] = passed(sent, pairs)
            if p == 0 and k == 0:
                state["up_far"] = exchanged(after(up_own, sent))
                state["rhs_far"] = exchanged(after(rhs_sent, sent))
            if p == 0 and k == 1:
                state["down_far"] = exchanged(state["down_own"])
            if p == 0 and k == last:
                early = [pipe[0] for pipe in pipes]
                other[early[0]], other[early[1]] = (exchanged(state["sol_far", c]) for c in early)
                solved = placed(early, None, *pace)
                pace = [solved]
        if k == 0:
            state["down_own"] = merged(sent)
            pace.append(state["down_own"])
        if k == last - 1:
            (update,) = run(
                place_bottom_kernel, (upd_own, after(upd_far, sent), upd_other), [], whole=(whole, None), scratch=sems(1)
            )
            pace.append(update)
        if k == top - 1:
            bases = run(
                functools.partial(ancestor_kernel, top),
                (state["down_own"], state["down_far"]),
                [shape(nodes, F32)] * chunks,
                raw=(after(ancestor, sent),),
                scratch=[pltpu.VMEM((count, half, width), BF16), pltpu.SemaphoreType.DMA((1,))],
            )
            state.update({("top_base", c): bases[c] for c in range(chunks)})
            pace += bases
        residues = [state["residue", c] for c in range(chunks)] if k >= top else []
        if k == top:
            *bases, state[BELOW] = run(
                base_kernel,
                (after(rhs_own, sent), state["rhs_far"], rhs_sent, state["down_own"], state["down_far"], *residues),
                [shape(nodes, F32)] * chunks + [shape(count, F32)],
            )
            state.update({("low_base", c): bases[c] for c in range(chunks)})
            pace += bases
        if k == top + 2:
            upd_own, upd_far = run(
                update_kernel,
                (up_own, state["up_far"], *residues, *(state["own", c] for c in range(chunks)), *(state["far", c] for c in range(chunks))),
                [half_shape] * 2,
            )
            upd_other = exchanged(upd_far)
    solved = placed([pipe[-1] for pipe in pipes], solved)
    return solved[None], update[None]


def solution(mesh):
    placed = (
        P(LEVEL, SUB, "rhs", None),
        P(LEVEL, SUB, None, None),
        P(LEVEL, SUB, None, None),
        P(LEVEL, SUB, None, None),
        P(LEVEL, SUB, None, None),
        P(SUB, "rhs", None),
        P(),
    )
    return jax.shard_map(
        pair_body if mesh.shape[SUB] == 2 else general_body,
        mesh=mesh,
        in_specs=placed,
        out_specs=(P(LEVEL, SUB, "rhs", None), P(LEVEL, SUB, "rhs", None)),
        check_vma=False,
    )
```
